32 devices in a mesh: batch: 8 (over z, y), rows: 4 (over x, core).
Axes of the slice: x: 2, y: 2, z: 4, core: 2. Of those that a mesh axis runs over, the one named last changes fastest.
Arguments:
- features: bfloat16 [72, 16, 14, 1024], P('batch', 'rows'), may hold values from -6 to 6
- w_reduce: bfloat16 [1024, 512], P('rows'), may hold values from -0.1875 to 0.1875
- w_spatial: bfloat16 [3, 3, 512, 512], P(None, None, 'rows'), may hold values from -0.09375 to 0.09375
- w_expand: bfloat16 [512, 2048], P('rows'), may hold values from -0.25 to 0.25
- w_shortcut: bfloat16 [1024, 2048], P('rows'), may hold values from -0.1875 to 0.1875
- w_squeeze: bfloat16 [2048, 512], P('rows'), may hold values from -0.125 to 0.125
- w_mixing: bfloat16 [3, 3, 512, 512], P(None, None, 'rows'), may hold values from -0.09375 to 0.09375
- w_widen: bfloat16 [512, 2048], P('rows'), may hold values from -0.25 to 0.25
- norm_reduce: float32 [2, 3, 512], replicated, as said below
- norm_spatial: float32 [2, 3, 512], replicated, as said below
- norm_expand: float32 [2, 3, 2048], replicated, as said below
- norm_shortcut: float32 [2, 3, 2048], replicated, as said below
- norm_squeeze: float32 [2, 3, 512], replicated, as said below
- norm_mixing: float32 [2, 3, 512], replicated, as said below
- norm_widen: float32 [2, 3, 2048], replicated, as said below
- cotangent: bfloat16 [72, 8, 7, 2048], P('batch', 'rows'), may hold values from -6 to 6
- resolution: int32 [72], replicated, may hold values from 0 to 2, as said below
- active: int32 [3], replicated, may hold values from 256 to 512, as said below
Outputs:
- mixed: bfloat16 [72, 8, 7, 2048], P('batch')
- grad_input: float32 [72, 16, 14, 1024], P('batch', 'rows')
- gw_reduce: float32 [1024, 512], P('batch')
- gw_spatial: float32 [3, 3, 512, 512], P(None, None, 'batch')
- gw_expand: float32 [512, 2048], P('batch')
- gw_shortcut: float32 [1024, 2048], P('batch')
- gw_squeeze: float32 [2048, 512], P('batch')
- gw_mixing: float32 [3, 3, 512, 512], P(None, None, 'batch')
- gw_widen: float32 [512, 2048], P('batch')
- gn_reduce: float32 [2, 3, 512], replicated
- gn_spatial: float32 [2, 3, 512], replicated
- gn_expand: float32 [2, 3, 2048], replicated
- gn_shortcut: float32 [2, 3, 2048], replicated
- gn_squeeze: float32 [2, 3, 512], replicated
- gn_mixing: float32 [2, 3, 512], replicated
- gn_widen: float32 [2, 3, 2048], replicated
The draws below stay inside these ranges and needn't reach their ends.
Inputs may be any that keep to these rules, and one draw needn't show every extreme that they name: `resolution`: each of 0, 1, 2 (inputs of 160, 192, 224 pixels) names exactly 24 images. `active`: a multiple of 64; one group uses all 512. `norm_reduce`: row 0 gains between 0.5 and 1.5, row 1 biases between -0.8 and 0.8. `norm_spatial`: as norm_reduce. `norm_expand`: as norm_reduce. `norm_shortcut`: as norm_reduce. `norm_squeeze`: as norm_reduce. `norm_mixing`: as norm_reduce. `norm_widen`: as norm_reduce.
All inputs are finite; a program needn't handle non-finite values.
Results may differ from the reference program's by a relative error of at most 0.02.
Values may be sent and summed in bfloat16 or wider, within the bound.
A program may use at most 192 MiB of HBM per device.

```python
import jax
import jax.numpy as jnp
from jax import lax

CIN = 1024
MID = 512
WIDE = 2048
IN_ROWS = 16
IN_COLS = 14
OUT_ROWS = 8
OUT_COLS = 7
IMAGES = 72


def norm_pair(key, span_width):
    gain_key, bias_key = jax.random.split(key)
    gains = jax.random.uniform(gain_key, (1, 3, span_width), jnp.float32, 0.5, 1.5)
    biases = jax.random.uniform(bias_key, (1, 3, span_width), jnp.float32, -0.8, 0.8)
    return jnp.concatenate([gains, biases], axis=0)


def draw_norm_reduce(key, part):
    key = jax.random.fold_in(key, 11)
    return norm_pair(key, MID)


def draw_norm_spatial(key, part):
    key = jax.random.fold_in(key, 12)
    return norm_pair(key, MID)


def draw_norm_expand(key, part):
    key = jax.random.fold_in(key, 13)
    return norm_pair(key, WIDE)


def draw_norm_shortcut(key, part):
    key = jax.random.fold_in(key, 14)
    return norm_pair(key, WIDE)


def draw_norm_squeeze(key, part):
    key = jax.random.fold_in(key, 15)
    return norm_pair(key, MID)


def draw_norm_mixing(key, part):
    key = jax.random.fold_in(key, 16)
    return norm_pair(key, MID)


def draw_norm_widen(key, part):
    key = jax.random.fold_in(key, 17)
    return norm_pair(key, WIDE)


def draw_resolution(key, part):
    key = jax.random.fold_in(key, 3)
    order = jax.random.permutation(key, IMAGES)
    return (order % 3).astype(jnp.int32)


def draw_active(key, part):
    key = jax.random.fold_in(key, 5)
    level_key, full_key = jax.random.split(key)
    levels = jax.random.randint(level_key, (3,), 4, 9)
    widest = jax.random.randint(full_key, (), 0, 3)
    levels = jnp.where(jnp.arange(3) == widest, 8, levels)
    return (MID * levels // 8).astype(jnp.int32)


def level_of(stream_key, shape, cuts, smallest, high):
    def one(dim, parts):
        draws = jax.random.uniform(jax.random.fold_in(jax.random.fold_in(stream_key, 6), dim), (parts,), jnp.float32, smallest / len(cuts), high / len(cuts))
        return jnp.repeat(jnp.exp(draws), shape[dim] // parts).reshape((-1,) + (1,) * (len(shape) - dim - 1))

    gain = one(*cuts[0])
    for cut in cuts[1:]:
        gain = gain * one(*cut)
    return gain


def normal_values(key, dims, spread, limit, shards=(), held_as=jnp.bfloat16):
    entries = spread * jax.random.normal(key, dims, jnp.float32)
    if shards:
        entries = entries * level_of(key, dims, shards, -0.22, 0.18)
    return jnp.clip(entries, -limit, limit).astype(held_as)


def setup_inputs(seed: int = 0) -> dict:
    keys = jax.random.split(jax.random.key(seed), 19)
    return {
        "features": normal_values(keys[0], (IMAGES, IN_ROWS, IN_COLS, CIN), 1.0, 6.0, ((0, 8), (1, 4))),
        "w_reduce": normal_values(keys[1], (CIN, MID), CIN ** -0.5, 0.1875, ((0, 4),)),
        "w_spatial": normal_values(keys[2], (3, 3, MID, MID), (9 * MID) ** -0.5, 0.09375, ((2, 4),)),
        "w_expand": normal_values(keys[3], (MID, WIDE), MID ** -0.5, 0.25, ((0, 4),)),
        "w_shortcut": normal_values(keys[4], (CIN, WIDE), CIN ** -0.5, 0.1875, ((0, 4),)),
        "w_squeeze": normal_values(keys[5], (WIDE, MID), WIDE ** -0.5, 0.125, ((0, 4),)),
        "w_mixing": normal_values(keys[6], (3, 3, MID, MID), (9 * MID) ** -0.5, 0.09375, ((2, 4),)),
        "w_widen": normal_values(keys[7], (MID, WIDE), MID ** -0.5, 0.25, ((0, 4),)),
        "norm_reduce": draw_norm_reduce(jax.random.fold_in(keys[18], 71), 0),
        "norm_spatial": draw_norm_spatial(jax.random.fold_in(keys[18], 71), 0),
        "norm_expand": draw_norm_expand(jax.random.fold_in(keys[18], 71), 0),
        "norm_shortcut": draw_norm_shortcut(jax.random.fold_in(keys[18], 71), 0),
        "norm_squeeze": draw_norm_squeeze(jax.random.fold_in(keys[18], 71), 0),
        "norm_mixing": draw_norm_mixing(jax.random.fold_in(keys[18], 71), 0),
        "norm_widen": draw_norm_widen(jax.random.fold_in(keys[18], 71), 0),
        "cotangent": normal_values(keys[15], (IMAGES, OUT_ROWS, OUT_COLS, WIDE), 1.0, 6.0, ((0, 8), (1, 4))),
        "resolution": draw_resolution(jax.random.fold_in(keys[18], 71), 0),
        "active": draw_active(jax.random.fold_in(keys[18], 71), 0),
    }


eps = 1e-05
highest = lax.Precision.HIGHEST

@jax.custom_vjp
def low(v):
    return lax.optimization_barrier(v.astype(jnp.bfloat16)).astype(jnp.float32)

@jax.custom_vjp
def low_back(v):
    return v

def low_keep(v):
    return (low(v), None)

def low_pass(kept, grad):
    return (grad,)

def back_keep(v):
    return (v, None)

def back_low(kept, grad):
    return (low(grad),)
low.defvjp(low_keep, low_pass)
low_back.defvjp(back_keep, back_low)

def frame_masks(sides, frame_rows, frame_cols):
    row_ids = jnp.arange(frame_rows, dtype=jnp.int32)
    col_ids = jnp.arange(frame_cols, dtype=jnp.int32)
    inside = (row_ids[None, :, None] < sides[:, None, None]) & (col_ids[None, None, :] < sides[:, None, None])
    return inside.astype(jnp.float32)

def channel_mask(active_img, factor, channels):
    return (jnp.arange(channels, dtype=jnp.int32)[None, :] < active_img[:, None] * factor).astype(jnp.float32)

def normalize(pre, params, pixels, onehot, counts):
    masked = pre * pixels[..., None]
    totals = jnp.dot(onehot.T, lax.optimization_barrier(jnp.sum(masked, axis=(1, 2))), precision=highest)
    squares = jnp.dot(onehot.T, lax.optimization_barrier(jnp.sum(masked * pre, axis=(1, 2))), precision=highest)
    mean_grp = totals / counts[:, None]
    var_grp = squares / counts[:, None] - mean_grp * mean_grp
    inverse = lax.rsqrt(var_grp + eps)
    mean_img = jnp.dot(onehot, mean_grp, precision=highest)
    inverse_img = jnp.dot(onehot, inverse, precision=highest)
    gain_img = jnp.dot(onehot, params[0], precision=highest)
    bias_img = jnp.dot(onehot, params[1], precision=highest)
    normed = (pre - mean_img[:, None, None, :]) * inverse_img[:, None, None, :]
    return normed * gain_img[:, None, None, :] + bias_img[:, None, None, :]

def convolve(values, kernel, stride, padding):
    return lax.conv_general_dilated(values, kernel, (stride, stride), padding, dimension_numbers=('NHWC', 'HWIO', 'NHWC'), precision=highest)

def project(values, weight):
    return jnp.einsum('irck,kn->ircn', values, weight, precision=highest)

def reference(features, w_reduce, w_spatial, w_expand, w_shortcut, w_squeeze, w_mixing, w_widen, norm_reduce, norm_spatial, norm_expand, norm_shortcut, norm_squeeze, norm_mixing, norm_widen, cotangent, resolution, active):
    groups = jnp.arange(3, dtype=jnp.int32)
    onehot_int = (resolution[:, None] == groups[None, :]).astype(jnp.int32)
    onehot = onehot_int.astype(jnp.float32)
    members = lax.optimization_barrier(jnp.sum(onehot, axis=0))
    sides_grp = 10.0 + 2.0 * groups.astype(jnp.float32)
    count_in = members * sides_grp * sides_grp
    count_out = members * (sides_grp * 0.5) * (sides_grp * 0.5)
    sides = 10 + 2 * resolution
    pixel_in = frame_masks(sides, features.shape[1], features.shape[2])
    pixel_out = frame_masks(sides // 2, features.shape[1] // 2, features.shape[2] // 2)
    active_img = lax.optimization_barrier(jnp.sum(onehot_int * active[None, :], axis=1))
    mid_width = w_reduce.shape[1]
    chan_in = channel_mask(active_img, features.shape[3] // mid_width, features.shape[3])
    chan_mid = channel_mask(active_img, 1, mid_width)
    chan_wide = channel_mask(active_img, w_expand.shape[1] // mid_width, w_expand.shape[1])
    mask_in = pixel_in[..., None] * chan_in[:, None, None, :]
    mask_mid_in = pixel_in[..., None] * chan_mid[:, None, None, :]
    mask_mid_out = pixel_out[..., None] * chan_mid[:, None, None, :]
    mask_wide_out = pixel_out[..., None] * chan_wide[:, None, None, :]

    def norm_in(pre, params):
        return normalize(pre, params, pixel_in, onehot, count_in)

    def norm_out(pre, params):
        return normalize(pre, params, pixel_out, onehot, count_out)

    def forward(inputs, k_reduce, k_spatial, k_expand, k_shortcut, k_squeeze, k_mixing, k_widen, m_reduce, m_spatial, m_expand, m_shortcut, m_squeeze, m_mixing, m_widen):
        masked_input = inputs * mask_in
        pre_one = low_back(project(masked_input, k_reduce))
        act_one = low(jax.nn.silu(norm_in(pre_one, m_reduce)) * mask_mid_in)
        pre_two = low_back(convolve(act_one, k_spatial, 2, ((1, 0), (1, 0))))
        act_two = low(jax.nn.silu(norm_out(pre_two, m_spatial)) * mask_mid_out)
        pre_three = low_back(project(act_two, k_expand))
        pre_short = low_back(project(masked_input[:, ::2, ::2], k_shortcut))
        block_one = low(jax.nn.silu(norm_out(pre_three, m_expand) + norm_out(pre_short, m_shortcut)) * mask_wide_out)
        pre_four = low_back(project(block_one, k_squeeze))
        act_four = low(jax.nn.silu(norm_out(pre_four, m_squeeze)) * mask_mid_out)
        pre_five = low_back(convolve(act_four, k_mixing, 1, ((1, 1), (1, 1))))
        act_five = low(jax.nn.silu(norm_out(pre_five, m_mixing)) * mask_mid_out)
        pre_six = low_back(project(act_five, k_widen))
        return jax.nn.silu(norm_out(pre_six, m_widen) + block_one) * mask_wide_out
    primals = (features.astype(jnp.float32), w_reduce.astype(jnp.float32), w_spatial.astype(jnp.float32), w_expand.astype(jnp.float32), w_shortcut.astype(jnp.float32), w_squeeze.astype(jnp.float32), w_mixing.astype(jnp.float32), w_widen.astype(jnp.float32), norm_reduce.astype(jnp.float32), norm_spatial.astype(jnp.float32), norm_expand.astype(jnp.float32), norm_shortcut.astype(jnp.float32), norm_squeeze.astype(jnp.float32), norm_mixing.astype(jnp.float32), norm_widen.astype(jnp.float32))
    result, pullback = jax.vjp(forward, *primals)
    grads = pullback(cotangent.astype(jnp.float32))
    return (result.astype(jnp.bfloat16), grads[0], grads[1], grads[2], grads[3], grads[4], grads[5], grads[6], grads[7], grads[8], grads[9], grads[10], grads[11], grads[12], grads[13], grads[14])
```

```python
import functools
from types import SimpleNamespace

import jax
import jax.numpy as jnp
from jax import lax
from jax.experimental import pallas as pl
from jax.experimental.pallas import tpu as pltpu
from jax.sharding import PartitionSpec as P

eps = 1e-05
MESH = pl.DeviceIdType.MESH
BF = jnp.bfloat16
F32 = jnp.float32
LANES = 128


def dot(a, b):
    return jnp.dot(a, b, preferred_element_type=F32)


def dot_t(a, b):
    return lax.dot_general(a, b, (((1,), (1,)), ((), ())), preferred_element_type=F32)


def dot_w(a, b):
    return lax.dot_general(a, b, (((0,), (0,)), ((), ())), preferred_element_type=F32)


def aligned(index, size):
    return pl.ds(pl.multiple_of(index * size, size), size)


def loop(count, body):
    def step(i, carry):
        body(i)
        return carry

    lax.fori_loop(0, count, step, 0)


def silu_parts(u):
    s = jax.nn.sigmoid(u)
    return s, u * s


def slope(u):
    s = jax.nn.sigmoid(u)
    return s * (1.0 + u * (1.0 - s))


def block_kernel(names, cfg, *refs):
    R = SimpleNamespace(**dict(zip(names, refs)))
    S, RD, OD, NB = cfg.slots, cfg.in_rows, cfg.out_rows, cfg.batch
    MID, WIDE, CIN = cfg.mid, cfg.wide, cfg.cin
    M = OD * S
    b = lax.axis_index("batch")
    r = lax.axis_index("rows")
    core = lax.rem(r, 2)
    xb = lax.div(r, 2)
    core_peer = r + 1 - 2 * core
    x_row = lax.rem(r + 2, 4)
    diag = 3 - r
    half = lax.rem(b, 2)
    y_b = b + 1 - 2 * half

    def flip(i, j):
        out = jnp.int32(0)
        bit = 1
        while bit < 2 * NB:
            p, q = lax.rem(lax.div(i, bit), 2), lax.rem(lax.div(j, bit), 2)
            out = out + bit * (p + q - 2 * p * q)
            bit *= 2
        return out

    me = b * 2 + xb

    def remote(src, dst, send, recv, dev):
        return pltpu.make_async_remote_copy(
            src_ref=src, dst_ref=dst, send_sem=send, recv_sem=recv, device_id=dev, device_id_type=MESH
        )

    def team(id2):
        return (lax.div(id2, 2), 2 * lax.rem(id2, 2) + core)

    bar = pltpu.get_barrier_semaphore()
    for dev in ((b, core_peer), (b, diag)):
        pl.semaphore_signal(bar, inc=1, device_id=dev, device_id_type=MESH)

    def greet(j):
        pl.semaphore_signal(bar, inc=1, device_id=team(flip(me, j + 1)), device_id_type=MESH)

    loop(2 * NB - 1, greet)
    pl.semaphore_wait(bar, 2 * NB + 1)

    units = cfg.units
    wsend, wrecv, wloc = R.wsend, R.wrecv, R.wloc

    def wview(u, shard, part, source):
        name, conv, k0, kn = units[u]
        full = getattr(R, "f_" + name)
        if source:
            ref = getattr(R, name)
            if conv:
                if part is None:
                    return ref.at[pl.ds(k0, kn)]
                h = ref.shape[1] // 2
                return ref.at[pl.ds(k0, kn), aligned(part, h)]
            if part is None:
                return ref.at[pl.ds(k0, kn)]
            h = kn // 2
            return ref.at[pl.ds(pl.multiple_of(k0 + part * h, h), h)]
        if conv:
            if part is None:
                return full.at[pl.ds(k0, kn), shard]
            h = full.shape[2] // 2
            return full.at[pl.ds(k0, kn), shard, aligned(part, h)]
        if part is None:
            return full.at[shard, pl.ds(k0, kn)]
        h = kn // 2
        return full.at[shard, pl.ds(pl.multiple_of(k0 + part * h, h), h)]

    def w_copy(u, i):
        if i < 2:
            part = None if i == 0 else half
            dev = (b, core_peer) if i == 0 else (b, x_row)
            src, dst = wview(u, r, part, True), wview(u, r, part, False)
        else:
            src = dst = wview(u, x_row, 1 - half if i == 4 else half, False)
            dev = (y_b, r) if i == 3 else (b, core_peer)
        return remote(src, dst, wsend.at[u, i], wrecv.at[u, i], dev)

    def w_local(u):
        return pltpu.make_async_copy(wview(u, r, None, True), wview(u, r, None, False), wloc.at[u])

    def w_start(u):
        w_copy(u, 1).start()
        w_copy(u, 0).start()
        w_local(u).start()

    def w_second(u):
        w_copy(u, 1).wait_recv()
        w_copy(u, 3).start()
        w_copy(u, 2).start()

    def w_third(u):
        w_copy(u, 3).wait_recv()
        w_copy(u, 4).start()

    def w_ready(u):
        w_local(u).wait()
        for i in (0, 2, 4):
            w_copy(u, i).wait_recv()

    pumped = [0]

    def pump(steps):
        for _ in range(steps):
            n = pumped[0]
            if n >= len(units) + 2:
                return
            if n < len(units):
                w_start(n)
            if 0 <= n - 1 < len(units):
                w_second(n - 1)
            if 0 <= n - 2 < len(units):
                w_third(n - 2)
            pumped[0] = n + 1

    def need(name):
        last = max(u for u in range(len(units)) if units[u][0] == name)
        while pumped[0] < last + 3:
            pump(1)
        for u in range(len(units)):
            if units[u][0] == name:
                w_ready(u)

    def mid_start(k):
        p = k % 2
        swap = remote(R.loc.at[1 - core], R.rc.at[p], R.ms.at[0], R.mr.at[0, p], (b, core_peer))
        swap.start()
        swap.wait_recv()
        R.rq[p, me] = R.loc[core] + R.rc[p]

        def send(j):
            to = team(flip(me, j + 1))
            remote(R.rq.at[p, me], R.rq.at[p, me], R.ms.at[1], R.mr.at[1, p], to).start()

        loop(2 * NB - 1, send)
        swap.wait_send()

    def mid_finish(k, tot):
        p = k % 2
        rest = R.rq.at[p, pl.ds(0, 2 * NB - 1)]
        every = remote(rest, rest, R.ms.at[1], R.mr.at[1, p], (b, x_row))
        every.wait_recv()
        total = R.rq[p, 0]
        for j in range(1, 2 * NB):
            total = total + R.rq[p, j]
        tot[core] = total
        back = remote(tot.at[core], tot.at[core], R.ms.at[2], R.mr.at[2, p], (b, core_peer))
        back.start()
        every.wait_send()
        back.wait()

    def wide_start(k, loc):
        n = loc.shape[1]
        rw, wb = R.rw.at[k, :, pl.ds(0, n)], R.wb.at[k % 2, :, pl.ds(0, n)]
        rw[r] = loc[r]
        for to in (core_peer, x_row, diag):
            remote(loc.at[to], rw.at[r], R.ws.at[k, 0], R.wr.at[k, 0], (b, to)).start()
        three = remote(loc.at[pl.ds(0, 3)], rw.at[pl.ds(0, 3)], R.ws.at[k, 0], R.wr.at[k, 0], (b, core_peer))
        three.wait_recv()
        wb[b] = rw[0] + rw[1] + (rw[2] + rw[3])

        def send(j):
            to = lax.rem(b + j + 1, NB)
            remote(wb.at[b], wb.at[b], R.ws.at[k, 1], R.wr.at[k, 1], (to, r)).start()

        loop(NB - 1, send)
        three.wait_send()

    def wide_finish(k, tot):
        n = tot.shape[1]
        wb = R.wb.at[k % 2, :, pl.ds(0, n)]
        rest = wb.at[pl.ds(0, NB - 1)]
        every = remote(rest, rest, R.ws.at[k, 1], R.wr.at[k, 1], (b, x_row))
        every.wait_recv()
        total = wb[0]
        for j in range(1, NB):
            total = total + wb[j]
        tot[r] = total
        for to in (core_peer, x_row, diag):
            remote(tot.at[r], tot.at[r], R.ws.at[k, 2], R.wr.at[k, 2], (b, to)).start()
        three = remote(tot.at[pl.ds(0, 3)], tot.at[pl.ds(0, 3)], R.ws.at[k, 2], R.wr.at[k, 2], (b, core_peer))
        every.wait_send()
        three.wait()

    def mid_at(ref, j):
        return ref.at[lax.div(j, 2), :, aligned(lax.rem(j, 2), LANES)]

    def wide_at(ref, j):
        return ref.at[lax.div(j, 4), :, aligned(lax.rem(j, 4), LANES)]

    def group_rows(ref, row, values):
        for g in range(3):
            ref[row + g : row + g + 1, :] = jnp.sum(values * R.onehot[g], axis=0, keepdims=True)

    def blank(ref, row, rows):
        ref[row : row + rows, :] = jnp.zeros((rows, LANES), F32)

    def spread(rows3):
        return rows3[0] * R.onehot[0] + rows3[1] * R.onehot[1] + rows3[2] * R.onehot[2]

    def moments(sums, inv_n, row=0):
        means, invs = [], []
        for g in range(3):
            n = R.counts[inv_n + g : inv_n + g + 1, :]
            mean = sums[row + g : row + g + 1, :] * n
            var = sums[row + 3 + g : row + 4 + g, :] * n - mean * mean
            means.append(mean)
            invs.append(lax.rsqrt(var + eps))
        return means, invs

    IN, OUT = 0, 3

    def forward_terms(sums, params, cols, inv_n, row=0):
        means, invs = moments(sums, inv_n, row)
        scales = [invs[g] * params[g : g + 1, cols] for g in range(3)]
        shifts = [params[3 + g : 4 + g, cols] - means[g] * scales[g] for g in range(3)]
        return spread(scales), spread(shifts)

    def xhat_terms(sums, inv_n, row=0):
        means, invs = moments(sums, inv_n, row)
        return spread(invs), spread([-means[g] * invs[g] for g in range(3)])

    def backward_terms(sums, grads, params, cols, inv_n, row=0, g0=0, g1=3):
        means, invs = moments(sums, inv_n, row)
        fs, az, bz = [], [], []
        for g in range(3):
            n = R.counts[inv_n + g : inv_n + g + 1, :]
            f = invs[g] * params[g : g + 1, cols]
            gain = grads[g0 + g : g0 + g + 1, :] * n * invs[g]
            bias = grads[g1 + g : g1 + g + 1, :] * n
            fs.append(f)
            bz.append(f * gain)
            az.append(f * (bias - means[g] * gain))
        return spread(fs), spread(az), spread(bz)

    def keep(mask_ref, cols):
        return spread([mask_ref[g : g + 1, cols] for g in range(3)])

    def out_rows(k):
        return slice(k * S, (k + 1) * S)

    def forward_stats(z, loc_at, row=0):
        def body(j):
            cols = aligned(j, LANES)
            s = jnp.zeros((S, LANES), F32)
            q = jnp.zeros((S, LANES), F32)
            for o in range(OD):
                v = z[out_rows(o), cols]
                m = v * R.pix_out[out_rows(o), :]
                s = s + m
                q = q + m * v
            st = loc_at(j)
            group_rows(st, row, s)
            group_rows(st, row + 3, q)
            blank(st, row + 6, 2)

        loop(z.shape[-1] // LANES, body)

    def rolled(v, by):
        return pltpu.roll(v, by % S, 0)

    def unit_windows(halo, win, rows, flipped):
        def body(j):
            cols = aligned(j, LANES)
            for k in rows:
                v = halo[k, :, cols].astype(F32)
                moved = (rolled(v, 1).astype(BF), v.astype(BF), rolled(v, -1).astype(BF))
                for dr in range(3):
                    o = k - dr
                    if not 0 <= o < OD:
                        continue
                    for dc in range(3):
                        t = (2 - dr) * 3 + 2 - dc if flipped else dr * 3 + dc
                        win[out_rows(o), pl.ds(pl.multiple_of(t * MID + j * LANES, LANES), LANES)] = moved[dc]

        loop(MID // LANES, body)

    def edge_exchange(halo, k):
        up = remote(halo.at[1], halo.at[OD + 1], R.es.at[k, 0], R.er.at[k, 0], (b, jnp.maximum(r - 1, 0)))
        down = remote(halo.at[OD], halo.at[0], R.es.at[k, 1], R.er.at[k, 1], (b, jnp.minimum(r + 1, 3)))

        @pl.when(r > 0)
        def _():
            up.start()

        @pl.when(r < 3)
        def _():
            down.start()

        @pl.when(r == 0)
        def _():
            halo[0] = jnp.zeros(halo.shape[1:], BF)

        @pl.when(r == 3)
        def _():
            halo[OD + 1] = jnp.zeros(halo.shape[1:], BF)

        return up, down

    def edge_wait(pair):
        up, down = pair

        @pl.when(r < 3)
        def _():
            up.wait_recv()
            down.wait_send()

        @pl.when(r > 0)
        def _():
            down.wait_recv()
            up.wait_send()

    pump(3)
    need("w_reduce")

    def z1_rows(k):
        w = R.f_w_reduce[...].reshape(CIN, MID)
        R.z1[k] = dot(R.x0[k], w)

    loop(RD, z1_rows)

    def z1_stats(j):
        cols = aligned(j, LANES)
        s = jnp.zeros((S, LANES), F32)
        q = jnp.zeros((S, LANES), F32)
        for k in range(RD):
            for p in range(2):
                v = R.z1[k, out_rows(p), cols]
                m = v * R.pix_in[k, out_rows(p), :]
                s = s + m
                q = q + m * v
        st = mid_at(R.loc, j)
        group_rows(st, 0, s)
        group_rows(st, 3, q)
        blank(st, 6, 2)

    loop(MID // LANES, z1_stats)
    mid_start(0)
    pump(1)
    mid_finish(0, R.t1)

    last = RD - 1

    def h1_body(j):
        cols = aligned(j, LANES)
        sc, sh = forward_terms(mid_at(R.t1, j), R.norm_reduce, cols, IN)
        ch = keep(R.chan_mid, cols)
        for k in range(RD - 1, -1, -1):
            for p in range(2):
                u = R.z1[k, out_rows(p), cols] * sc + sh
                h = silu_parts(u)[1] * (ch * R.pix_in[k, out_rows(p), :])
                if k == last:
                    R.h1s[p, :, cols] = h.astype(BF)
                for dr in range(3):
                    o2 = k + 1 - dr
                    if o2 % 2 or not 0 <= o2 // 2 < OD:
                        continue
                    o = o2 // 2
                    taps = ((1, h),) if p == 0 else ((0, rolled(h, 1)), (2, h))
                    for dc, v in taps:
                        t = dr * 3 + dc
                        R.win1[out_rows(o), pl.ds(pl.multiple_of(t * MID + j * LANES, LANES), LANES)] = v.astype(BF)

    loop(MID // LANES, h1_body)
    down = remote(R.h1s, R.h1r, R.hs.at[0], R.hr.at[0], (b, jnp.minimum(r + 1, 3)))

    @pl.when(r < 3)
    def _():
        down.start()

    pump(1)

    @pl.when(r > 0)
    def _():
        down.wait_recv()

    @pl.when(r == 0)
    def _():
        R.h1r[...] = jnp.zeros(R.h1r.shape, BF)

    def h1_halo(j):
        cols = aligned(j, LANES)
        even = R.h1r[0, :, cols]
        odd = R.h1r[1, :, cols]
        for dc, v in ((0, rolled(odd.astype(F32), 1).astype(BF)), (1, even), (2, odd)):
            R.win1[out_rows(0), pl.ds(pl.multiple_of(dc * MID + j * LANES, LANES), LANES)] = v

    loop(MID // LANES, h1_halo)

    @pl.when(r < 3)
    def _():
        down.wait_send()

    need("w_spatial")

    def conv(win, weight, z):
        def body(j):
            cols = aligned(j, 256)
            z[:, cols] = dot(win[...], weight[:, :, :, cols].reshape(9 * MID, 256))

        loop(MID // 256, body)

    conv(R.win1, R.f_w_spatial, R.z2)
    forward_stats(R.z2, lambda j: mid_at(R.loc, j))
    mid_start(1)
    pump(1)
    mid_finish(1, R.t2)

    def activate(z, tot, params, dest):
        def body(j):
            cols = aligned(j, LANES)
            sc, sh = forward_terms(mid_at(tot, j), params, cols, OUT)
            ch = keep(R.chan_mid, cols)
            for o in range(OD):
                u = z[out_rows(o), cols] * sc + sh
                dest(o, cols, (silu_parts(u)[1] * (ch * R.pix_out[out_rows(o), :])).astype(BF))

        loop(MID // LANES, body)

    def to_h2(o, cols, v):
        R.h2[out_rows(o), cols] = v

    activate(R.z2, R.t2, R.norm_spatial, to_h2)
    need("w_expand")

    def expand_to(h, weight, z):
        def body(j):
            cols = aligned(j, 512)
            z[:, cols] = dot(h[...], weight[:, :, cols].reshape(-1, 512))

        loop(WIDE // 512, body)

    expand_to(R.h2, R.f_w_expand, R.z3)
    need("w_shortcut")

    def zs_body(j):
        cols = aligned(j, 512)
        w = R.f_w_shortcut[:, :, cols].reshape(CIN, 512)
        for o in range(OD):
            R.zs[out_rows(o), cols] = dot(R.x0[2 * o, 0:S, :], w)

    loop(WIDE // 512, zs_body)
    forward_stats(R.z3, lambda j: wide_at(R.locw2, j), 0)
    forward_stats(R.zs, lambda j: wide_at(R.locw2, j), 8)
    wide_start(0, R.locw2)
    pump(2)
    wide_finish(0, R.t3)

    def u1_terms(j):
        cols = aligned(j, LANES)
        tot = wide_at(R.t3, j)
        sc3, sh3 = forward_terms(tot, R.norm_expand, cols, OUT, 0)
        scs, shs = forward_terms(tot, R.norm_shortcut, cols, OUT, 8)
        shift = sh3 + shs

        def u1(o):
            return R.z3[out_rows(o), cols] * sc3 + R.zs[out_rows(o), cols] * scs + shift

        return u1

    def y1_body(j):
        cols = aligned(j, LANES)
        u1 = u1_terms(j)
        ch = keep(R.chan_wide, cols)
        for o in range(OD):
            y = silu_parts(u1(o))[1] * (ch * R.pix_out[out_rows(o), :])
            R.y1[out_rows(o), cols] = y.astype(BF)

    loop(WIDE // LANES, y1_body)
    need("w_squeeze")

    def squeeze_body(j):
        cols = aligned(j, 256)
        R.z4[:, cols] = dot(R.y1[...], R.f_w_squeeze[:, :, cols].reshape(WIDE, 256))

    loop(MID // 256, squeeze_body)
    forward_stats(R.z4, lambda j: mid_at(R.loc, j))
    mid_start(2)
    pump(2)
    mid_finish(2, R.t4)

    def to_h4(o, cols, v):
        R.h4[o + 1, :, cols] = v

    activate(R.z4, R.t4, R.norm_squeeze, to_h4)
    pair = edge_exchange(R.h4, 0)
    pump(1)
    unit_windows(R.h4, R.win4, range(1, OD + 1), False)
    edge_wait(pair)
    unit_windows(R.h4, R.win4, (0, OD + 1), False)
    need("w_mixing")
    conv(R.win4, R.f_w_mixing, R.z5)
    forward_stats(R.z5, lambda j: mid_at(R.loc, j))
    mid_start(3)
    pump(20)
    mid_finish(3, R.t5)

    def to_h5(o, cols, v):
        R.h5[out_rows(o), cols] = v

    activate(R.z5, R.t5, R.norm_mixing, to_h5)
    need("w_widen")
    expand_to(R.h5, R.f_w_widen, R.z6)
    forward_stats(R.z6, lambda j: wide_at(R.locw, j))
    wide_start(1, R.locw)
    wide_finish(1, R.t6)

    def u2_body(j):
        cols = aligned(j, LANES)
        tot = wide_at(R.t6, j)
        sc, sh = forward_terms(tot, R.norm_widen, cols, OUT)
        xa, xs = xhat_terms(tot, OUT)
        ch = keep(R.chan_wide, cols)
        g0 = jnp.zeros((S, LANES), F32)
        g1 = jnp.zeros((S, LANES), F32)
        for o in range(OD):
            z = R.z6[out_rows(o), cols]
            u = z * sc + sh + R.y1[out_rows(o), cols].astype(F32)
            mask = ch * R.pix_out[out_rows(o), :]
            s, su = silu_parts(u)
            R.mixed_local[o, :, cols] = (su * mask).astype(BF)
            d = R.cotangent[out_rows(o), cols].astype(F32) * mask * (s * (1.0 + u * (1.0 - s)))
            R.du2[out_rows(o), cols] = d
            g0 = g0 + d * (z * xa + xs)
            g1 = g1 + d
        st = wide_at(R.locw, j)
        group_rows(st, 0, g0)
        group_rows(st, 3, g1)
        blank(st, 6, 2)

    loop(WIDE // LANES, u2_body)
    wide_start(2, R.locw)
    mixed_copies = [
        remote(R.mixed_local, R.mixed.at[r], R.xs.at[i], R.xr.at[i], (b, to))
        for i, to in enumerate((core_peer, x_row))
    ]
    for c in mixed_copies:
        c.start()
    own = pltpu.make_async_copy(R.mixed_local, R.mixed.at[r], R.xl)
    own.start()
    wide_finish(2, R.g6)

    def widen_back(j):
        cols = aligned(j, LANES)
        f, a, bz = backward_terms(wide_at(R.t6, j), wide_at(R.g6, j), R.norm_widen, cols, OUT)
        for o in range(OD):
            d = f * R.du2[out_rows(o), cols] - a - R.z6[out_rows(o), cols] * bz
            R.dz6[out_rows(o), cols] = (d * R.pix_out[out_rows(o), :]).astype(BF)

    loop(WIDE // LANES, widen_back)

    grad_out = [None, None]
    turn = [0]

    def staged(n, off, fill):
        i = turn[0] % 2
        turn[0] += 1
        if grad_out[i] is not None:
            grad_out[i].wait()
        stage = R.stage.at[i]
        fill(stage)
        copy = pltpu.make_async_copy(
            stage.at[:, :, pl.ds(0, n)], R.grads.at[:, :, pl.ds(off, n)], R.gs.at[i]
        )
        copy.start()
        grad_out[i] = copy

    def fill_out(act, dz):
        def fill(stage):
            def body(j):
                res = dot_w(act(), dz[:, aligned(j, 512)])
                n = res.shape[0] // 8
                stage[:, j, 0:n, :] = res.reshape(8, n, 512).astype(BF)

            loop(WIDE // 512, body)

        return fill

    def fill_conv(win, dz):
        def fill(stage):
            def body(t):
                res = dot_w(win[:, aligned(t, MID)], dz())
                n = MID // 32
                stage[:, :, aligned(t, n), :] = res.reshape(8, 4, n, MID).astype(BF)

            loop(9, body)

        return fill

    def mid_back_sums(dh, z, tot, params):
        def body(j):
            cols = aligned(j, LANES)
            sums = mid_at(tot, j)
            sc, sh = forward_terms(sums, params, cols, OUT)
            xa, xs = xhat_terms(sums, OUT)
            ch = keep(R.chan_mid, cols)
            g0 = jnp.zeros((S, LANES), F32)
            g1 = jnp.zeros((S, LANES), F32)
            for o in range(OD):
                v = z[out_rows(o), cols]
                d = dh[out_rows(o), cols] * (ch * R.pix_out[out_rows(o), :]) * slope(v * sc + sh)
                dh[out_rows(o), cols] = d
                g0 = g0 + d * (v * xa + xs)
                g1 = g1 + d
            st = mid_at(R.loc, j)
            group_rows(st, 0, g0)
            group_rows(st, 3, g1)
            blank(st, 6, 2)

        loop(MID // LANES, body)

    def mid_back_apply(dh, z, tot, grads, params, dest):
        def body(j):
            cols = aligned(j, LANES)
            f, a, bz = backward_terms(mid_at(tot, j), mid_at(grads, j), params, cols, OUT)
            for o in range(OD):
                d = f * dh[out_rows(o), cols] - a - z[out_rows(o), cols] * bz
                dest(o, cols, (d * R.pix_out[out_rows(o), :]).astype(BF))

        loop(MID // LANES, body)

    def reduce_back(dz, weight, dh):
        def body(j):
            w = weight[aligned(j, 2)].reshape(MID // 2, WIDE)
            dh[:, aligned(j, MID // 2)] = dot_t(dz[...], w)

        loop(2, body)

    reduce_back(R.dz6, R.f_w_widen, R.dh)
    mid_back_sums(R.dh, R.z5, R.t5, R.norm_mixing)
    mid_start(4)
    staged(cfg.rows["w_widen"], cfg.offs["w_widen"], fill_out(lambda: R.h5[...], R.dz6))
    mid_finish(4, R.g5)

    def to_d5(o, cols, v):
        R.d5[o + 1, :, cols] = v

    mid_back_apply(R.dh, R.z5, R.t5, R.g5, R.norm_mixing, to_d5)
    pair = edge_exchange(R.d5, 1)
    unit_windows(R.d5, R.win5, range(1, OD + 1), True)
    edge_wait(pair)
    unit_windows(R.d5, R.win5, (0, OD + 1), True)

    def conv_back(j):
        acc = None
        for t in range(9):
            w = R.f_w_mixing[t, aligned(j, 2)].reshape(MID // 2, MID)
            v = dot_t(R.win5[:, t * MID : (t + 1) * MID], w)
            acc = v if acc is None else acc + v
        R.dh[:, aligned(j, MID // 2)] = acc

    loop(2, conv_back)
    mid_back_sums(R.dh, R.z4, R.t4, R.norm_squeeze)
    mid_start(5)
    staged(
        cfg.rows["w_mixing"],
        cfg.offs["w_mixing"],
        fill_conv(R.win4, lambda: R.d5[1 : OD + 1].reshape(M, MID)),
    )
    mid_finish(5, R.g4)

    def to_d4(o, cols, v):
        R.dz4[out_rows(o), cols] = v

    mid_back_apply(R.dh, R.z4, R.t4, R.g4, R.norm_squeeze, to_d4)

    def squeeze_back(j):
        w = R.f_w_squeeze[j]
        n = w.shape[0]
        R.du1[:, aligned(j, n)] = dot_t(R.dz4[...], w)

    loop(4, squeeze_back)

    def u1_back(j):
        cols = aligned(j, LANES)
        u1 = u1_terms(j)
        tot = wide_at(R.t3, j)
        xa3, xs3 = xhat_terms(tot, OUT, 0)
        xas, xss = xhat_terms(tot, OUT, 8)
        ch = keep(R.chan_wide, cols)
        g0 = jnp.zeros((S, LANES), F32)
        g1 = jnp.zeros((S, LANES), F32)
        g2 = jnp.zeros((S, LANES), F32)
        for o in range(OD):
            rows = out_rows(o)
            d = (R.du1[rows, cols] + R.du2[rows, cols]) * (ch * R.pix_out[rows, :]) * slope(u1(o))
            R.du1[rows, cols] = d
            g0 = g0 + d * (R.z3[rows, cols] * xa3 + xs3)
            g2 = g2 + d * (R.zs[rows, cols] * xas + xss)
            g1 = g1 + d
        st = wide_at(R.locw2, j)
        group_rows(st, 0, g0)
        group_rows(st, 3, g1)
        blank(st, 6, 2)
        group_rows(st, 8, g2)
        blank(st, 11, 5)

    loop(WIDE // LANES, u1_back)
    wide_start(3, R.locw2)

    def fill_squeeze(stage):
        def body(j):
            res = dot_w(R.y1[:, aligned(j, WIDE // 8)], R.dz4[...])
            n = res.shape[0] // 4
            stage[j, :, 0:n, :] = res.reshape(4, n, MID).astype(BF)

        loop(8, body)

    staged(cfg.rows["w_squeeze"], cfg.offs["w_squeeze"], fill_squeeze)
    wide_finish(3, R.g3)

    mixed_copies[1].wait_recv()
    onward = remote(R.mixed.at[x_row], R.mixed.at[x_row], R.xs.at[2], R.xr.at[2], (b, core_peer))
    onward.start()

    def u1_apply(j):
        cols = aligned(j, LANES)
        tot, grads = wide_at(R.t3, j), wide_at(R.g3, j)
        f3, a3, b3 = backward_terms(tot, grads, R.norm_expand, cols, OUT, 0, 0, 3)
        fs, as_, bs = backward_terms(tot, grads, R.norm_shortcut, cols, OUT, 8, 8, 3)
        for o in range(OD):
            rows = out_rows(o)
            d = R.du1[rows, cols]
            pix = R.pix_out[rows, :]
            R.dz3[rows, cols] = ((f3 * d - a3 - R.z3[rows, cols] * b3) * pix).astype(BF)
            R.dzs[rows, cols] = ((fs * d - as_ - R.zs[rows, cols] * bs) * pix).astype(BF)

    loop(WIDE // LANES, u1_apply)
    reduce_back(R.dz3, R.f_w_expand, R.dh)
    mid_back_sums(R.dh, R.z2, R.t2, R.norm_spatial)
    mid_start(6)
    staged(cfg.rows["w_expand"], cfg.offs["w_expand"], fill_out(lambda: R.h2[...], R.dz3))
    mid_finish(6, R.g2)

    def to_d2(o, cols, v):
        R.d2[o, :, cols] = v

    mid_back_apply(R.dh, R.z2, R.t2, R.g2, R.norm_spatial, to_d2)
    up = remote(R.d2.at[0], R.d2.at[OD], R.hs.at[1], R.hr.at[1], (b, jnp.maximum(r - 1, 0)))

    @pl.when(r > 0)
    def _():
        up.start()

    @pl.when(r == 3)
    def _():
        R.d2[OD] = jnp.zeros(R.d2.shape[1:], BF)

    def even_rows():
        return jnp.concatenate([R.x0[2 * o, 0:S, :] for o in range(OD)], axis=0)

    staged(cfg.rows["w_shortcut"], cfg.offs["w_shortcut"], fill_out(even_rows, R.dzs))

    @pl.when(r < 3)
    def _():
        up.wait_recv()

    @pl.when(r > 0)
    def _():
        up.wait_send()

    def d2_left(j):
        cols = aligned(j, LANES)
        for k in range(OD + 1):
            R.d2l[k, :, cols] = rolled(R.d2[k, :, cols].astype(F32), -1).astype(BF)

    loop(MID // LANES, d2_left)

    def spatial_back(j):
        here, left = R.d2[0:OD].reshape(M, MID), R.d2l[0:OD].reshape(M, MID)
        below, below_left = R.d2[1 : OD + 1].reshape(M, MID), R.d2l[1 : OD + 1].reshape(M, MID)

        def w(dr, dc):
            return R.f_w_spatial[dr * 3 + dc, aligned(j, 2)].reshape(MID // 2, MID)

        cols = aligned(j, MID // 2)
        parts = (
            ((here, 1, 1),),
            ((here, 1, 2), (left, 1, 0)),
            ((here, 2, 1), (below, 0, 1)),
            ((here, 2, 2), (left, 2, 0), (below, 0, 2), (below_left, 0, 0)),
        )
        for i, terms in enumerate(parts):
            rp, cp = divmod(i, 2)
            acc = None
            for v, dr, dc in terms:
                y = dot_t(v, w(dr, dc))
                acc = y if acc is None else acc + y
            for o in range(OD):
                R.dh1[2 * o + rp, out_rows(cp), cols] = acc[out_rows(o)]

    loop(2, spatial_back)

    def h1_back(j):
        cols = aligned(j, LANES)
        sums = mid_at(R.t1, j)
        sc, sh = forward_terms(sums, R.norm_reduce, cols, IN)
        xa, xs = xhat_terms(sums, IN)
        ch = keep(R.chan_mid, cols)
        g0 = jnp.zeros((S, LANES), F32)
        g1 = jnp.zeros((S, LANES), F32)
        for k in range(RD):
            for p in range(2):
                rows = out_rows(p)
                v = R.z1[k, rows, cols]
                d = R.dh1[k, rows, cols] * (ch * R.pix_in[k, rows, :]) * slope(v * sc + sh)
                R.dh1[k, rows, cols] = d
                g0 = g0 + d * (v * xa + xs)
                g1 = g1 + d
        st = mid_at(R.loc, j)
        group_rows(st, 0, g0)
        group_rows(st, 3, g1)
        blank(st, 6, 2)

    loop(MID // LANES, h1_back)
    mid_start(7)
    staged(
        cfg.rows["w_spatial"],
        cfg.offs["w_spatial"],
        fill_conv(R.win1, lambda: R.d2[0:OD].reshape(M, MID)),
    )

    def short_back(j):
        n = CIN // 4
        R.short[:, aligned(j, n)] = dot_t(R.dzs[...], R.f_w_shortcut[j])

    loop(4, short_back)
    mid_finish(7, R.g1)

    def h1_apply(j):
        cols = aligned(j, LANES)
        f, a, bz = backward_terms(mid_at(R.t1, j), mid_at(R.g1, j), R.norm_reduce, cols, IN)
        for k in range(RD):
            for p in range(2):
                rows = out_rows(p)
                d = f * R.dh1[k, rows, cols] - a - R.z1[k, rows, cols] * bz
                R.dz1[k, rows, cols] = (d * R.pix_in[k, rows, :]).astype(BF)

    loop(MID // LANES, h1_apply)

    def fill_reduce(stage):
        n = CIN // 32

        def body(j):
            act = R.x0[:, :, aligned(j, 256)].reshape(RD * 2 * S, 256)
            res = dot_w(act, R.dz1[...].reshape(RD * 2 * S, MID))
            c = 256 // (4 * n)
            stage[pl.ds(j * c, c), :, 0:n, :] = res.reshape(c, 4, n, MID).astype(BF)

        loop(CIN // 256, body)

    staged(cfg.rows["w_reduce"], cfg.offs["w_reduce"], fill_reduce)

    def input_grad(j):
        cols = aligned(j, CIN // 4)
        w = R.f_w_reduce[j]
        ch = jnp.concatenate(
            [keep(R.chan_in, pl.ds(pl.multiple_of(j * (CIN // 4) + i * LANES, LANES), LANES)) for i in range(CIN // 4 // LANES)],
            axis=1,
        )
        for k in range(RD):
            y = dot_t(R.dz1[k], w)
            for p in range(2):
                v = y[out_rows(p)]
                if p == 0 and k % 2 == 0:
                    v = v + R.short[out_rows(k // 2), cols]
                pix = R.pix_in[k, out_rows(p), :]
                R.gin[k, out_rows(p), cols] = v * ch * jnp.concatenate([pix] * (CIN // 4 // LANES), axis=1)

    loop(4, input_grad)

    for name, n in (("g1", 0), ("g2", 0), ("g4", 0), ("g5", 0)):
        out, src = getattr(R, "o" + name), getattr(R, name)
        out[...] = src[...]
    R.og3[...] = R.g3[...]
    R.og6[...] = R.g6[...]

    own.wait()
    mixed_copies[0].wait()
    mixed_copies[1].wait_send()
    onward.wait()
    for u in range(len(units)):
        for i in range(5):
            w_copy(u, i).wait_send()
    for copy in grad_out:
        if copy is not None:
            copy.wait()


def plan(features, w_reduce, w_expand, batch):
    images, rd, _, cin = features.shape
    mid, wide = w_reduce.shape[1], w_expand.shape[1]
    cfg = SimpleNamespace(
        slots=-(-images * 8 // 16) * 16, in_rows=rd, out_rows=rd // 2, batch=batch, mid=mid, wide=wide, cin=cin
    )
    q = (cin // 4, mid // 4, wide // 4)
    cfg.units = (
        [("w_reduce", False, 0, q[0])]
        + [("w_spatial", True, k, 3) for k in (0, 3, 6)]
        + [("w_expand", False, 0, q[1])]
        + [("w_shortcut", False, k * q[0] // 2, q[0] // 2) for k in (0, 1)]
        + [("w_squeeze", False, 0, q[2])]
        + [("w_mixing", True, k, 3) for k in (0, 3, 6)]
        + [("w_widen", False, 0, q[1])]
    )
    cfg.rows = {
        "w_reduce": cin // 32,
        "w_spatial": 9 * mid // 32,
        "w_expand": mid // 8,
        "w_shortcut": cin // 8,
        "w_squeeze": wide // 32,
        "w_mixing": 9 * mid // 32,
        "w_widen": mid // 8,
    }
    cfg.offs, total = {}, 0
    for name, n in cfg.rows.items():
        cfg.offs[name] = total
        total += n
    cfg.total = total
    return cfg


def run_blocks(cfg, vmem_args, hbm_args):
    S, RD, OD, NB = cfg.slots, cfg.in_rows, cfg.out_rows, cfg.batch
    MID, WIDE, CIN = cfg.mid, cfg.wide, cfg.cin
    M = OD * S
    U = len(cfg.units)
    vmem = pl.BlockSpec(memory_space=pltpu.VMEM)
    hbm = pl.BlockSpec(memory_space=pl.ANY)
    sds = jax.ShapeDtypeStruct
    outs = {
        "mixed": (sds((4, OD, S, WIDE), BF), hbm),
        "grads": (sds((8, 4, cfg.total, 512), BF), hbm),
        "gin": (sds((RD, 2 * S, CIN), F32), vmem),
        "og1": (sds((2, 8, MID // 2), F32), vmem),
        "og2": (sds((2, 8, MID // 2), F32), vmem),
        "og3": (sds((4, 16, WIDE // 4), F32), vmem),
        "og4": (sds((2, 8, MID // 2), F32), vmem),
        "og5": (sds((2, 8, MID // 2), F32), vmem),
        "og6": (sds((4, 8, WIDE // 4), F32), vmem),
    }
    V = pltpu.VMEM
    mid_tot = V((2, 8, MID // 2), F32)
    scratch = {
        "f_w_reduce": V((4, CIN // 4, MID), BF),
        "f_w_spatial": V((9, 4, MID // 4, MID), BF),
        "f_w_expand": V((4, MID // 4, WIDE), BF),
        "f_w_shortcut": V((4, CIN // 4, WIDE), BF),
        "f_w_squeeze": V((4, WIDE // 4, MID), BF),
        "f_w_mixing": V((9, 4, MID // 4, MID), BF),
        "f_w_widen": V((4, MID // 4, WIDE), BF),
        "z1": V((RD, 2 * S, MID), F32),
        "win1": V((M, 9 * MID), BF),
        "h1s": V((2, S, MID), BF),
        "h1r": V((2, S, MID), BF),
        "z2": V((M, MID), F32),
        "h2": V((M, MID), BF),
        "z3": V((M, WIDE), F32),
        "zs": V((M, WIDE), F32),
        "y1": V((M, WIDE), BF),
        "z4": V((M, MID), F32),
        "h4": V((OD + 2, S, MID), BF),
        "win4": V((M, 9 * MID), BF),
        "z5": V((M, MID), F32),
        "h5": V((M, MID), BF),
        "z6": V((M, WIDE), F32),
        "mixed_local": V((OD, S, WIDE), BF),
        "du2": V((M, WIDE), F32),
        "dz6": V((M, WIDE), BF),
        "dh": V((M, MID), F32),
        "d5": V((OD + 2, S, MID), BF),
        "win5": V((M, 9 * MID), BF),
        "dz4": V((M, MID), BF),
        "du1": V((M, WIDE), F32),
        "dz3": V((M, WIDE), BF),
        "dzs": V((M, WIDE), BF),
        "d2": V((OD + 1, S, MID), BF),
        "d2l": V((OD + 1, S, MID), BF),
        "dh1": V((RD, 2 * S, MID), F32),
        "dz1": V((RD, 2 * S, MID), BF),
        "short": V((M, CIN), F32),
        "stage": V((2, 8, 4, max(cfg.rows.values()), 512), BF),
        "loc": mid_tot,
        "locw": V((4, 8, WIDE // 4), F32),
        "locw2": V((4, 16, WIDE // 4), F32),
        "t1": mid_tot,
        "t2": mid_tot,
        "t3": V((4, 16, WIDE // 4), F32),
        "t4": mid_tot,
        "t5": mid_tot,
        "t6": V((4, 8, WIDE // 4), F32),
        "g1": mid_tot,
        "g2": mid_tot,
        "g3": V((4, 16, WIDE // 4), F32),
        "g4": mid_tot,
        "g5": mid_tot,
        "g6": V((4, 8, WIDE // 4), F32),
        "rc": V((2, 8, MID // 2), F32),
        "rq": V((2, 2 * NB, 8, MID // 2), F32),
        "rw": V((4, 4, 16, WIDE // 4), F32),
        "wb": V((2, NB, 16, WIDE // 4), F32),
        "wsend": pltpu.SemaphoreType.DMA((U, 5)),
        "wrecv": pltpu.SemaphoreType.DMA((U, 5)),
        "wloc": pltpu.SemaphoreType.DMA((U,)),
        "ms": pltpu.SemaphoreType.DMA((3,)),
        "mr": pltpu.SemaphoreType.DMA((3, 2)),
        "ws": pltpu.SemaphoreType.DMA((4, 3)),
        "wr": pltpu.SemaphoreType.DMA((4, 3)),
        "hs": pltpu.SemaphoreType.DMA((2,)),
        "hr": pltpu.SemaphoreType.DMA((2,)),
        "es": pltpu.SemaphoreType.DMA((2, 2)),
        "er": pltpu.SemaphoreType.DMA((2, 2)),
        "xs": pltpu.SemaphoreType.DMA((3,)),
        "xr": pltpu.SemaphoreType.DMA((3,)),
        "xl": pltpu.SemaphoreType.DMA,
        "gs": pltpu.SemaphoreType.DMA((2,)),
    }
    names = list(vmem_args) + list(hbm_args) + list(outs) + list(scratch)
    res = pl.pallas_call(
        functools.partial(block_kernel, names, cfg),
        out_shape=[o[0] for o in outs.values()],
        in_specs=[vmem] * len(vmem_args) + [hbm] * len(hbm_args),
        out_specs=[o[1] for o in outs.values()],
        scratch_shapes=list(scratch.values()),
        compiler_params=pltpu.CompilerParams(
            collective_id=0, has_side_effects=True, vmem_limit_bytes=63 * 2**20
        ),
    )(*vmem_args.values(), *hbm_args.values())
    return SimpleNamespace(**dict(zip(outs, res)))


def slot_layout(x, slots):
    images, rows, cols, channels = x.shape
    x = jnp.transpose(x, (1, 0, 2, 3)).reshape(rows, images * cols, channels)
    return jnp.pad(x, ((0, 0), (0, slots - images * cols), (0, 0)))


def lanes(x):
    return jnp.broadcast_to(x[..., None], x.shape + (LANES,))


def pad8(x):
    x = x.reshape(-1, x.shape[-1])
    return jnp.pad(x, ((0, 8 - x.shape[0]), (0, 0)))


def unfold_mid(g):
    return jnp.transpose(g, (1, 0, 2)).reshape(8, -1)


def per_device(
    features, w_reduce, w_spatial, w_expand, w_shortcut, w_squeeze, w_mixing, w_widen,
    norm_reduce, norm_spatial, norm_expand, norm_shortcut, norm_squeeze, norm_mixing, norm_widen,
    cotangent, resolution, active,
):
    images, rd, cols_in, cin = features.shape
    od = rd // 2
    nb = lax.axis_size("batch")
    cfg = plan(features, w_reduce, w_expand, nb)
    S, mid, wide = cfg.slots, cfg.mid, cfg.wide
    groups = jnp.arange(3, dtype=jnp.int32)
    members = jnp.sum((resolution[:, None] == groups[None, :]).astype(F32), axis=0)
    sides_grp = 10.0 + 2.0 * groups.astype(F32)
    count_in = members * sides_grp * sides_grp
    count_out = members * (sides_grp * 0.5) * (sides_grp * 0.5)
    counts = jnp.concatenate([1.0 / count_in, 1.0 / count_out, jnp.zeros((2,), F32)])
    local_res = lax.dynamic_slice_in_dim(resolution, lax.axis_index("batch") * images, images)
    row = lax.axis_index("rows")
    slot_res = jnp.pad(jnp.repeat(local_res, 8), (0, S - 8 * images), constant_values=-1)
    slot_col = jnp.pad(jnp.tile(jnp.arange(8, dtype=jnp.int32), images), (0, S - 8 * images))
    onehot = (slot_res[None, :] == groups[:, None]).astype(F32)
    side_out = jnp.where(slot_res >= 0, 5 + slot_res, 0)
    rows_out = row * od + jnp.arange(od, dtype=jnp.int32)
    rows_in = row * rd + jnp.arange(rd, dtype=jnp.int32)
    pix_out = ((rows_out[:, None] < side_out[None, :]) & (slot_col[None, :] < side_out[None, :])).astype(F32)
    parity = jnp.arange(2, dtype=jnp.int32)
    pix_in = (
        (rows_in[:, None, None] < 2 * side_out[None, None, :])
        & ((2 * slot_col[None, None, :] + parity[None, :, None]) < 2 * side_out[None, None, :])
    ).astype(F32)

    def chan(width):
        limit = active * (width // mid)
        return pad8((jnp.arange(width, dtype=jnp.int32)[None, :] < limit[:, None]).astype(F32))

    chan_in = chan(cin)
    x = jnp.pad(features, ((0, 0), (0, 0), (0, 16 - cols_in), (0, 0)))
    x = x.reshape(images, rd, 8, 2, cin)
    x = jnp.transpose(x, (1, 3, 0, 2, 4)).reshape(rd, 2, images * 8, cin)
    x = jnp.pad(x, ((0, 0), (0, 0), (0, S - images * 8), (0, 0)))
    slot_chan = jnp.where(slot_res[:, None] == 0, chan_in[0:1], jnp.where(slot_res[:, None] == 1, chan_in[1:2], chan_in[2:3]))
    x0 = jnp.where((pix_in[..., None] * slot_chan[None, None]) > 0, x, jnp.zeros((), BF)).reshape(rd, 2 * S, cin)
    ct = slot_layout(jnp.pad(cotangent, ((0, 0), (0, 0), (0, 8 - cotangent.shape[2]), (0, 0))), S)

    vmem_args = {
        "x0": x0,
        "cotangent": ct.reshape(od * S, wide),
        "pix_in": lanes(pix_in).reshape(rd, 2 * S, LANES),
        "pix_out": lanes(pix_out).reshape(od * S, LANES),
        "onehot": lanes(onehot),
        "counts": lanes(counts),
        "chan_mid": chan(mid),
        "chan_wide": chan(wide),
        "chan_in": chan_in,
        "norm_reduce": pad8(norm_reduce),
        "norm_spatial": pad8(norm_spatial),
        "norm_expand": pad8(norm_expand),
        "norm_shortcut": pad8(norm_shortcut),
        "norm_squeeze": pad8(norm_squeeze),
        "norm_mixing": pad8(norm_mixing),
        "norm_widen": pad8(norm_widen),
    }
    hbm_args = {
        "w_reduce": w_reduce,
        "w_spatial": w_spatial.reshape(9, -1, mid),
        "w_expand": w_expand,
        "w_shortcut": w_shortcut,
        "w_squeeze": w_squeeze,
        "w_mixing": w_mixing.reshape(9, -1, mid),
        "w_widen": w_widen,
    }
    res = run_blocks(cfg, vmem_args, hbm_args)
    out_cols = cotangent.shape[2]
    mixed = res.mixed.reshape(4 * od, S, wide)[:, : images * 8].reshape(4 * od, images, 8, wide)
    mixed = jnp.transpose(mixed, (1, 0, 2, 3))[:, :, :out_cols]
    gin = res.gin.reshape(rd, 2, S, cin)[:, :, : images * 8].reshape(rd, 2, images, 8, cin)
    gin = jnp.transpose(gin, (2, 0, 3, 1, 4)).reshape(images, rd, 16, cin)[:, :, :cols_in]

    def unpack(grads, name, b8):
        g = grads[:, :, cfg.offs[name] : cfg.offs[name] + cfg.rows[name]]
        n = cfg.rows[name]
        if name in ("w_spatial", "w_mixing"):
            k = n // 9
            return jnp.transpose(g.reshape(b8, 4, 9, k, 512), (2, 0, 1, 3, 4)).reshape(3, 3, b8 * 4 * k, 512)
        if name in ("w_expand", "w_shortcut", "w_widen"):
            return jnp.transpose(g, (0, 2, 1, 3)).reshape(b8 * n, 2048)
        return g.reshape(b8 * 4 * n, 512)

    order = ("w_reduce", "w_spatial", "w_expand", "w_shortcut", "w_squeeze", "w_mixing", "w_widen")
    totals = []
    for name in order:
        part = unpack(res.grads, name, 8)
        dim = 2 if part.ndim == 4 else 0
        part = lax.psum_scatter(part, "batch", scatter_dimension=dim, tiled=True)
        totals.append(lax.psum(part, "rows").astype(F32))

    def mid_norm(g):
        return unfold_mid(g)[:6].reshape(2, 3, mid)

    def wide_norm(g):
        return jnp.transpose(g, (1, 0, 2)).reshape(g.shape[1], wide)

    g3 = wide_norm(res.og3)
    return (
        mixed,
        gin,
        *totals,
        mid_norm(res.og1),
        mid_norm(res.og2),
        g3[:6].reshape(2, 3, wide),
        jnp.concatenate([g3[8:11], g3[3:6]]).reshape(2, 3, wide),
        mid_norm(res.og4),
        mid_norm(res.og5),
        wide_norm(res.og6)[:6].reshape(2, 3, wide),
    )


def solution(mesh):
    w2, w4 = P("rows", None), P(None, None, "rows", None)
    o2, o4 = P("batch", None), P(None, None, "batch", None)
    return jax.shard_map(
        per_device,
        mesh=mesh,
        in_specs=(P("batch", "rows", None, None), w2, w4, w2, w2, w2, w4, w2)
        + (P(),) * 7
        + (P("batch", "rows", None, None), P(), P()),
        out_specs=(P("batch", None, None, None), P("batch", "rows", None, None), o2, o4, o2, o2, o2, o4, o2)
        + (P(),) * 7,
        check_vma=False,
    )
```

```python
import functools
from types import SimpleNamespace

import jax
import jax.numpy as jnp
from jax import lax
from jax.experimental import pallas as pl
from jax.experimental.pallas import tpu as pltpu
from jax.sharding import PartitionSpec as P

eps = 1e-05
MESH = pl.DeviceIdType.MESH
BF = jnp.bfloat16
F32 = jnp.float32
LANES = 128
REDUCE, SPATIAL, EXPAND, SHORTCUT, SQUEEZE, MIXING, WIDEN = range(7)
DX, DY, DN, DF = range(4)


def dot(a, b):
    return jnp.dot(a, b, preferred_element_type=F32)


def dot_t(a, b):
    return lax.dot_general(a, b, (((1,), (1,)), ((), ())), preferred_element_type=F32)


def dot_w(a, b):
    return lax.dot_general(a, b, (((0,), (0,)), ((), ())), preferred_element_type=F32)


def aligned(index, size):
    return pl.ds(pl.multiple_of(index * size, size), size)


def loop(count, body):
    def step(i, carry):
        body(i)
        return carry

    lax.fori_loop(0, count, step, 0)


def silu_parts(u):
    s = jax.nn.sigmoid(u)
    return s, u * s


def slope(u):
    s = jax.nn.sigmoid(u)
    return s * (1.0 + u * (1.0 - s))


def block_kernel(names, cfg, *refs):
    R = SimpleNamespace(**dict(zip(names, refs)))
    S, RD, OD, NB = cfg.slots, cfg.in_rows, cfg.out_rows, cfg.batch
    MID, WIDE, CIN = cfg.mid, cfg.wide, cfg.cin
    M = OD * S
    b = lax.axis_index("batch")
    r = lax.axis_index("rows")
    core = lax.rem(r, 2)
    xb = lax.div(r, 2)
    core_peer = r + 1 - 2 * core
    x_row = lax.rem(r + 2, 4)
    diag = 3 - r
    half = lax.rem(b, 2)
    y_b = b + 1 - 2 * half

    def flip(i, j):
        out = jnp.int32(0)
        bit = 1
        while bit < 2 * NB:
            p, q = lax.rem(lax.div(i, bit), 2), lax.rem(lax.div(j, bit), 2)
            out = out + bit * (p + q - 2 * p * q)
            bit *= 2
        return out

    me = b * 2 + xb

    def remote(src, dst, send, recv, dev):
        return pltpu.make_async_remote_copy(
            src_ref=src, dst_ref=dst, send_sem=send, recv_sem=recv, device_id=dev, device_id_type=MESH
        )

    def team(id2):
        return (lax.div(id2, 2), 2 * lax.rem(id2, 2) + core)

    units = cfg.units
    wsend, wrecv, wloc = R.wsend, R.wrecv, R.wloc

    def wview(u, shard, part):
        w, k0, kn = units[u]
        start, size = k0, kn
        if part is not None:
            size = kn // 2
            start = k0 + part * size
        full = getattr(R, "f" + str(w))
        return full.at[pl.ds(pl.multiple_of(shard * (full.shape[0] // 4) + start, 16), size)]

    def w_copy(u, i):
        if i < 2:
            view = wview(u, r, None if i == 0 else half)
            dev = (b, core_peer) if i == 0 else (b, x_row)
        else:
            view = wview(u, x_row, 1 - half if i == 4 else half)
            dev = (y_b, r) if i == 3 else (b, core_peer)
        return remote(view, view, wsend.at[u, i], wrecv.at[u, i], dev)

    def w_local(w):
        src, full = getattr(R, "w" + str(w)), getattr(R, "f" + str(w))
        n, quarter = src.shape[0], full.shape[0] // 4
        return [
            pltpu.make_async_copy(
                src.at[:, pl.ds(512 * i, 512)],
                full.at[pl.ds(pl.multiple_of(r * quarter + i * n, 16), n)],
                wloc.at[w, i],
            )
            for i in range(src.shape[1] // 512)
        ]

    loaded = [w_local(w) for w in range(7)]
    for w in range(7):
        for c in loaded[w]:
            c.start()
        if w == 0:
            x0_load = pltpu.make_async_copy(R.features, R.x0, R.ld.at[0])
            x0_load.start()
    ct_load = pltpu.make_async_copy(R.cotangent, R.ct, R.ld.at[1])
    ct_load.start()
    at_home = set()

    images = cfg.images
    column = lax.broadcasted_iota(jnp.int32, (8, LANES), 0).astype(F32)
    if 8 * images < S:
        tail = slice(8 * images, S)
        none = jnp.zeros((S - 8 * images, LANES), F32)
        R.active_slot[tail, :] = none
        for g in range(3):
            R.onehot[g, tail, :] = none
        for o in range(OD):
            R.pix_out[o * S + 8 * images : (o + 1) * S, :] = none
        for k in range(RD):
            for p in range(2):
                R.pix_in[k, p * S + 8 * images : (p + 1) * S, :] = none

    for i in range(images):
        group = R.resolution[b * images + i]
        side = (5 + group).astype(F32)
        here = slice(8 * i, 8 * i + 8)
        limit = jnp.zeros((8, LANES), F32)
        for g in range(3):
            is_g = jnp.where(group == g, 1.0, 0.0)
            R.onehot[g, here, :] = jnp.full((8, LANES), is_g, F32)
            limit = limit + is_g * R.active[g].astype(F32)
        R.active_slot[here, :] = limit
        for o in range(OD):
            inside = jnp.where((r * OD + o).astype(F32) < side, side, 0.0)
            R.pix_out[o * S + 8 * i : o * S + 8 * i + 8, :] = jnp.where(column < inside, 1.0, 0.0)
        for k in range(RD):
            inside = jnp.where((r * RD + k).astype(F32) < 2.0 * side, 2.0 * side, 0.0)
            for p in range(2):
                R.pix_in[k, p * S + 8 * i : p * S + 8 * i + 8, :] = jnp.where(2.0 * column + p < inside, 1.0, 0.0)

    bar = pltpu.get_barrier_semaphore()
    for dev in ((b, core_peer), (b, diag)):
        pl.semaphore_signal(bar, inc=1, device_id=dev, device_id_type=MESH)

    def greet(j):
        pl.semaphore_signal(bar, inc=1, device_id=team(flip(me, j + 1)), device_id_type=MESH)

    loop(2 * NB - 1, greet)
    pl.semaphore_wait(bar, 2 * NB + 1)

    def w_start(u):
        w = units[u][0]
        if w not in at_home:
            at_home.add(w)
            for c in loaded[w]:
                c.wait()
        w_copy(u, 1).start()
        w_copy(u, 0).start()

    def w_second(u):
        w_copy(u, 1).wait_recv()
        w_copy(u, 3).start()
        w_copy(u, 2).start()

    def w_third(u):
        w_copy(u, 3).wait_recv()
        w_copy(u, 4).start()

    def w_ready(u):
        for i in (0, 2, 4):
            w_copy(u, i).wait_recv()

    pumped = [0]

    def pump(steps):
        for _ in range(steps):
            n = pumped[0]
            if n >= len(units) + 2:
                return
            if n < len(units):
                w_start(n)
            if 0 <= n - 1 < len(units):
                w_second(n - 1)
            if 0 <= n - 2 < len(units):
                w_third(n - 2)
            pumped[0] = n + 1

    def need(name):
        last = max(u for u in range(len(units)) if units[u][0] == name)
        while pumped[0] < last + 3:
            pump(1)
        for u in range(len(units)):
            if units[u][0] == name:
                w_ready(u)

    def mid_start(k):
        p = k % 2
        swap = remote(R.loc.at[1 - core], R.rc.at[p], R.ms.at[0], R.mr.at[0, p], (b, core_peer))
        swap.start()
        swap.wait_recv()
        R.rq[p, me] = R.loc[core] + R.rc[p]

        def send(j):
            to = team(flip(me, j + 1))
            remote(R.rq.at[p, me], R.rq.at[p, me], R.ms.at[1], R.mr.at[1, p], to).start()

        loop(2 * NB - 1, send)
        swap.wait_send()

    def mid_finish(k, tot):
        p = k % 2
        rest = R.rq.at[p, pl.ds(0, 2 * NB - 1)]
        every = remote(rest, rest, R.ms.at[1], R.mr.at[1, p], (b, x_row))
        every.wait_recv()
        total = R.rq[p, 0]
        for j in range(1, 2 * NB):
            total = total + R.rq[p, j]
        tot[core] = total
        back = remote(tot.at[core], tot.at[core], R.ms.at[2], R.mr.at[2, p], (b, core_peer))
        back.start()
        every.wait_send()
        back.wait()

    def wide_start(k, loc):
        n = loc.shape[1]
        rw, wb = R.rw.at[k % 2, :, pl.ds(0, n)], R.wb.at[k % 2, :, pl.ds(0, n)]
        rw[r] = loc[r]
        for to in (core_peer, x_row, diag):
            remote(loc.at[to], rw.at[r], R.ws.at[k, 0], R.wr.at[k, 0], (b, to)).start()
        three = remote(loc.at[pl.ds(0, 3)], rw.at[pl.ds(0, 3)], R.ws.at[k, 0], R.wr.at[k, 0], (b, core_peer))
        three.wait_recv()
        wb[b] = rw[0] + rw[1] + (rw[2] + rw[3])

        def send(j):
            to = lax.rem(b + j + 1, NB)
            remote(wb.at[b], wb.at[b], R.ws.at[k, 1], R.wr.at[k, 1], (to, r)).start()

        loop(NB - 1, send)
        three.wait_send()

    def wide_finish(k, tot):
        n = tot.shape[1]
        wb = R.wb.at[k % 2, :, pl.ds(0, n)]
        rest = wb.at[pl.ds(0, NB - 1)]
        every = remote(rest, rest, R.ws.at[k, 1], R.wr.at[k, 1], (b, x_row))
        every.wait_recv()
        total = wb[0]
        for j in range(1, NB):
            total = total + wb[j]
        tot[r] = total
        for to in (core_peer, x_row, diag):
            remote(tot.at[r], tot.at[r], R.ws.at[k, 2], R.wr.at[k, 2], (b, to)).start()
        three = remote(tot.at[pl.ds(0, 3)], tot.at[pl.ds(0, 3)], R.ws.at[k, 2], R.wr.at[k, 2], (b, core_peer))
        every.wait_send()
        three.wait()

    def mid_at(ref, j):
        return ref.at[lax.div(j, 2), :, aligned(lax.rem(j, 2), LANES)]

    def wide_at(ref, j):
        return ref.at[lax.div(j, 4), :, aligned(lax.rem(j, 4), LANES)]

    def group_rows(ref, row, values):
        for g in range(3):
            ref[row + g : row + g + 1, :] = jnp.sum(values * R.onehot[g], axis=0, keepdims=True)

    def blank(ref, row, rows):
        ref[row : row + rows, :] = jnp.zeros((rows, LANES), F32)

    def spread(rows3):
        return rows3[0] * R.onehot[0] + rows3[1] * R.onehot[1] + rows3[2] * R.onehot[2]

    def moments(sums, inv_n, row=0):
        means, invs = [], []
        for g in range(3):
            n = 1.0 / inv_n[g]
            mean = sums[row + g : row + g + 1, :] * n
            var = sums[row + 3 + g : row + 4 + g, :] * n - mean * mean
            means.append(mean)
            invs.append(lax.rsqrt(var + eps))
        return means, invs

    OUT = [cfg.members * (5.0 + g) * (5.0 + g) for g in range(3)]
    IN = [cfg.members * (10.0 + 2.0 * g) * (10.0 + 2.0 * g) for g in range(3)]

    def forward_terms(sums, params, cols, inv_n, row=0):
        means, invs = moments(sums, inv_n, row)
        scales = [invs[g] * params[0, g : g + 1, cols] for g in range(3)]
        shifts = [params[1, g : g + 1, cols] - means[g] * scales[g] for g in range(3)]
        return spread(scales), spread(shifts)

    def xhat_terms(sums, inv_n, row=0):
        means, invs = moments(sums, inv_n, row)
        return spread(invs), spread([-means[g] * invs[g] for g in range(3)])

    def backward_terms(sums, grads, params, cols, inv_n, row=0, g0=0, g1=3):
        means, invs = moments(sums, inv_n, row)
        fs, az, bz = [], [], []
        for g in range(3):
            n = 1.0 / inv_n[g]
            f = invs[g] * params[0, g : g + 1, cols]
            gain = grads[g0 + g : g0 + g + 1, :] * n * invs[g]
            bias = grads[g1 + g : g1 + g + 1, :] * n
            fs.append(f)
            bz.append(f * gain)
            az.append(f * (bias - means[g] * gain))
        return spread(fs), spread(az), spread(bz)

    def keep(j, ratio):
        lane = lax.broadcasted_iota(jnp.int32, (S, LANES), 1).astype(F32) + j * float(LANES)
        return jnp.where(lane < R.active_slot[...] * ratio, 1.0, 0.0)

    def out_rows(k):
        return slice(k * S, (k + 1) * S)

    def groups16(o):
        return slice(o * (S // 16), (o + 1) * (S // 16))

    def forward_stats(z, loc_at, row=0):
        def body(j):
            cols = aligned(j, LANES)
            s = jnp.zeros((S, LANES), F32)
            q = jnp.zeros((S, LANES), F32)
            for o in range(OD):
                v = z[out_rows(o), cols]
                m = v * R.pix_out[out_rows(o), :]
                s = s + m
                q = q + m * v
            st = loc_at(j)
            group_rows(st, row, s)
            group_rows(st, row + 3, q)
            blank(st, row + 6, 2)

        loop(z.shape[-1] // LANES, body)

    def rolled(v, by):
        return pltpu.roll(v, by % S, 0)

    def by_shard(t, j):
        return pl.ds(pl.multiple_of(j * (9 * LANES) + t * LANES, LANES), LANES)

    def by_tap(t, j):
        return pl.ds(pl.multiple_of(t * MID + j * LANES, LANES), LANES)

    def unit_windows(halo, win, rows, flipped):
        place = by_tap if flipped else by_shard

        def body(j):
            cols = aligned(j, LANES)
            for k in rows:
                v = halo[k, :, cols].astype(F32)
                moved = (rolled(v, 1).astype(BF), v.astype(BF), rolled(v, -1).astype(BF))
                for dr in range(3):
                    o = k - dr
                    if not 0 <= o < OD:
                        continue
                    for dc in range(3):
                        t = (2 - dr) * 3 + 2 - dc if flipped else dr * 3 + dc
                        win[out_rows(o), place(t, j)] = moved[dc]

        loop(MID // LANES, body)

    def edge_exchange(halo, k):
        up = remote(halo.at[1], halo.at[OD + 1], R.es.at[k, 0], R.er.at[k, 0], (b, jnp.maximum(r - 1, 0)))
        down = remote(halo.at[OD], halo.at[0], R.es.at[k, 1], R.er.at[k, 1], (b, jnp.minimum(r + 1, 3)))

        @pl.when(r > 0)
        def _():
            up.start()

        @pl.when(r < 3)
        def _():
            down.start()

        @pl.when(r == 0)
        def _():
            halo[0] = jnp.zeros(halo.shape[1:], BF)

        @pl.when(r == 3)
        def _():
            halo[OD + 1] = jnp.zeros(halo.shape[1:], BF)

        return up, down

    def edge_wait(pair):
        up, down = pair

        @pl.when(r < 3)
        def _():
            up.wait_recv()
            down.wait_send()

        @pl.when(r > 0)
        def _():
            down.wait_recv()
            up.wait_send()

    pump(3)
    x0_load.wait()
    need(REDUCE)

    def z1_rows(k):
        def mask(j):
            cols = aligned(j, LANES)
            ch = keep(j, float(CIN // MID))
            for p in range(2):
                m = (ch * R.pix_in[k, out_rows(p), :]).astype(BF)
                R.x0[k, out_rows(p), cols] = R.x0[k, out_rows(p), cols] * m

        loop(CIN // LANES, mask)
        R.z1[k] = dot(R.x0[k], R.f0[...])

    loop(RD, z1_rows)

    def z1_stats(j):
        cols = aligned(j, LANES)
        s = jnp.zeros((S, LANES), F32)
        q = jnp.zeros((S, LANES), F32)
        for k in range(RD):
            for p in range(2):
                v = R.z1[k, out_rows(p), cols]
                m = v * R.pix_in[k, out_rows(p), :]
                s = s + m
                q = q + m * v
        st = mid_at(R.loc, j)
        group_rows(st, 0, s)
        group_rows(st, 3, q)
        blank(st, 6, 2)

    loop(MID // LANES, z1_stats)
    mid_start(0)
    pump(1)
    mid_finish(0, R.t1)

    last = RD - 1

    def h1_body(j):
        cols = aligned(j, LANES)
        sc, sh = forward_terms(mid_at(R.t1, j), R.norm_reduce, cols, IN)
        ch = keep(j, 1.0)
        for k in range(RD - 1, -1, -1):
            for p in range(2):
                u = R.z1[k, out_rows(p), cols] * sc + sh
                h = silu_parts(u)[1] * (ch * R.pix_in[k, out_rows(p), :])
                if k == last:
                    R.h1s[p, :, cols] = h.astype(BF)
                for dr in range(3):
                    o2 = k + 1 - dr
                    if o2 % 2 or not 0 <= o2 // 2 < OD:
                        continue
                    o = o2 // 2
                    taps = ((1, h),) if p == 0 else ((0, rolled(h, 1)), (2, h))
                    for dc, v in taps:
                        t = dr * 3 + dc
                        R.win1[out_rows(o), by_shard(t, j)] = v.astype(BF)

    loop(MID // LANES, h1_body)
    down = remote(R.h1s, R.h1r, R.hs.at[0], R.hr.at[0], (b, jnp.minimum(r + 1, 3)))

    @pl.when(r < 3)
    def _():
        down.start()

    pump(1)

    @pl.when(r > 0)
    def _():
        down.wait_recv()

    @pl.when(r == 0)
    def _():
        R.h1r[...] = jnp.zeros(R.h1r.shape, BF)

    def h1_halo(j):
        cols = aligned(j, LANES)
        even = R.h1r[0, :, cols]
        odd = R.h1r[1, :, cols]
        for dc, v in ((0, rolled(odd.astype(F32), 1).astype(BF)), (1, even), (2, odd)):
            R.win1[out_rows(0), by_shard(dc, j)] = v

    loop(MID // LANES, h1_halo)

    @pl.when(r < 3)
    def _():
        down.wait_send()

    need(SPATIAL)

    def conv(win, weight, z):
        def body(j):
            cols = aligned(j, 256)
            z[:, cols] = dot(win[...], weight[:, cols])

        loop(MID // 256, body)

    conv(R.win1, R.f1, R.z2)
    forward_stats(R.z2, lambda j: mid_at(R.loc, j))
    mid_start(1)
    pump(1)
    mid_finish(1, R.t2)

    def activate(z, tot, params, dest):
        def body(j):
            cols = aligned(j, LANES)
            sc, sh = forward_terms(mid_at(tot, j), params, cols, OUT)
            ch = keep(j, 1.0)
            for o in range(OD):
                u = z[out_rows(o), cols] * sc + sh
                dest(o, cols, (silu_parts(u)[1] * (ch * R.pix_out[out_rows(o), :])).astype(BF))

        loop(MID // LANES, body)

    def to_h2(o, cols, v):
        R.h2[out_rows(o), cols] = v

    activate(R.z2, R.t2, R.norm_spatial, to_h2)
    need(EXPAND)

    def piece(weight, shard, j):
        n = weight.shape[0] // 16
        return weight[pl.ds(pl.multiple_of((shard * 4 + j) * n, n), n), :]

    def block(weight, j):
        return jnp.concatenate([piece(weight, q, j) for q in range(4)], axis=0)

    def expand_to(h, weight, z):
        def body(j):
            z[:, aligned(j, 512)] = dot(h[...], block(weight, j))

        loop(WIDE // 512, body)

    expand_to(R.h2, R.f2, R.z3)
    need(SHORTCUT)

    def zs_body(j):
        cols = aligned(j, 512)
        w = block(R.f3, j)
        for o in range(OD):
            R.zs[out_rows(o), cols] = dot(R.x0[2 * o, 0:S, :], w)

    loop(WIDE // 512, zs_body)
    forward_stats(R.z3, lambda j: wide_at(R.locw2, j), 0)
    forward_stats(R.zs, lambda j: wide_at(R.locw2, j), 8)
    wide_start(0, R.locw2)
    pump(2)
    wide_finish(0, R.t3)

    def u1_terms(j):
        cols = aligned(j, LANES)
        tot = wide_at(R.t3, j)
        sc3, sh3 = forward_terms(tot, R.norm_expand, cols, OUT, 0)
        scs, shs = forward_terms(tot, R.norm_shortcut, cols, OUT, 8)
        shift = sh3 + shs

        def u1(o):
            return R.z3[out_rows(o), cols] * sc3 + R.zs[out_rows(o), cols] * scs + shift

        return u1

    def y1_body(j):
        cols = aligned(j, LANES)
        u1 = u1_terms(j)
        ch = keep(j, float(WIDE // MID))
        for o in range(OD):
            y = silu_parts(u1(o))[1] * (ch * R.pix_out[out_rows(o), :])
            R.y1[out_rows(o), cols] = y.astype(BF)

    loop(WIDE // LANES, y1_body)
    need(SQUEEZE)

    def squeeze_body(j):
        cols = aligned(j, 256)
        R.z4[:, cols] = dot(R.y1[...], R.f4[:, cols])

    loop(MID // 256, squeeze_body)
    forward_stats(R.z4, lambda j: mid_at(R.loc, j))
    mid_start(2)
    pump(2)
    mid_finish(2, R.t4)

    def to_h4(o, cols, v):
        R.h4[o + 1, :, cols] = v

    activate(R.z4, R.t4, R.norm_squeeze, to_h4)
    pair = edge_exchange(R.h4, 0)
    pump(1)
    unit_windows(R.h4, R.win4, range(1, OD + 1), False)
    edge_wait(pair)
    unit_windows(R.h4, R.win4, (0, OD + 1), False)
    need(MIXING)
    conv(R.win4, R.f5, R.z5)
    forward_stats(R.z5, lambda j: mid_at(R.loc, j))
    mid_start(3)
    pump(20)
    mid_finish(3, R.t5)

    def to_h5(o, cols, v):
        R.h5[out_rows(o), cols] = v

    activate(R.z5, R.t5, R.norm_mixing, to_h5)
    need(WIDEN)
    expand_to(R.h5, R.f6, R.z6)
    forward_stats(R.z6, lambda j: wide_at(R.locw, j))
    wide_start(1, R.locw)
    wide_finish(1, R.t6)
    for u in range(len(units)):
        for i in range(5):
            w_copy(u, i).wait_send()

    def u2_body(j):
        cols = aligned(j, LANES)
        tot = wide_at(R.t6, j)
        sc, sh = forward_terms(tot, R.norm_widen, cols, OUT)
        xa, xs = xhat_terms(tot, OUT)
        ch = keep(j, float(WIDE // MID))
        g0 = jnp.zeros((S, LANES), F32)
        g1 = jnp.zeros((S, LANES), F32)
        for o in range(OD):
            z = R.z6[out_rows(o), cols]
            u = z * sc + sh + R.y1[out_rows(o), cols].astype(F32)
            mask = ch * R.pix_out[out_rows(o), :]
            s, su = silu_parts(u)
            R.mixed_local[o, :, :, cols] = (su * mask).reshape(S // 8, 8, LANES).astype(BF)
            d = R.ct[out_rows(o), cols].astype(F32) * mask * (s * (1.0 + u * (1.0 - s)))
            R.du2[groups16(o), :, cols] = d.reshape(S // 16, 16, LANES)
            g0 = g0 + d * (z * xa + xs)
            g1 = g1 + d
        st = wide_at(R.locw, j)
        group_rows(st, 0, g0)
        group_rows(st, 3, g1)
        blank(st, 6, 2)

    ct_load.wait()
    loop(WIDE // LANES, u2_body)
    wide_start(2, R.locw)
    def mixed_copy(i, o):
        row = (x_row if i == 2 else r) * OD + o
        dst = R.mixed.at[:, row]
        src = dst if i == 2 else R.mixed_local.at[o, pl.ds(0, images)]
        if i == 3:
            return pltpu.make_async_copy(src, dst, R.xl.at[o])
        return remote(src, dst, R.xs.at[i, o], R.xr.at[i, o], (b, x_row if i == 1 else core_peer))

    for o in range(OD):
        for i in (1, 0, 3):
            mixed_copy(i, o).start()
    wide_finish(2, R.g6)

    def widen_back(j):
        cols = aligned(j, LANES)
        f, a, bz = backward_terms(wide_at(R.t6, j), wide_at(R.g6, j), R.norm_widen, cols, OUT)
        for o in range(OD):
            d = f * R.du2[groups16(o), :, cols].reshape(S, LANES) - a - R.z6[out_rows(o), cols] * bz
            R.dz6[out_rows(o), cols] = (d * R.pix_out[out_rows(o), :]).astype(BF)

    loop(WIDE // LANES, widen_back)

    mine = {DY: lax.rem(b, 2), DN: lax.rem(lax.div(b, 2), 2), DF: lax.div(b, 4), DX: xb}
    turn = [1]
    begun = {}

    def partner(d):
        other = 1 - 2 * mine[d]
        if d == DX:
            return (b, x_row)
        return (b + other * {DY: 1, DN: 2, DF: 4}[d], r)

    def put(stage, w, core_of, bits, start, value):
        for n0, np_, order in cfg.parts[w]:
            lo, hi = max(start, n0), min(start + value.shape[0], n0 + np_)
            if lo >= hi:
                continue
            idx = 0
            for d in order:
                idx = 2 * idx + bits[d]
            row = 32 * n0 + (core_of * 16 + idx) * np_ + lo - n0
            stage[pl.ds(row if isinstance(row, int) else pl.multiple_of(row, 16), hi - lo), :] = value[
                lo - start : hi - start
            ].astype(BF)

    def batch_bits(y, zn, zf, x):
        return {DY: y, DN: zn, DF: zf, DX: x}

    def staged(w, fill):
        i = turn[0] % 2
        turn[0] += 1
        stage = (R.stage0, R.stage1)[i]
        n = cfg.rows[w]
        assert 32 * n <= stage.shape[0], w
        if cfg.reduce:
            fill(stage)
            begun[w] = (stage, 0)
            for p in range(len(cfg.parts[w])):
                rs_core(w, p).start()
            return
        if i in begun:
            begun[i].wait()
        fill(stage)
        off = 32 * cfg.offs[w]
        begun[i] = pltpu.make_async_copy(
            stage.at[pl.ds(0, 32 * n)], R.grads.at[pl.ds(off, 32 * n)], R.gs.at[i]
        )
        begun[i].start()

    def land_of(w):
        return getattr(R, ("l" if w in cfg.own_landing else "f") + str(w))

    def rs_core(w, p):
        n0, np_, order = cfg.parts[w][p]
        stage = begun[w][0]
        src = stage.at[pl.ds(pl.multiple_of(32 * n0 + (1 - core) * 16 * np_, 16), 16 * np_)]
        dst = land_of(w).at[pl.ds(32 * n0, 16 * np_)]
        return remote(src, dst, R.rs.at[w, p, 0], R.rr.at[w, p, 0], (b, core_peer))

    def rs_kept(w, p, step):
        n0, np_, order = cfg.parts[w][p]
        at, size = 0, 16 * np_
        for d in order[:step]:
            size = size // 2
            at = at + mine[d] * size
        return at, size

    def rs_link(w, p, step):
        n0, np_, order = cfg.parts[w][p]
        at, size = rs_kept(w, p, step - 1)
        size = size // 2
        d = order[step - 1]
        src = land_of(w).at[pl.ds(pl.multiple_of(32 * n0 + at + (1 - mine[d]) * size, 16), size)]
        dst = land_of(w).at[pl.ds(32 * n0 + 32 * np_ - 2 * size, size)]
        i = w
        return remote(src, dst, R.rs.at[i, p, step], R.rr.at[i, p, step], partner(d))

    def final(w):
        return getattr(R, "e" + str(w))

    def rs_add(w, p, step):
        n0, np_, order = cfg.parts[w][p]
        land = land_of(w)
        at, size = rs_kept(w, p, step)
        if step == 0:
            other, start = begun[w][0], 32 * n0 + core * 16 * np_
        else:
            other, start = land, 32 * n0 + 32 * np_ - 2 * size
        last_step = step == 4

        def body(i):
            rows = pl.ds(pl.multiple_of(32 * n0 + at + i * np_, 16), np_)
            v = land[rows, :] + other[pl.ds(pl.multiple_of(start + i * np_, 16), np_), :]
            if not last_step:
                land[rows, :] = v
            elif w in (SPATIAL, MIXING):
                k = cfg.rows[w] // 9
                final(w)[n0 // k : (n0 + np_) // k] = v.reshape(np_ // k, k, 512)
            else:
                final(w)[n0 : n0 + np_, :] = v

        if size == np_:
            body(0)
        else:
            loop(size // np_, body)

    def home(w, row):
        out, n = getattr(R, "o" + str(w)), cfg.rows[w]
        if w in (SPATIAL, MIXING):
            return out.at[:, aligned(row, n // 9)]
        if w in (EXPAND, SHORTCUT, WIDEN):
            return out.at[:, aligned(row, 512)]
        return out.at[aligned(row, n)]

    def fin_copy(w, i):
        dst = home(w, x_row if i == 2 else r)
        src = dst if i == 2 else final(w)
        if i == 3:
            return pltpu.make_async_copy(src, dst, R.fl.at[w])
        return remote(src, dst, R.fs.at[w, i], R.fr.at[w, i], (b, x_row if i == 1 else core_peer))

    def rs_step(*kernels):
        if not cfg.reduce:
            return
        for w in kernels:
            stage, step = begun[w]
            if step == 5:
                fin_copy(w, 1).wait_recv()
                fin_copy(w, 2).start()
            else:
                for p in range(len(cfg.parts[w])):
                    c = rs_core(w, p) if step == 0 else rs_link(w, p, step)
                    c.wait_recv()
                    rs_add(w, p, step)
                    if step < 4:
                        rs_link(w, p, step + 1).start()
                    c.wait_send()
                if step == 4:
                    for i in (1, 0, 3):
                        fin_copy(w, i).start()
            begun[w] = (stage, step + 1)

    def rs_end():
        if not cfg.reduce:
            for copy in begun.values():
                copy.wait()
            return
        left = True
        while left:
            left = [w for w in cfg.rows if begun[w][1] < 6]
            if left:
                low = min(begun[w][1] for w in left)
                rs_step(*[w for w in left if begun[w][1] == low])
        for w in cfg.rows:
            fin_copy(w, 0).wait()
            fin_copy(w, 1).wait_send()
            fin_copy(w, 2).wait()
            fin_copy(w, 3).wait()

    def fill_out(w, act, dz):
        def fill(stage):
            def body(j):
                res = dot_w(act(), dz[:, aligned(j, 512)])
                n = res.shape[0] // 8
                for i in range(8):
                    bits = batch_bits(i % 2, i // 2 % 2, i // 4, lax.div(j, 2))
                    put(stage, w, lax.rem(j, 2), bits, 0, res[i * n : (i + 1) * n])

            loop(WIDE // 512, body)

        return fill

    def fill_conv(w, win, dz):
        def fill(stage):
            n = MID // 32

            def body(q):
                for t0 in range(0, 9, 3):
                    cols = pl.ds(pl.multiple_of(q * (9 * LANES) + t0 * LANES, LANES), 3 * LANES)
                    res = dot_w(win[:, cols], dz())
                    for t in range(3):
                        for i in range(8):
                            bits = batch_bits(i // 4, lax.rem(q, 2), lax.div(q, 2), i // 2 % 2)
                            at = t * LANES + i * n
                            put(stage, w, i % 2, bits, (t0 + t) * n, res[at : at + n])

            loop(4, body)

        return fill

    def mid_back_sums(dh, z, tot, params):
        def body(j):
            cols = aligned(j, LANES)
            sums = mid_at(tot, j)
            sc, sh = forward_terms(sums, params, cols, OUT)
            xa, xs = xhat_terms(sums, OUT)
            ch = keep(j, 1.0)
            g0 = jnp.zeros((S, LANES), F32)
            g1 = jnp.zeros((S, LANES), F32)
            for o in range(OD):
                v = z[out_rows(o), cols]
                d = dh[out_rows(o), cols] * (ch * R.pix_out[out_rows(o), :]) * slope(v * sc + sh)
                dh[out_rows(o), cols] = d
                g0 = g0 + d * (v * xa + xs)
                g1 = g1 + d
            st = mid_at(R.loc, j)
            group_rows(st, 0, g0)
            group_rows(st, 3, g1)
            blank(st, 6, 2)

        loop(MID // LANES, body)

    def mid_back_apply(dh, z, tot, grads, params, dest):
        def body(j):
            cols = aligned(j, LANES)
            f, a, bz = backward_terms(mid_at(tot, j), mid_at(grads, j), params, cols, OUT)
            for o in range(OD):
                d = f * dh[out_rows(o), cols] - a - z[out_rows(o), cols] * bz
                dest(o, cols, (d * R.pix_out[out_rows(o), :]).astype(BF))

        loop(MID // LANES, body)

    def reduce_back(dz, weight, dh):
        def body(i):
            acc = None
            for j in range(4):
                w = jnp.concatenate([piece(weight, 2 * i + q, j) for q in range(2)], axis=0)
                v = dot_t(dz[:, j * 512 : (j + 1) * 512], w)
                acc = v if acc is None else acc + v
            dh[:, aligned(i, MID // 2)] = acc

        loop(2, body)

    def tap_rows(weight, i, t):
        n = MID // 4
        return jnp.concatenate(
            [weight[pl.ds(pl.multiple_of(((2 * i + q) * 9 + t) * n, n), n), :] for q in range(2)], axis=0
        )

    reduce_back(R.dz6, R.f6, R.dh)
    mid_back_sums(R.dh, R.z5, R.t5, R.norm_mixing)
    mid_start(4)
    staged(WIDEN, fill_out(WIDEN, lambda: R.h5[...], R.dz6))
    mid_finish(4, R.g5)

    def to_d5(o, cols, v):
        R.d5[o + 1, :, cols] = v

    mid_back_apply(R.dh, R.z5, R.t5, R.g5, R.norm_mixing, to_d5)
    pair = edge_exchange(R.d5, 1)
    rs_step(WIDEN)
    unit_windows(R.d5, R.win5, range(1, OD + 1), True)
    edge_wait(pair)
    unit_windows(R.d5, R.win5, (0, OD + 1), True)

    def conv_back(j):
        acc = None
        for t in range(9):
            v = dot_t(R.win5[:, t * MID : (t + 1) * MID], tap_rows(R.f5, j, t))
            acc = v if acc is None else acc + v
        R.dh[:, aligned(j, MID // 2)] = acc

    loop(2, conv_back)
    mid_back_sums(R.dh, R.z4, R.t4, R.norm_squeeze)
    mid_start(5)
    rs_step(WIDEN)
    staged(MIXING, fill_conv(MIXING, R.win4, lambda: R.d5[1 : OD + 1].reshape(M, MID)))
    mid_finish(5, R.g4)

    def to_d4(o, cols, v):
        R.dz4[out_rows(o), cols] = v

    mid_back_apply(R.dh, R.z4, R.t4, R.g4, R.norm_squeeze, to_d4)

    def squeeze_back(j):
        n = WIDE // 4
        R.du1[:, :, aligned(j, n)] = dot_t(R.dz4[...], R.f4[aligned(j, n), :]).reshape(M // 16, 16, n)

    loop(4, squeeze_back)

    def u1_back(j):
        cols = aligned(j, LANES)
        u1 = u1_terms(j)
        tot = wide_at(R.t3, j)
        xa3, xs3 = xhat_terms(tot, OUT, 0)
        xas, xss = xhat_terms(tot, OUT, 8)
        ch = keep(j, float(WIDE // MID))
        g0 = jnp.zeros((S, LANES), F32)
        g1 = jnp.zeros((S, LANES), F32)
        g2 = jnp.zeros((S, LANES), F32)
        for o in range(OD):
            rows = out_rows(o)
            d = (R.du1[groups16(o), :, cols] + R.du2[groups16(o), :, cols]).reshape(S, LANES) * (ch * R.pix_out[rows, :]) * slope(u1(o))
            R.du1[groups16(o), :, cols] = d.reshape(S // 16, 16, LANES)
            g0 = g0 + d * (R.z3[rows, cols] * xa3 + xs3)
            g2 = g2 + d * (R.zs[rows, cols] * xas + xss)
            g1 = g1 + d
        st = wide_at(R.locw2, j)
        group_rows(st, 0, g0)
        group_rows(st, 3, g1)
        blank(st, 6, 2)
        group_rows(st, 8, g2)
        blank(st, 11, 5)

    loop(WIDE // LANES, u1_back)
    wide_start(3, R.locw2)

    def fill_squeeze(stage):
        def body(j):
            res = dot_w(R.y1[:, aligned(j, WIDE // 8)], R.dz4[...])
            n = res.shape[0] // 4
            bits = (lax.rem(j, 2), lax.rem(lax.div(j, 2), 2), lax.div(j, 4))
            for i in range(4):
                put(stage, SQUEEZE, i % 2, batch_bits(*bits, i // 2), 0, res[i * n : (i + 1) * n])

        loop(8, body)

    rs_step(MIXING, WIDEN)
    staged(SQUEEZE, fill_squeeze)
    wide_finish(3, R.g3)

    for o in range(OD):
        mixed_copy(1, o).wait_recv()
        mixed_copy(2, o).start()

    def u1_apply(j):
        cols = aligned(j, LANES)
        tot, grads = wide_at(R.t3, j), wide_at(R.g3, j)
        f3, a3, b3 = backward_terms(tot, grads, R.norm_expand, cols, OUT, 0, 0, 3)
        fs, as_, bs = backward_terms(tot, grads, R.norm_shortcut, cols, OUT, 8, 8, 3)
        for o in range(OD):
            rows = out_rows(o)
            d = R.du1[groups16(o), :, cols].reshape(S, LANES)
            pix = R.pix_out[rows, :]
            R.dz6[rows, cols] = ((f3 * d - a3 - R.z3[rows, cols] * b3) * pix).astype(BF)
            R.dzs[rows, cols] = ((fs * d - as_ - R.zs[rows, cols] * bs) * pix).astype(BF)

    loop(WIDE // LANES, u1_apply)
    reduce_back(R.dz6, R.f2, R.dh)
    mid_back_sums(R.dh, R.z2, R.t2, R.norm_spatial)
    mid_start(6)
    rs_step(SQUEEZE, MIXING, WIDEN)
    staged(EXPAND, fill_out(EXPAND, lambda: R.h2[...], R.dz6))

    def even_rows():
        return jnp.concatenate([R.x0[2 * o, 0:S, :] for o in range(OD)], axis=0)

    staged(SHORTCUT, fill_out(SHORTCUT, even_rows, R.dzs))
    mid_finish(6, R.g2)

    def to_d2(o, cols, v):
        R.d2[o, :, cols] = v

    mid_back_apply(R.dh, R.z2, R.t2, R.g2, R.norm_spatial, to_d2)
    up = remote(R.d2.at[0], R.d2.at[OD], R.hs.at[1], R.hr.at[1], (b, jnp.maximum(r - 1, 0)))

    @pl.when(r > 0)
    def _():
        up.start()

    @pl.when(r == 3)
    def _():
        R.d2[OD] = jnp.zeros(R.d2.shape[1:], BF)

    rs_step(EXPAND, SHORTCUT, WIDEN)
    staged(SPATIAL, fill_conv(SPATIAL, R.win1, lambda: R.d2[0:OD].reshape(M, MID)))

    @pl.when(r < 3)
    def _():
        up.wait_recv()

    @pl.when(r > 0)
    def _():
        up.wait_send()

    def dh1_at(k, j, width):
        return pl.ds(pl.multiple_of(k * MID + j * width, LANES), width)

    def d2_left(j):
        cols = aligned(j, LANES)
        for k in range(OD + 1):
            R.d2l[k, :, cols] = rolled(R.d2[k, :, cols].astype(F32), -1).astype(BF)

    loop(MID // LANES, d2_left)

    def spatial_back(j):
        here, left = R.d2[0:OD].reshape(M, MID), R.d2l[0:OD].reshape(M, MID)
        below, below_left = R.d2[1 : OD + 1].reshape(M, MID), R.d2l[1 : OD + 1].reshape(M, MID)

        def w(dr, dc):
            return tap_rows(R.f1, j, dr * 3 + dc)

        cols = aligned(j, MID // 2)
        parts = (
            ((here, 1, 1),),
            ((here, 1, 2), (left, 1, 0)),
            ((here, 2, 1), (below, 0, 1)),
            ((here, 2, 2), (left, 2, 0), (below, 0, 2), (below_left, 0, 0)),
        )
        for i, terms in enumerate(parts):
            rp, cp = divmod(i, 2)
            acc = None
            for v, dr, dc in terms:
                y = dot_t(v, w(dr, dc))
                acc = y if acc is None else acc + y
            for o in range(OD):
                R.zs[out_rows(cp), dh1_at(2 * o + rp, j, MID // 2)] = acc[out_rows(o)]

    loop(2, spatial_back)

    def h1_back(j):
        cols = aligned(j, LANES)
        sums = mid_at(R.t1, j)
        sc, sh = forward_terms(sums, R.norm_reduce, cols, IN)
        xa, xs = xhat_terms(sums, IN)
        ch = keep(j, 1.0)
        g0 = jnp.zeros((S, LANES), F32)
        g1 = jnp.zeros((S, LANES), F32)
        for k in range(RD):
            for p in range(2):
                rows = out_rows(p)
                v = R.z1[k, rows, cols]
                d = R.zs[rows, dh1_at(k, j, LANES)] * (ch * R.pix_in[k, rows, :]) * slope(v * sc + sh)
                R.zs[rows, dh1_at(k, j, LANES)] = d
                g0 = g0 + d * (v * xa + xs)
                g1 = g1 + d
        st = mid_at(R.loc, j)
        group_rows(st, 0, g0)
        group_rows(st, 3, g1)
        blank(st, 6, 2)

    loop(MID // LANES, h1_back)
    mid_start(7)
    rs_step(SPATIAL, SQUEEZE, MIXING, EXPAND, SHORTCUT)

    def short_back(j):
        acc = None
        for i in range(4):
            v = dot_t(R.dzs[:, i * 512 : (i + 1) * 512], piece(R.f3, j, i))
            acc = v if acc is None else acc + v
        R.z6[:, aligned(j, CIN // 4)] = acc

    loop(4, short_back)
    mid_finish(7, R.g1)

    def h1_apply(j):
        cols = aligned(j, LANES)
        f, a, bz = backward_terms(mid_at(R.t1, j), mid_at(R.g1, j), R.norm_reduce, cols, IN)
        for k in range(RD):
            for p in range(2):
                rows = out_rows(p)
                d = f * R.zs[rows, dh1_at(k, j, LANES)] - a - R.z1[k, rows, cols] * bz
                R.y1[rows, dh1_at(k, j, LANES)] = (d * R.pix_in[k, rows, :]).astype(BF)

    loop(MID // LANES, h1_apply)

    def dz1(k):
        return R.y1[:, k * MID : (k + 1) * MID]

    def fill_reduce(stage):
        n = CIN // 32

        def body(j):
            act = R.x0[:, :, aligned(j, 256)].reshape(RD * 2 * S, 256)
            res = dot_w(act, jnp.concatenate([dz1(k) for k in range(RD)], axis=0))
            for i in range(8):
                bits = batch_bits(i // 4, lax.rem(j, 2), lax.div(j, 2), i // 2 % 2)
                put(stage, REDUCE, i % 2, bits, 0, res[i * n : (i + 1) * n])

        loop(4, body)

    rs_step(SPATIAL, SQUEEZE, MIXING, EXPAND, SHORTCUT)
    staged(REDUCE, fill_reduce)
    rs_step(SPATIAL, SQUEEZE, MIXING, EXPAND, SHORTCUT)

    def input_grad(j):
        cols = aligned(j, CIN // 4)
        w = R.f0[aligned(j, CIN // 4), :]
        ch = jnp.concatenate(
            [keep(j * (CIN // 4 // LANES) + i, float(CIN // MID)) for i in range(CIN // 4 // LANES)],
            axis=1,
        )
        for k in range(RD):
            y = dot_t(dz1(k), w)
            for c in range(0, CIN // 4, LANES):
                base = c // LANES * 2 * S
                for p in range(2):
                    v = y[out_rows(p), c : c + LANES]
                    if p == 0 and k % 2 == 0:
                        v = v + R.z6[out_rows(k // 2), pl.ds(pl.multiple_of(j * (CIN // 4) + c, LANES), LANES)]
                    v = v * (ch[:, c : c + LANES] * R.pix_in[k, out_rows(p), :])
                    R.weave[pl.ds(base + p, S, stride=2), :] = v
                at = pl.ds(pl.multiple_of(k % 2 * CIN + j * (CIN // 4) + c, LANES), LANES)
                woven = R.weave[base : base + 2 * S, :]
                (R.du2, R.du1)[k // 2][:, :, at] = woven.reshape(M // 16, 16, LANES)

    loop(4, input_grad)
    gin_copies = [
        pltpu.make_async_copy(
            (R.du2, R.du1)[k // 2].at[pl.ds(0, images), :, pl.ds(k % 2 * CIN, CIN)], R.gin.at[:, k], R.gn.at[k]
        )
        for k in range(RD)
    ]
    for c in gin_copies:
        c.start()
    rs_end()

    for out, src in ((R.gn1, R.g1), (R.gn2, R.g2), (R.gn4, R.g4), (R.gn5, R.g5)):
        for h in range(2):
            for i in range(2):
                out[i, :, h * (MID // 2) : (h + 1) * (MID // 2)] = src[h, 3 * i : 3 * i + 3, :]
    for out, src, rows in ((R.gn3, R.g3, (0, 3)), (R.gns, R.g3, (8, 3)), (R.gn6, R.g6, (0, 3))):
        for h in range(4):
            for i in range(2):
                out[i, :, h * (WIDE // 4) : (h + 1) * (WIDE // 4)] = src[h, rows[i] : rows[i] + 3, :]

    for o in range(OD):
        mixed_copy(0, o).wait()
        mixed_copy(1, o).wait_send()
        mixed_copy(2, o).wait()
        mixed_copy(3, o).wait()
    for c in gin_copies:
        c.wait()


def plan(features, w_reduce, w_expand, batch):
    images, rd, _, cin = features.shape
    mid, wide = w_reduce.shape[1], w_expand.shape[1]
    cfg = SimpleNamespace(
        images=images,
        members=images * batch // 3,
        slots=-(-images * 8 // 16) * 16, in_rows=rd, out_rows=rd // 2, batch=batch, mid=mid, wide=wide, cin=cin
    )
    flat = {
        REDUCE: cin,
        SPATIAL: 9 * mid,
        EXPAND: mid * wide // 512,
        SHORTCUT: cin * wide // 512,
        SQUEEZE: wide,
        MIXING: 9 * mid,
        WIDEN: mid * wide // 512,
    }
    pieces = {SPATIAL: 3, MIXING: 3, SHORTCUT: 2}
    cfg.units = []
    for name, n in flat.items():
        k = pieces.get(name, 1)
        cfg.units += [(name, i * n // 4 // k, n // 4 // k) for i in range(k)]
    cfg.flat = flat
    cfg.rows = {name: n // 32 for name, n in flat.items()}
    cfg.reduce = batch == 8
    orders = ((DX, DY, DN, DF), (DY, DX, DN, DF), (DN, DF, DX, DY))
    thirds = {WIDEN: 1, SQUEEZE: 0, EXPAND: 2}
    cfg.parts = {}
    for name, n in cfg.rows.items():
        if not cfg.reduce:
            cfg.parts[name] = [(0, n, (DF, DN, DY, DX))]
            continue
        tiles = [n // 16 // 3] * 3
        for i in range(n // 16 - sum(tiles)):
            tiles[(thirds.get(name, 0) + i) % 3] += 1
        cfg.parts[name], n0 = [], 0
        for tile, order in zip(tiles, orders):
            if tile:
                cfg.parts[name].append((n0, 16 * tile, order))
                n0 += 16 * tile
    cfg.own_landing = (REDUCE, SPATIAL, SHORTCUT)
    cfg.offs, total = {}, 0
    for name, n in cfg.rows.items():
        cfg.offs[name] = total
        total += n
    cfg.total = total
    return cfg


def run_blocks(cfg, smem_args, vmem_args, hbm_args):
    S, RD, OD, NB = cfg.slots, cfg.in_rows, cfg.out_rows, cfg.batch
    MID, WIDE, CIN = cfg.mid, cfg.wide, cfg.cin
    M = OD * S
    U = len(cfg.units)
    vmem = pl.BlockSpec(memory_space=pltpu.VMEM)
    hbm = pl.BlockSpec(memory_space=pl.ANY)
    sds = jax.ShapeDtypeStruct
    outs = dict(
        mixed=(sds((cfg.images, 4 * OD, 8, WIDE), BF), hbm),
        gin=(sds((cfg.images, RD, 16, CIN), F32), hbm),
        gn1=(sds((2, 3, MID), F32), vmem),
        gn2=(sds((2, 3, MID), F32), vmem),
        gn3=(sds((2, 3, WIDE), F32), vmem),
        gns=(sds((2, 3, WIDE), F32), vmem),
        gn4=(sds((2, 3, MID), F32), vmem),
        gn5=(sds((2, 3, MID), F32), vmem),
        gn6=(sds((2, 3, WIDE), F32), vmem),
    )
    final = {}
    if cfg.reduce:
        for w, n in cfg.rows.items():
            final[w] = (9, n // 9, 512) if w in (SPATIAL, MIXING) else (n, 512)
            shape = (n, 2048) if w in (EXPAND, SHORTCUT, WIDEN) else final[w][:-2] + (4 * final[w][-2], 512)
            outs["o" + str(w)] = (sds(shape, BF), hbm)
    else:
        outs.update(grads=(sds((32 * cfg.total, 512), BF), hbm))
    V = pltpu.VMEM
    mid_tot = V((2, 8, MID // 2), F32)
    scratch = dict(
        z1=V((RD, 2 * S, MID), F32),
        win1=V((M, 9 * MID), BF),
        h1s=V((2, S, MID), BF),
        h1r=V((2, S, MID), BF),
        z2=V((M, MID), F32),
        h2=V((M, MID), BF),
        z3=V((M, WIDE), F32),
        zs=V((M, WIDE), F32),
        y1=V((M, WIDE), BF),
        z4=V((M, MID), F32),
        h4=V((OD + 2, S, MID), BF),
        win4=V((M, 9 * MID), BF),
        z5=V((M, MID), F32),
        h5=V((M, MID), BF),
        z6=V((M, WIDE), F32),
        mixed_local=V((OD, S // 8, 8, WIDE), BF),
        du2=V((M // 16, 16, WIDE), F32),
        dz6=V((M, WIDE), BF),
        dh=V((M, MID), F32),
        d5=V((OD + 2, S, MID), BF),
        win5=V((M, 9 * MID), BF),
        dz4=V((M, MID), BF),
        du1=V((M // 16, 16, WIDE), F32),
        dzs=V((M, WIDE), BF),
        d2=V((OD + 1, S, MID), BF),
        d2l=V((OD + 1, S, MID), BF),
        stage0=V((32 * cfg.rows[MIXING], 512), BF),
        stage1=V((32 * cfg.rows[SHORTCUT], 512), BF),
        loc=mid_tot,
        locw=V((4, 8, WIDE // 4), F32),
        locw2=V((4, 16, WIDE // 4), F32),
        t1=mid_tot,
        t2=mid_tot,
        t3=V((4, 16, WIDE // 4), F32),
        t4=mid_tot,
        t5=mid_tot,
        t6=V((4, 8, WIDE // 4), F32),
        g1=mid_tot,
        g2=mid_tot,
        g3=V((4, 16, WIDE // 4), F32),
        g4=mid_tot,
        g5=mid_tot,
        g6=V((4, 8, WIDE // 4), F32),
        rc=V((2, 8, MID // 2), F32),
        rq=V((2, 2 * NB, 8, MID // 2), F32),
        rw=V((2, 4, 16, WIDE // 4), F32),
        wb=V((2, NB, 16, WIDE // 4), F32),
        wsend=pltpu.SemaphoreType.DMA((U, 5)),
        wrecv=pltpu.SemaphoreType.DMA((U, 5)),
        wloc=pltpu.SemaphoreType.DMA((7, 4)),
        ms=pltpu.SemaphoreType.DMA((3,)),
        mr=pltpu.SemaphoreType.DMA((3, 2)),
        ws=pltpu.SemaphoreType.DMA((4, 3)),
        wr=pltpu.SemaphoreType.DMA((4, 3)),
        hs=pltpu.SemaphoreType.DMA((2,)),
        hr=pltpu.SemaphoreType.DMA((2,)),
        es=pltpu.SemaphoreType.DMA((2, 2)),
        er=pltpu.SemaphoreType.DMA((2, 2)),
        xs=pltpu.SemaphoreType.DMA((3, OD)),
        xr=pltpu.SemaphoreType.DMA((3, OD)),
        xl=pltpu.SemaphoreType.DMA((OD,)),
        gs=pltpu.SemaphoreType.DMA((2,)),
        gn=pltpu.SemaphoreType.DMA((RD,)),
        rs=pltpu.SemaphoreType.DMA((7, 3, 5)),
        rr=pltpu.SemaphoreType.DMA((7, 3, 5)),
        fs=pltpu.SemaphoreType.DMA((7, 3)),
        fr=pltpu.SemaphoreType.DMA((7, 3)),
        fl=pltpu.SemaphoreType.DMA((7,)),
        x0=V((RD, 2 * S, CIN), BF),
        weave=V((4 * S, LANES), F32),
        ct=V((M, WIDE), BF),
        onehot=V((3, S, LANES), F32),
        active_slot=V((S, LANES), F32),
        pix_in=V((RD, 2 * S, LANES), F32),
        pix_out=V((M, LANES), F32),
        ld=pltpu.SemaphoreType.DMA((2,)),
    )
    scratch.update({"f" + str(name): V((n, 512), BF) for name, n in cfg.flat.items()})
    scratch.update({"l" + str(name): V((cfg.flat[name], 512), BF) for name in cfg.own_landing if cfg.reduce})
    scratch.update({"e" + str(w): V(shape, BF) for w, shape in final.items()})
    names = list(smem_args) + list(vmem_args) + list(hbm_args) + list(outs) + list(scratch)
    smem = pl.BlockSpec(memory_space=pltpu.SMEM)
    res = pl.pallas_call(
        functools.partial(block_kernel, names, cfg),
        out_shape=[o[0] for o in outs.values()],
        in_specs=[smem] * len(smem_args) + [vmem] * len(vmem_args) + [hbm] * len(hbm_args),
        out_specs=[o[1] for o in outs.values()],
        scratch_shapes=list(scratch.values()),
        compiler_params=pltpu.CompilerParams(
            collective_id=0, has_side_effects=True, vmem_limit_bytes=63 * 2**20
        ),
    )(*smem_args.values(), *vmem_args.values(), *hbm_args.values())
    return SimpleNamespace(**dict(zip(outs, res)))


def slot_layout(x, slots):
    images, rows, cols, channels = x.shape
    x = jnp.transpose(x, (1, 0, 2, 3)).reshape(rows, images * cols, channels)
    return jnp.pad(x, ((0, 0), (0, slots - images * cols), (0, 0)))


def per_device(
    features, w_reduce, w_spatial, w_expand, w_shortcut, w_squeeze, w_mixing, w_widen,
    norm_reduce, norm_spatial, norm_expand, norm_shortcut, norm_squeeze, norm_mixing, norm_widen,
    cotangent, resolution, active,
):
    images, rd, cols_in, cin = features.shape
    od = rd // 2
    nb = lax.axis_size("batch")
    cfg = plan(features, w_reduce, w_expand, nb)
    S, mid, wide = cfg.slots, cfg.mid, cfg.wide
    x = jnp.pad(features, ((0, 0), (0, 0), (0, 16 - cols_in), (0, 0)))
    x = x.reshape(images, rd, 8, 2, cin)
    x = jnp.transpose(x, (1, 3, 0, 2, 4)).reshape(rd, 2, images * 8, cin)
    x = jnp.pad(x, ((0, 0), (0, 0), (0, S - images * 8), (0, 0))).reshape(rd, 2 * S, cin)
    out_cols = cotangent.shape[2]
    ct = slot_layout(jnp.pad(cotangent, ((0, 0), (0, 0), (0, 8 - out_cols), (0, 0))), S)
    res = run_blocks(
        cfg,
        dict(resolution=resolution, active=active),
        dict(
            norm_reduce=norm_reduce,
            norm_spatial=norm_spatial,
            norm_expand=norm_expand,
            norm_shortcut=norm_shortcut,
            norm_squeeze=norm_squeeze,
            norm_mixing=norm_mixing,
            norm_widen=norm_widen,
        ),
        dict(
            features=x,
            cotangent=ct.reshape(od * S, wide),
            w0=w_reduce,
            w1=w_spatial.reshape(-1, mid),
            w2=w_expand,
            w3=w_shortcut,
            w4=w_squeeze,
            w5=w_mixing.reshape(-1, mid),
            w6=w_widen,
        ),
    )
    mixed = res.mixed[:, :, :out_cols]
    gin = res.gin[:, :, :cols_in]

    def unpack(g, name):
        b8, _, n, _ = g.shape
        if name in (SPATIAL, MIXING):
            k = n // 9
            return jnp.transpose(g.reshape(b8, 4, 9, k, 512), (2, 0, 1, 3, 4)).reshape(3, 3, b8 * 4 * k, 512)
        if name in (EXPAND, SHORTCUT, WIDEN):
            return jnp.transpose(g, (0, 2, 1, 3)).reshape(b8 * n, 2048)
        return g.reshape(b8 * 4 * n, 512)

    totals = []
    for name, n in cfg.rows.items():
        if cfg.reduce:
            g = getattr(res, "o" + str(name)).astype(F32)
            totals.append(g.reshape((3, 3) + g.shape[1:]) if g.ndim == 3 else g)
            continue
        at = cfg.offs[name]
        part = res.grads[32 * at : 32 * (at + n)].reshape(2, 8, 2, n, 512)
        part = unpack(jnp.transpose(part, (1, 2, 0, 3, 4)).reshape(8, 4, n, 512), name)
        dim = 2 if part.ndim == 4 else 0
        part = lax.psum_scatter(part, "batch", scatter_dimension=dim, tiled=True)
        totals.append(lax.psum(part, "rows").astype(F32))

    return (mixed, gin, *totals, res.gn1, res.gn2, res.gn3, res.gns, res.gn4, res.gn5, res.gn6)


def solution(mesh):
    w2, w4 = P("rows", None), P(None, None, "rows", None)
    o2, o4 = P("batch", None), P(None, None, "batch", None)
    return jax.shard_map(
        per_device,
        mesh=mesh,
        in_specs=(P("batch", "rows", None, None), w2, w4, w2, w2, w2, w4, w2)
        + (P(),) * 7
        + (P("batch", "rows", None, None), P(), P()),
        out_specs=(P("batch", None, None, None), P("batch", "rows", None, None), o2, o4, o2, o2, o2, o4, o2)
        + (P(),) * 7,
        check_vma=False,
    )
```

```python
import functools
from types import SimpleNamespace

import jax
import jax.numpy as jnp
from jax import lax
from jax.experimental import pallas as pl
from jax.experimental.pallas import tpu as pltpu
from jax.sharding import PartitionSpec as P

eps = 1e-05
MESH = pl.DeviceIdType.MESH
BF = jnp.bfloat16
F32 = jnp.float32
LANES = 128
REDUCE, SPATIAL, EXPAND, SHORTCUT, SQUEEZE, MIXING, WIDEN = range(7)
DX, DY, DN, DF = range(4)


def dot(a, b):
    return jnp.dot(a, b, preferred_element_type=F32)


def dot_t(a, b):
    return lax.dot_general(a, b, (((1,), (1,)), ((), ())), preferred_element_type=F32)


def dot_w(a, b):
    return lax.dot_general(a, b, (((0,), (0,)), ((), ())), preferred_element_type=F32)


def aligned(index, size):
    return pl.ds(pl.multiple_of(index * size, size), size)


def loop(count, body):
    def step(i, carry):
        body(i)
        return carry

    lax.fori_loop(0, count, step, 0)


def each(count, body):
    if count > 16:
        loop(count, body)
        return
    for i in range(count):
        body(i)


def silu_parts(u):
    s = jax.nn.sigmoid(u)
    return s, u * s


def slope(u):
    s = jax.nn.sigmoid(u)
    return s * (1.0 + u * (1.0 - s))


def block_kernel(names, cfg, *refs):
    R = SimpleNamespace(**dict(zip(names, refs)))
    S, RD, OD, NB = cfg.slots, cfg.in_rows, cfg.out_rows, cfg.batch
    MID, WIDE, CIN = cfg.mid, cfg.wide, cfg.cin
    M = OD * S
    b = lax.axis_index("batch")
    r = lax.axis_index("rows")
    core = lax.rem(r, 2)
    xb = lax.div(r, 2)
    core_peer = r + 1 - 2 * core
    x_row = lax.rem(r + 2, 4)
    diag = 3 - r
    half = lax.rem(b, 2)

    def flip(i, j):
        if isinstance(j, int):
            out = i
            for bit in range((2 * NB - 1).bit_length()):
                if j >> bit & 1:
                    out = out + (1 << bit) * (1 - 2 * lax.rem(lax.div(i, 1 << bit), 2))
            return out
        out = jnp.int32(0)
        bit = 1
        while bit < 2 * NB:
            p, q = lax.rem(lax.div(i, bit), 2), lax.rem(lax.div(j, bit), 2)
            out = out + bit * (p + q - 2 * p * q)
            bit *= 2
        return out

    me = b * 2 + xb

    def remote(src, dst, send, recv, dev):
        return pltpu.make_async_remote_copy(
            src_ref=src, dst_ref=dst, send_sem=send, recv_sem=recv, device_id=dev, device_id_type=MESH
        )

    def team(id2):
        return (lax.div(id2, 2), 2 * lax.rem(id2, 2) + core)

    units = cfg.units
    wsend, wrecv, wloc = R.wsend, R.wrecv, R.wloc
    near = lax.rem(lax.div(b, 2), 2)
    sides = ((half, (b + 1 - 2 * half, r)), (near, (b + 2 - 4 * near, r)))

    def wview(u, shard, at, fourths):
        w, k0, kn, _ = units[u]
        full = getattr(R, "f" + str(w))
        start = shard * (full.shape[0] // 4) + k0 + at * (kn // 4)
        return full.at[pl.ds(pl.multiple_of(start, 16), fourths * kn // 4)]

    def w_copy(u, i):
        mode = units[u][3]
        first, second = sides if mode == 1 else sides[::-1]
        quarter = x_row if i > 1 else r
        at, fourths, dev = 0, 4, (b, core_peer)
        if i == 1:
            dev = (b, x_row)
        if mode and i > 0:
            fourths = 2 if i > 4 else 1
            at = 2 * second[0] + first[0]
            if i == 3:
                dev = first[1]
            elif i == 4:
                at = at + 1 - 2 * first[0]
            elif i == 5:
                at, dev = 2 * second[0], second[1]
            elif i == 6:
                at = 2 - 2 * second[0]
        view = wview(u, quarter, at, fourths)
        return remote(view, view, wsend.at[u, i], wrecv.at[u, i], dev)

    def w_stages(u):
        return range(7) if units[u][3] else range(3)

    def w_local(w):
        src, full = getattr(R, "w" + str(w)), getattr(R, "f" + str(w))
        n, quarter = src.shape[0], full.shape[0] // 4
        return [
            pltpu.make_async_copy(
                src.at[:, pl.ds(512 * i, 512)],
                full.at[pl.ds(pl.multiple_of(r * quarter + i * n, 16), n)],
                wloc.at[w, i],
            )
            for i in range(src.shape[1] // 512)
        ]

    bar = pltpu.get_barrier_semaphore()
    for dev in ((b, core_peer), (b, diag)):
        pl.semaphore_signal(bar, inc=1, device_id=dev, device_id_type=MESH)

    def greet(j):
        pl.semaphore_signal(bar, inc=1, device_id=team(flip(me, j + 1)), device_id_type=MESH)

    loop(2 * NB - 1, greet)

    loaded = [w_local(w) for w in range(7)]
    for w in range(7):
        for c in loaded[w]:
            c.start()
        if w == 0:
            x0_load = pltpu.make_async_copy(R.features, R.x0, R.ld.at[0])
            x0_load.start()
    norm_load = pltpu.make_async_copy(R.norms, R.norm_values, R.ld.at[2])
    norm_load.start()
    ct_load = pltpu.make_async_copy(R.cotangent, R.ct, R.ld.at[1])
    ct_load.start()
    norm_reduce, norm_spatial, norm_squeeze, norm_mixing, norm_expand, norm_shortcut, norm_widen = [
        R.norm_values.at[:, :, pl.ds(at, width)] for at, width in cfg.norm_columns
    ]
    at_home = set()

    images = cfg.images
    column = lax.broadcasted_iota(jnp.int32, (8, LANES), 0).astype(F32)
    if 8 * images < S:
        tail = slice(8 * images, S)
        none = jnp.zeros((S - 8 * images, LANES), F32)
        R.active_slot[tail, :] = none
        for g in range(3):
            R.onehot[g, tail, :] = none
        for o in range(OD):
            R.pix_out[o * S + 8 * images : (o + 1) * S, :] = none
        for k in range(RD):
            for p in range(2):
                R.pix_in[k, p * S + 8 * images : (p + 1) * S, :] = none

    for i in range(images):
        group = R.resolution[b * images + i]
        side = (5 + group).astype(F32)
        here = slice(8 * i, 8 * i + 8)
        limit = jnp.zeros((8, LANES), F32)
        for g in range(3):
            is_g = jnp.where(group == g, 1.0, 0.0)
            R.onehot[g, here, :] = jnp.full((8, LANES), is_g, F32)
            limit = limit + is_g * R.active[g].astype(F32)
        R.active_slot[here, :] = limit
        for o in range(OD):
            inside = jnp.where((r * OD + o).astype(F32) < side, side, 0.0)
            R.pix_out[o * S + 8 * i : o * S + 8 * i + 8, :] = jnp.where(column < inside, 1.0, 0.0)
        for k in range(RD):
            inside = jnp.where((r * RD + k).astype(F32) < 2.0 * side, 2.0 * side, 0.0)
            for p in range(2):
                R.pix_in[k, p * S + 8 * i : p * S + 8 * i + 8, :] = jnp.where(2.0 * column + p < inside, 1.0, 0.0)

    pl.semaphore_wait(bar, 2 * NB + 1)

    def w_start(u):
        w = units[u][0]
        if w not in at_home:
            at_home.add(w)
            for c in loaded[w]:
                c.wait()
        w_copy(u, 1).start()
        w_copy(u, 0).start()

    def w_second(u):
        w_copy(u, 1).wait_recv()
        if units[u][3]:
            w_copy(u, 3).start()
        w_copy(u, 2).start()

    def w_third(u):
        if units[u][3]:
            w_copy(u, 3).wait_recv()
            w_copy(u, 5).start()
            w_copy(u, 4).start()

    def w_fourth(u):
        if units[u][3]:
            w_copy(u, 5).wait_recv()
            w_copy(u, 6).start()

    def w_ready(u):
        for i in w_stages(u)[::2]:
            w_copy(u, i).wait_recv()

    pumped = [0]
    lags = cfg.lags

    def pump(steps):
        for _ in range(steps):
            n = pumped[0]
            for lag, stage in zip(lags, (w_start, w_second, w_third, w_fourth)):
                if 0 <= n - lag < len(units):
                    stage(n - lag)
            pumped[0] = n + 1

    def need(name):
        last = max(u for u in range(len(units)) if units[u][0] == name)
        while pumped[0] < last + lags[3 if units[last][3] else 1] + 1:
            pump(1)
        for u in range(len(units)):
            if units[u][0] == name:
                w_ready(u)

    def mid_start(k):
        p = k % 2
        swap = remote(R.loc.at[1 - core], R.rc.at[p], R.ms.at[0], R.mr.at[0, p], (b, core_peer))
        swap.start()
        swap.wait_recv()
        R.rq[p, me] = R.loc[core] + R.rc[p]

        def send(j):
            to = team(flip(me, j + 1))
            remote(R.rq.at[p, me, pl.ds(0, 6)], R.rq.at[p, me, pl.ds(0, 6)], R.ms.at[1], R.mr.at[1, p], to).start()

        each(2 * NB - 1, send)
        swap.wait_send()

    def mid_finish(k, tot):
        p = k % 2
        rest = R.rq.at[p, pl.ds(0, 2 * NB - 1), pl.ds(0, 6)]
        every = remote(rest, rest, R.ms.at[1], R.mr.at[1, p], (b, x_row))
        every.wait_recv()
        total = R.rq[p, 0]
        for j in range(1, 2 * NB):
            total = total + R.rq[p, j]
        tot[core] = total
        back = remote(tot.at[core], tot.at[core], R.ms.at[2], R.mr.at[2, p], (b, core_peer))
        back.start()
        every.wait_send()
        back.wait()

    def wide_start(k, loc):
        n = loc.shape[1]
        rw, wb = R.rw.at[k % 2, :, pl.ds(0, n)], R.wb.at[k % 2, :, pl.ds(0, n)]
        rw[r] = loc[r]
        for to in (core_peer, x_row, diag):
            remote(loc.at[to], rw.at[r], R.ws.at[k, 0], R.wr.at[k, 0], (b, to)).start()
        three = remote(loc.at[pl.ds(0, 3)], rw.at[pl.ds(0, 3)], R.ws.at[k, 0], R.wr.at[k, 0], (b, core_peer))
        three.wait_recv()
        wb[b] = rw[0] + rw[1] + (rw[2] + rw[3])

        def send(j):
            to = lax.rem(b + j + 1, NB)
            remote(wb.at[b], wb.at[b], R.ws.at[k, 1], R.wr.at[k, 1], (to, r)).start()

        each(NB - 1, send)
        three.wait_send()

    def wide_finish(k, tot):
        n = tot.shape[1]
        wb = R.wb.at[k % 2, :, pl.ds(0, n)]
        rest = wb.at[pl.ds(0, NB - 1)]
        every = remote(rest, rest, R.ws.at[k, 1], R.wr.at[k, 1], (b, x_row))
        every.wait_recv()
        total = wb[0]
        for j in range(1, NB):
            total = total + wb[j]
        tot[r] = total
        for to in (core_peer, x_row, diag):
            remote(tot.at[r], tot.at[r], R.ws.at[k, 2], R.wr.at[k, 2], (b, to)).start()
        three = remote(tot.at[pl.ds(0, 3)], tot.at[pl.ds(0, 3)], R.ws.at[k, 2], R.wr.at[k, 2], (b, core_peer))
        every.wait_send()
        three.wait()

    def mid_at(ref, j):
        return ref.at[lax.div(j, 2), :, aligned(lax.rem(j, 2), LANES)]

    def wide_at(ref, j):
        return ref.at[lax.div(j, 4), :, aligned(lax.rem(j, 4), LANES)]

    def group_rows(ref, row, values):
        for g in range(3):
            ref[row + g : row + g + 1, :] = jnp.sum(values * R.onehot[g], axis=0, keepdims=True)

    def blank(ref, row, rows):
        ref[row : row + rows, :] = jnp.zeros((rows, LANES), F32)

    def spread(rows3):
        return rows3[0] * R.onehot[0] + rows3[1] * R.onehot[1] + rows3[2] * R.onehot[2]

    def moments(sums, inv_n, row=0):
        means, invs = [], []
        for g in range(3):
            n = 1.0 / inv_n[g]
            mean = sums[row + g : row + g + 1, :] * n
            var = sums[row + 3 + g : row + 4 + g, :] * n - mean * mean
            means.append(mean)
            invs.append(lax.rsqrt(var + eps))
        return means, invs

    OUT = [cfg.members * (5.0 + g) * (5.0 + g) for g in range(3)]
    IN = [cfg.members * (10.0 + 2.0 * g) * (10.0 + 2.0 * g) for g in range(3)]

    def forward_terms(sums, params, cols, inv_n, row=0):
        means, invs = moments(sums, inv_n, row)
        scales = [invs[g] * params[g, 0:1, cols] for g in range(3)]
        shifts = [params[g, 1:2, cols] - means[g] * scales[g] for g in range(3)]
        return spread(scales), spread(shifts)

    def xhat_terms(sums, inv_n, row=0):
        means, invs = moments(sums, inv_n, row)
        return spread(invs), spread([-means[g] * invs[g] for g in range(3)])

    def backward_terms(sums, grads, params, cols, inv_n, row=0, g0=0, g1=3):
        means, invs = moments(sums, inv_n, row)
        fs, az, bz = [], [], []
        for g in range(3):
            n = 1.0 / inv_n[g]
            f = invs[g] * params[g, 0:1, cols]
            gain = grads[g0 + g : g0 + g + 1, :] * n * invs[g]
            bias = grads[g1 + g : g1 + g + 1, :] * n
            fs.append(f)
            bz.append(f * gain)
            az.append(f * (bias - means[g] * gain))
        return spread(fs), spread(az), spread(bz)

    def keep(j, ratio):
        lane = lax.broadcasted_iota(jnp.int32, (S, LANES), 1).astype(F32) + j * float(LANES)
        return jnp.where(lane < R.active_slot[...] * ratio, 1.0, 0.0)

    def out_rows(k):
        return slice(k * S, (k + 1) * S)

    def groups16(o):
        return slice(o * (S // 16), (o + 1) * (S // 16))

    def forward_stats(z, loc_at, row=0):
        def body(j):
            cols = aligned(j, LANES)
            s = jnp.zeros((S, LANES), F32)
            q = jnp.zeros((S, LANES), F32)
            for o in range(OD):
                v = z[out_rows(o), cols]
                m = v * R.pix_out[out_rows(o), :]
                s = s + m
                q = q + m * v
            st = loc_at(j)
            group_rows(st, row, s)
            group_rows(st, row + 3, q)
            blank(st, row + 6, 2)

        loop(z.shape[-1] // LANES, body)

    def rolled(v, by):
        return pltpu.roll(v, by % S, 0)

    def by_shard(t, j):
        return pl.ds(pl.multiple_of(j * (9 * LANES) + t * LANES, LANES), LANES)

    def by_tap(t, j):
        return pl.ds(pl.multiple_of(t * MID + j * LANES, LANES), LANES)

    def unit_windows(halo, win, rows, flipped):
        place = by_tap if flipped else by_shard

        def body(j):
            cols = aligned(j, LANES)
            for k in rows:
                v = halo[k, :, cols].astype(F32)
                moved = (rolled(v, 1).astype(BF), v.astype(BF), rolled(v, -1).astype(BF))
                for dr in range(3):
                    o = k - dr
                    if not 0 <= o < OD:
                        continue
                    for dc in range(3):
                        t = (2 - dr) * 3 + 2 - dc if flipped else dr * 3 + dc
                        win[out_rows(o), place(t, j)] = moved[dc]

        loop(MID // LANES, body)

    def edge_exchange(halo, k):
        up = remote(halo.at[1], halo.at[OD + 1], R.es.at[k, 0], R.er.at[k, 0], (b, jnp.maximum(r - 1, 0)))
        down = remote(halo.at[OD], halo.at[0], R.es.at[k, 1], R.er.at[k, 1], (b, jnp.minimum(r + 1, 3)))

        @pl.when(r > 0)
        def _():
            up.start()

        @pl.when(r < 3)
        def _():
            down.start()

        @pl.when(r == 0)
        def _():
            halo[0] = jnp.zeros(halo.shape[1:], BF)

        @pl.when(r == 3)
        def _():
            halo[OD + 1] = jnp.zeros(halo.shape[1:], BF)

        return up, down

    def edge_wait(pair):
        up, down = pair

        @pl.when(r < 3)
        def _():
            up.wait_recv()
            down.wait_send()

        @pl.when(r > 0)
        def _():
            down.wait_recv()
            up.wait_send()

    x0_load.wait()
    norm_load.wait()
    need(REDUCE)

    def z1_rows(k):
        def mask(j):
            cols = aligned(j, LANES)
            ch = keep(j, float(CIN // MID))
            for p in range(2):
                m = (ch * R.pix_in[k, out_rows(p), :]).astype(BF)
                R.x0[k, out_rows(p), cols] = R.x0[k, out_rows(p), cols] * m

        loop(CIN // LANES, mask)
        R.z1[k] = dot(R.x0[k], R.f0[...])

    loop(RD, z1_rows)

    def z1_stats(j):
        cols = aligned(j, LANES)
        s = jnp.zeros((S, LANES), F32)
        q = jnp.zeros((S, LANES), F32)
        for k in range(RD):
            for p in range(2):
                v = R.z1[k, out_rows(p), cols]
                m = v * R.pix_in[k, out_rows(p), :]
                s = s + m
                q = q + m * v
        st = mid_at(R.loc, j)
        group_rows(st, 0, s)
        group_rows(st, 3, q)
        blank(st, 6, 2)

    loop(MID // LANES, z1_stats)
    mid_start(0)
    pump(cfg.pumps[0])
    mid_finish(0, R.t1)

    last = RD - 1

    def h1_body(j):
        cols = aligned(j, LANES)
        sc, sh = forward_terms(mid_at(R.t1, j), norm_reduce, cols, IN)
        ch = keep(j, 1.0)
        for k in range(RD - 1, -1, -1):
            for p in range(2):
                u = R.z1[k, out_rows(p), cols] * sc + sh
                h = silu_parts(u)[1] * (ch * R.pix_in[k, out_rows(p), :])
                if k == last:
                    R.h1s[p, :, cols] = h.astype(BF)
                for dr in range(3):
                    o2 = k + 1 - dr
                    if o2 % 2 or not 0 <= o2 // 2 < OD:
                        continue
                    o = o2 // 2
                    taps = ((1, h),) if p == 0 else ((0, rolled(h, 1)), (2, h))
                    for dc, v in taps:
                        t = dr * 3 + dc
                        R.win1[out_rows(o), by_shard(t, j)] = v.astype(BF)

    loop(MID // LANES, h1_body)
    down = remote(R.h1s, R.h1r, R.hs.at[0], R.hr.at[0], (b, jnp.minimum(r + 1, 3)))

    @pl.when(r < 3)
    def _():
        down.start()

    pump(cfg.pumps[1])

    @pl.when(r > 0)
    def _():
        down.wait_recv()

    @pl.when(r == 0)
    def _():
        R.h1r[...] = jnp.zeros(R.h1r.shape, BF)

    def h1_halo(j):
        cols = aligned(j, LANES)
        even = R.h1r[0, :, cols]
        odd = R.h1r[1, :, cols]
        for dc, v in ((0, rolled(odd.astype(F32), 1).astype(BF)), (1, even), (2, odd)):
            R.win1[out_rows(0), by_shard(dc, j)] = v

    loop(MID // LANES, h1_halo)

    @pl.when(r < 3)
    def _():
        down.wait_send()

    need(SPATIAL)

    def conv(win, weight, z):
        def body(j):
            cols = aligned(j, 256)
            z[:, cols] = dot(win[...], weight[:, cols])

        loop(MID // 256, body)

    conv(R.win1, R.f1, R.z2)
    forward_stats(R.z2, lambda j: mid_at(R.loc, j))
    mid_start(1)
    pump(cfg.pumps[2])
    mid_finish(1, R.t2)

    def activate(z, tot, params, dest):
        def body(j):
            cols = aligned(j, LANES)
            sc, sh = forward_terms(mid_at(tot, j), params, cols, OUT)
            ch = keep(j, 1.0)
            for o in range(OD):
                u = z[out_rows(o), cols] * sc + sh
                dest(o, cols, (silu_parts(u)[1] * (ch * R.pix_out[out_rows(o), :])).astype(BF))

        loop(MID // LANES, body)

    def to_h2(o, cols, v):
        R.h2[out_rows(o), cols] = v

    activate(R.z2, R.t2, norm_spatial, to_h2)
    need(EXPAND)

    def piece(weight, shard, j):
        n = weight.shape[0] // 16
        return weight[pl.ds(pl.multiple_of((shard * 4 + j) * n, n), n), :]

    def block(weight, j):
        return jnp.concatenate([piece(weight, q, j) for q in range(4)], axis=0)

    def expand_to(h, weight, z):
        def body(j):
            z[:, aligned(j, 512)] = dot(h[...], block(weight, j))

        loop(WIDE // 512, body)

    expand_to(R.h2, R.f2, R.z3)
    need(SHORTCUT)

    def zs_body(j):
        cols = aligned(j, 512)
        w = block(R.f3, j)
        for o in range(OD):
            R.zs[out_rows(o), cols] = dot(R.x0[2 * o, 0:S, :], w)

    loop(WIDE // 512, zs_body)
    forward_stats(R.z3, lambda j: wide_at(R.locw2, j), 0)
    forward_stats(R.zs, lambda j: wide_at(R.locw2, j), 8)
    wide_start(0, R.locw2)
    pump(cfg.pumps[3])
    wide_finish(0, R.t3)

    def u1_terms(j):
        cols = aligned(j, LANES)
        tot = wide_at(R.t3, j)
        sc3, sh3 = forward_terms(tot, norm_expand, cols, OUT, 0)
        scs, shs = forward_terms(tot, norm_shortcut, cols, OUT, 8)
        shift = sh3 + shs

        def u1(o):
            return R.z3[out_rows(o), cols] * sc3 + R.zs[out_rows(o), cols] * scs + shift

        return u1

    def y1_body(j):
        cols = aligned(j, LANES)
        u1 = u1_terms(j)
        ch = keep(j, float(WIDE // MID))
        for o in range(OD):
            y = silu_parts(u1(o))[1] * (ch * R.pix_out[out_rows(o), :])
            R.y1[out_rows(o), cols] = y.astype(BF)

    loop(WIDE // LANES, y1_body)
    need(SQUEEZE)

    def squeeze_body(j):
        cols = aligned(j, 256)
        R.z4[:, cols] = dot(R.y1[...], R.f4[:, cols])

    loop(MID // 256, squeeze_body)
    forward_stats(R.z4, lambda j: mid_at(R.loc, j))
    mid_start(2)
    pump(cfg.pumps[4])
    mid_finish(2, R.t4)

    def to_h4(o, cols, v):
        R.h4[o + 1, :, cols] = v

    activate(R.z4, R.t4, norm_squeeze, to_h4)
    pair = edge_exchange(R.h4, 0)
    pump(cfg.pumps[5])
    unit_windows(R.h4, R.win4, range(1, OD + 1), False)
    edge_wait(pair)
    unit_windows(R.h4, R.win4, (0, OD + 1), False)
    need(MIXING)
    conv(R.win4, R.f5, R.z5)
    forward_stats(R.z5, lambda j: mid_at(R.loc, j))
    mid_start(3)
    pump(cfg.pumps[6])
    mid_finish(3, R.t5)

    def to_h5(o, cols, v):
        R.h5[out_rows(o), cols] = v

    activate(R.z5, R.t5, norm_mixing, to_h5)
    need(WIDEN)
    expand_to(R.h5, R.f6, R.z6)
    forward_stats(R.z6, lambda j: wide_at(R.locw, j))
    wide_start(1, R.locw)
    wide_finish(1, R.t6)
    for u in range(len(units)):
        for i in w_stages(u):
            w_copy(u, i).wait_send()

    def u2_body(j):
        cols = aligned(j, LANES)
        tot = wide_at(R.t6, j)
        sc, sh = forward_terms(tot, norm_widen, cols, OUT)
        xa, xs = xhat_terms(tot, OUT)
        ch = keep(j, float(WIDE // MID))
        g0 = jnp.zeros((S, LANES), F32)
        g1 = jnp.zeros((S, LANES), F32)
        for o in range(OD):
            z = R.z6[out_rows(o), cols]
            u = z * sc + sh + R.y1[out_rows(o), cols].astype(F32)
            mask = ch * R.pix_out[out_rows(o), :]
            s, su = silu_parts(u)
            R.mixed_local[o, :, :, cols] = (su * mask).reshape(S // 8, 8, LANES).astype(BF)
            d = R.ct[out_rows(o), cols].astype(F32) * mask * (s * (1.0 + u * (1.0 - s)))
            R.du2[groups16(o), :, cols] = d.reshape(S // 16, 16, LANES)
            g0 = g0 + d * (z * xa + xs)
            g1 = g1 + d
        st = wide_at(R.locw, j)
        group_rows(st, 0, g0)
        group_rows(st, 3, g1)
        blank(st, 6, 2)

    ct_load.wait()
    loop(WIDE // LANES, u2_body)
    wide_start(2, R.locw)
    def mixed_copy(i, o):
        row = (x_row if i == 2 else r) * OD + o
        dst = R.mixed.at[:, row]
        src = dst if i == 2 else R.mixed_local.at[o, pl.ds(0, images)]
        if i == 3:
            return pltpu.make_async_copy(src, dst, R.xl.at[o])
        return remote(src, dst, R.xs.at[i, o], R.xr.at[i, o], (b, x_row if i == 1 else core_peer))

    for o in range(OD):
        for i in (0, 3):
            mixed_copy(i, o).start()
    wide_finish(2, R.g6)

    def widen_back(j):
        cols = aligned(j, LANES)
        f, a, bz = backward_terms(wide_at(R.t6, j), wide_at(R.g6, j), norm_widen, cols, OUT)
        for o in range(OD):
            d = f * R.du2[groups16(o), :, cols].reshape(S, LANES) - a - R.z6[out_rows(o), cols] * bz
            R.dz6[out_rows(o), cols] = (d * R.pix_out[out_rows(o), :]).astype(BF)

    loop(WIDE // LANES, widen_back)

    mine = {DY: lax.rem(b, 2), DN: lax.rem(lax.div(b, 2), 2), DF: lax.div(b, 4), DX: xb}
    turn = [1]
    begun = {}

    def partner(d):
        other = 1 - 2 * mine[d]
        if d == DX:
            return (b, x_row)
        return (b + other * {DY: 1, DN: 2, DF: 4}[d], r)

    def put(stage, w, core_of, bits, start, value):
        for n0, np_, order in cfg.parts[w]:
            lo, hi = max(start, n0), min(start + value.shape[0], n0 + np_)
            if lo >= hi:
                continue
            idx = 0
            for d in order:
                idx = 2 * idx + bits[d]
            row = 32 * n0 + (core_of * 16 + idx) * np_ + lo - n0
            stage[pl.ds(row if isinstance(row, int) else pl.multiple_of(row, 16), hi - lo), :] = value[
                lo - start : hi - start
            ].astype(BF)

    def batch_bits(y, zn, zf, x):
        return {DY: y, DN: zn, DF: zf, DX: x}

    def staged(w, fill):
        i = turn[0] % 2
        turn[0] += 1
        stage = (R.stage0, R.stage1)[i]
        n = cfg.rows[w]
        assert 32 * n <= stage.shape[0], w
        if cfg.reduce:
            fill(stage)
            begun[w] = (stage, 0)
            for p in range(len(cfg.parts[w])):
                rs_core(w, p).start()
            return
        if i in begun:
            begun[i].wait()
        fill(stage)
        off = 32 * cfg.offs[w]
        begun[i] = pltpu.make_async_copy(
            stage.at[pl.ds(0, 32 * n)], R.grads.at[pl.ds(off, 32 * n)], R.gs.at[i]
        )
        begun[i].start()

    def land_of(w):
        return getattr(R, ("l" if w in cfg.own_landing else "f") + str(w))

    def rs_core(w, p):
        n0, np_, order = cfg.parts[w][p]
        stage = begun[w][0]
        src = stage.at[pl.ds(pl.multiple_of(32 * n0 + (1 - core) * 16 * np_, 16), 16 * np_)]
        dst = land_of(w).at[pl.ds(32 * n0, 16 * np_)]
        return remote(src, dst, R.rs.at[w, p, 0], R.rr.at[w, p, 0], (b, core_peer))

    def rs_kept(w, p, step):
        n0, np_, order = cfg.parts[w][p]
        at, size = 0, 16 * np_
        for d in order[:step]:
            size = size // 2
            at = at + mine[d] * size
        return at, size

    def rs_link(w, p, step):
        n0, np_, order = cfg.parts[w][p]
        at, size = rs_kept(w, p, step - 1)
        size = size // 2
        d = order[step - 1]
        src = land_of(w).at[pl.ds(pl.multiple_of(32 * n0 + at + (1 - mine[d]) * size, 16), size)]
        dst = land_of(w).at[pl.ds(32 * n0 + 32 * np_ - 2 * size, size)]
        i = w
        return remote(src, dst, R.rs.at[i, p, step], R.rr.at[i, p, step], partner(d))

    def final(w):
        return getattr(R, "e" + str(w))

    def rs_add(w, p, step):
        n0, np_, order = cfg.parts[w][p]
        land = land_of(w)
        at, size = rs_kept(w, p, step)
        if step == 0:
            other, start = begun[w][0], 32 * n0 + core * 16 * np_
        else:
            other, start = land, 32 * n0 + 32 * np_ - 2 * size
        last_step = step == 4

        def body(i):
            rows = pl.ds(pl.multiple_of(32 * n0 + at + i * np_, 16), np_)
            v = land[rows, :] + other[pl.ds(pl.multiple_of(start + i * np_, 16), np_), :]
            if not last_step:
                land[rows, :] = v
            elif w in (SPATIAL, MIXING):
                k = cfg.rows[w] // 9
                final(w)[n0 // k : (n0 + np_) // k] = v.reshape(np_ // k, k, 512)
            else:
                final(w)[n0 : n0 + np_, :] = v

        if size == np_:
            body(0)
        else:
            loop(size // np_, body)

    def home(w, row):
        out, n = getattr(R, "o" + str(w)), cfg.rows[w]
        if w in (SPATIAL, MIXING):
            return out.at[:, aligned(row, n // 9)]
        if w in (EXPAND, SHORTCUT, WIDEN):
            return out.at[:, aligned(row, 512)]
        return out.at[aligned(row, n)]

    def fin_copy(w, i):
        dst = home(w, x_row if i == 2 else r)
        src = dst if i == 2 else final(w)
        if i == 3:
            return pltpu.make_async_copy(src, dst, R.fl.at[w])
        return remote(src, dst, R.fs.at[w, i], R.fr.at[w, i], (b, x_row if i == 1 else core_peer))

    def rs_step(*kernels):
        if not cfg.reduce:
            return
        for w in kernels:
            stage, step = begun[w]
            if step > 5:
                continue
            if step == 5:
                fin_copy(w, 1).wait_recv()
                fin_copy(w, 2).start()
            else:
                for p in range(len(cfg.parts[w])):
                    c = rs_core(w, p) if step == 0 else rs_link(w, p, step)
                    c.wait_recv()
                    rs_add(w, p, step)
                    if step < 4:
                        rs_link(w, p, step + 1).start()
                    c.wait_send()
                if step == 4:
                    for i in (1, 0, 3):
                        fin_copy(w, i).start()
            begun[w] = (stage, step + 1)

    def rs_round():
        if cfg.reduce:
            rs_step(*[w for w in reversed(list(begun)) if begun[w][1] < 6])

    def rs_end():
        if not cfg.reduce:
            for copy in begun.values():
                copy.wait()
            return
        while any(begun[w][1] < 6 for w in begun):
            rs_round()
        for w in cfg.rows:
            fin_copy(w, 0).wait()
            fin_copy(w, 1).wait_send()
            fin_copy(w, 2).wait()
            fin_copy(w, 3).wait()

    def fill_out(w, act, dz):
        def fill(stage):
            def body(j):
                res = dot_w(act(), dz[:, aligned(j, 512)])
                n = res.shape[0] // 8
                for i in range(8):
                    bits = batch_bits(i % 2, i // 2 % 2, i // 4, lax.div(j, 2))
                    put(stage, w, lax.rem(j, 2), bits, 0, res[i * n : (i + 1) * n])

            loop(WIDE // 512, body)

        return fill

    def fill_conv(w, win, dz):
        def fill(stage):
            n = MID // 32

            def body(q):
                for t0 in range(0, 9, 3):
                    cols = pl.ds(pl.multiple_of(q * (9 * LANES) + t0 * LANES, LANES), 3 * LANES)
                    res = dot_w(win[:, cols], dz())
                    for t in range(3):
                        for i in range(8):
                            bits = batch_bits(i // 4, lax.rem(q, 2), lax.div(q, 2), i // 2 % 2)
                            at = t * LANES + i * n
                            put(stage, w, i % 2, bits, (t0 + t) * n, res[at : at + n])

            loop(4, body)

        return fill

    def mid_back_sums(dh, z, tot, params):
        def body(j):
            cols = aligned(j, LANES)
            sums = mid_at(tot, j)
            sc, sh = forward_terms(sums, params, cols, OUT)
            xa, xs = xhat_terms(sums, OUT)
            ch = keep(j, 1.0)
            g0 = jnp.zeros((S, LANES), F32)
            g1 = jnp.zeros((S, LANES), F32)
            for o in range(OD):
                v = z[out_rows(o), cols]
                d = dh[out_rows(o), cols] * (ch * R.pix_out[out_rows(o), :]) * slope(v * sc + sh)
                dh[out_rows(o), cols] = d
                g0 = g0 + d * (v * xa + xs)
                g1 = g1 + d
            st = mid_at(R.loc, j)
            group_rows(st, 0, g0)
            group_rows(st, 3, g1)
            blank(st, 6, 2)

        loop(MID // LANES, body)

    def mid_back_apply(dh, z, tot, grads, params, dest):
        def body(j):
            cols = aligned(j, LANES)
            f, a, bz = backward_terms(mid_at(tot, j), mid_at(grads, j), params, cols, OUT)
            for o in range(OD):
                d = f * dh[out_rows(o), cols] - a - z[out_rows(o), cols] * bz
                dest(o, cols, (d * R.pix_out[out_rows(o), :]).astype(BF))

        loop(MID // LANES, body)

    def reduce_back(dz, weight, dh):
        def body(i):
            acc = None
            for j in range(4):
                w = jnp.concatenate([piece(weight, 2 * i + q, j) for q in range(2)], axis=0)
                v = dot_t(dz[:, j * 512 : (j + 1) * 512], w)
                acc = v if acc is None else acc + v
            dh[:, aligned(i, MID // 2)] = acc

        loop(2, body)

    def tap_rows(weight, i, t):
        n = MID // 4
        return jnp.concatenate(
            [weight[pl.ds(pl.multiple_of(((2 * i + q) * 9 + t) * n, n), n), :] for q in range(2)], axis=0
        )

    reduce_back(R.dz6, R.f6, R.dh)
    mid_back_sums(R.dh, R.z5, R.t5, norm_mixing)
    mid_start(4)
    mixed_copy(1, 0).start()
    staged(WIDEN, fill_out(WIDEN, lambda: R.h5[...], R.dz6))
    mid_finish(4, R.g5)

    def to_d5(o, cols, v):
        R.d5[o + 1, :, cols] = v

    mid_back_apply(R.dh, R.z5, R.t5, R.g5, norm_mixing, to_d5)
    pair = edge_exchange(R.d5, 1)
    rs_step(WIDEN)
    unit_windows(R.d5, R.win5, range(1, OD + 1), True)
    edge_wait(pair)
    unit_windows(R.d5, R.win5, (0, OD + 1), True)

    def conv_back(j):
        acc = None
        for t in range(9):
            v = dot_t(R.win5[:, t * MID : (t + 1) * MID], tap_rows(R.f5, j, t))
            acc = v if acc is None else acc + v
        R.dh[:, aligned(j, MID // 2)] = acc

    loop(2, conv_back)
    mid_back_sums(R.dh, R.z4, R.t4, norm_squeeze)
    mid_start(5)
    for o in range(1, OD):
        mixed_copy(1, o).start()
    rs_step(WIDEN)
    staged(MIXING, fill_conv(MIXING, R.win4, lambda: R.d5[1 : OD + 1].reshape(M, MID)))
    mid_finish(5, R.g4)

    def to_d4(o, cols, v):
        R.dz4[out_rows(o), cols] = v

    mid_back_apply(R.dh, R.z4, R.t4, R.g4, norm_squeeze, to_d4)

    def squeeze_back(j):
        n = WIDE // 4
        R.du1[:, :, aligned(j, n)] = dot_t(R.dz4[...], R.f4[aligned(j, n), :]).reshape(M // 16, 16, n)

    loop(4, squeeze_back)

    def u1_back(j):
        cols = aligned(j, LANES)
        u1 = u1_terms(j)
        tot = wide_at(R.t3, j)
        xa3, xs3 = xhat_terms(tot, OUT, 0)
        xas, xss = xhat_terms(tot, OUT, 8)
        ch = keep(j, float(WIDE // MID))
        g0 = jnp.zeros((S, LANES), F32)
        g1 = jnp.zeros((S, LANES), F32)
        g2 = jnp.zeros((S, LANES), F32)
        for o in range(OD):
            rows = out_rows(o)
            d = (R.du1[groups16(o), :, cols] + R.du2[groups16(o), :, cols]).reshape(S, LANES) * (ch * R.pix_out[rows, :]) * slope(u1(o))
            R.du1[groups16(o), :, cols] = d.reshape(S // 16, 16, LANES)
            g0 = g0 + d * (R.z3[rows, cols] * xa3 + xs3)
            g2 = g2 + d * (R.zs[rows, cols] * xas + xss)
            g1 = g1 + d
        st = wide_at(R.locw2, j)
        group_rows(st, 0, g0)
        group_rows(st, 3, g1)
        blank(st, 6, 2)
        group_rows(st, 8, g2)
        blank(st, 11, 5)

    loop(WIDE // LANES, u1_back)
    wide_start(3, R.locw2)

    def fill_squeeze(stage):
        def body(j):
            res = dot_w(R.y1[:, aligned(j, WIDE // 8)], R.dz4[...])
            n = res.shape[0] // 4
            bits = (lax.rem(j, 2), lax.rem(lax.div(j, 2), 2), lax.div(j, 4))
            for i in range(4):
                put(stage, SQUEEZE, i % 2, batch_bits(*bits, i // 2), 0, res[i * n : (i + 1) * n])

        loop(8, body)

    rs_step(MIXING, WIDEN)
    staged(SQUEEZE, fill_squeeze)
    wide_finish(3, R.g3)

    for o in range(OD):
        mixed_copy(1, o).wait_recv()
        mixed_copy(2, o).start()

    def u1_apply(j):
        cols = aligned(j, LANES)
        tot, grads = wide_at(R.t3, j), wide_at(R.g3, j)
        f3, a3, b3 = backward_terms(tot, grads, norm_expand, cols, OUT, 0, 0, 3)
        fs, as_, bs = backward_terms(tot, grads, norm_shortcut, cols, OUT, 8, 8, 3)
        for o in range(OD):
            rows = out_rows(o)
            d = R.du1[groups16(o), :, cols].reshape(S, LANES)
            pix = R.pix_out[rows, :]
            R.dz6[rows, cols] = ((f3 * d - a3 - R.z3[rows, cols] * b3) * pix).astype(BF)
            R.dzs[rows, cols] = ((fs * d - as_ - R.zs[rows, cols] * bs) * pix).astype(BF)

    loop(WIDE // LANES, u1_apply)
    reduce_back(R.dz6, R.f2, R.dh)
    mid_back_sums(R.dh, R.z2, R.t2, norm_spatial)
    mid_start(6)
    rs_step(SQUEEZE, MIXING, WIDEN)
    staged(EXPAND, fill_out(EXPAND, lambda: R.h2[...], R.dz6))

    def even_rows():
        return jnp.concatenate([R.x0[2 * o, 0:S, :] for o in range(OD)], axis=0)

    staged(SHORTCUT, fill_out(SHORTCUT, even_rows, R.dzs))
    mid_finish(6, R.g2)

    def to_d2(o, cols, v):
        R.d2[o, :, cols] = v

    mid_back_apply(R.dh, R.z2, R.t2, R.g2, norm_spatial, to_d2)
    up = remote(R.d2.at[0], R.d2.at[OD], R.hs.at[1], R.hr.at[1], (b, jnp.maximum(r - 1, 0)))

    @pl.when(r > 0)
    def _():
        up.start()

    @pl.when(r == 3)
    def _():
        R.d2[OD] = jnp.zeros(R.d2.shape[1:], BF)

    rs_step(EXPAND, SHORTCUT, WIDEN)
    staged(SPATIAL, fill_conv(SPATIAL, R.win1, lambda: R.d2[0:OD].reshape(M, MID)))

    @pl.when(r < 3)
    def _():
        up.wait_recv()

    @pl.when(r > 0)
    def _():
        up.wait_send()

    def dh1_at(k, j, width):
        return pl.ds(pl.multiple_of(k * MID + j * width, LANES), width)

    def d2_left(j):
        cols = aligned(j, LANES)
        for k in range(OD + 1):
            R.d2l[k, :, cols] = rolled(R.d2[k, :, cols].astype(F32), -1).astype(BF)

    loop(MID // LANES, d2_left)

    def spatial_back(j):
        here, left = R.d2[0:OD].reshape(M, MID), R.d2l[0:OD].reshape(M, MID)
        below, below_left = R.d2[1 : OD + 1].reshape(M, MID), R.d2l[1 : OD + 1].reshape(M, MID)

        def w(dr, dc):
            return tap_rows(R.f1, j, dr * 3 + dc)

        cols = aligned(j, MID // 2)
        parts = (
            ((here, 1, 1),),
            ((here, 1, 2), (left, 1, 0)),
            ((here, 2, 1), (below, 0, 1)),
            ((here, 2, 2), (left, 2, 0), (below, 0, 2), (below_left, 0, 0)),
        )
        for i, terms in enumerate(parts):
            rp, cp = divmod(i, 2)
            acc = None
            for v, dr, dc in terms:
                y = dot_t(v, w(dr, dc))
                acc = y if acc is None else acc + y
            for o in range(OD):
                R.zs[out_rows(cp), dh1_at(2 * o + rp, j, MID // 2)] = acc[out_rows(o)]

    loop(2, spatial_back)

    def h1_back(j):
        cols = aligned(j, LANES)
        sums = mid_at(R.t1, j)
        sc, sh = forward_terms(sums, norm_reduce, cols, IN)
        xa, xs = xhat_terms(sums, IN)
        ch = keep(j, 1.0)
        g0 = jnp.zeros((S, LANES), F32)
        g1 = jnp.zeros((S, LANES), F32)
        for k in range(RD):
            for p in range(2):
                rows = out_rows(p)
                v = R.z1[k, rows, cols]
                d = R.zs[rows, dh1_at(k, j, LANES)] * (ch * R.pix_in[k, rows, :]) * slope(v * sc + sh)
                R.zs[rows, dh1_at(k, j, LANES)] = d
                g0 = g0 + d * (v * xa + xs)
                g1 = g1 + d
        st = mid_at(R.loc, j)
        group_rows(st, 0, g0)
        group_rows(st, 3, g1)
        blank(st, 6, 2)

    loop(MID // LANES, h1_back)
    mid_start(7)
    rs_step(SPATIAL, SQUEEZE, MIXING, EXPAND, SHORTCUT)

    def norm_grads(i, src, gains, biases):
        at, width = cfg.norm_columns[i]
        parts, _, n = src.shape
        for h in range(parts):
            cols = slice(at + h * n, at + (h + 1) * n)
            for g in range(3):
                R.gn_values[g, 0:1, cols] = src[h, gains + g : gains + g + 1, :]
                R.gn_values[g, 1:2, cols] = src[h, biases + g : biases + g + 1, :]

    def gn_copy(first):
        at = MID if first else 0
        n = R.gn.shape[2] - MID if first else MID
        cols = pl.ds(at, n)
        return pltpu.make_async_copy(R.gn_values.at[:, :, cols], R.gn.at[:, :, cols], R.ld.at[3 + first])

    def short_back(j):
        acc = None
        for i in range(4):
            v = dot_t(R.dzs[:, i * 512 : (i + 1) * 512], piece(R.f3, j, i))
            acc = v if acc is None else acc + v
        R.z6[:, aligned(j, CIN // 4)] = acc

    loop(4, short_back)
    for i, (src, gains) in enumerate(((R.g2, 0), (R.g4, 0), (R.g5, 0), (R.g3, 0), (R.g3, 8), (R.g6, 0))):
        norm_grads(i + 1, src, gains, 3)
    gn_copies = [gn_copy(1)]
    gn_copies[0].start()
    mid_finish(7, R.g1)

    def h1_apply(j):
        cols = aligned(j, LANES)
        f, a, bz = backward_terms(mid_at(R.t1, j), mid_at(R.g1, j), norm_reduce, cols, IN)
        for k in range(RD):
            for p in range(2):
                rows = out_rows(p)
                d = f * R.zs[rows, dh1_at(k, j, LANES)] - a - R.z1[k, rows, cols] * bz
                R.y1[rows, dh1_at(k, j, LANES)] = (d * R.pix_in[k, rows, :]).astype(BF)

    loop(MID // LANES, h1_apply)

    def dz1(k):
        return R.y1[:, k * MID : (k + 1) * MID]

    def fill_reduce(stage):
        n = CIN // 32

        def body(j):
            act = R.x0[:, :, aligned(j, 256)].reshape(RD * 2 * S, 256)
            res = dot_w(act, jnp.concatenate([dz1(k) for k in range(RD)], axis=0))
            for i in range(8):
                bits = batch_bits(i // 4, lax.rem(j, 2), lax.div(j, 2), i // 2 % 2)
                put(stage, REDUCE, i % 2, bits, 0, res[i * n : (i + 1) * n])

        loop(4, body)

    staged(REDUCE, fill_reduce)
    rs_round()

    def input_grad(j):
        cols = aligned(j, CIN // 4)
        w = R.f0[aligned(j, CIN // 4), :]
        ch = jnp.concatenate(
            [keep(j * (CIN // 4 // LANES) + i, float(CIN // MID)) for i in range(CIN // 4 // LANES)],
            axis=1,
        )
        for k in range(RD):
            y = dot_t(dz1(k), w)
            for c in range(0, CIN // 4, LANES):
                base = c // LANES * 2 * S
                for p in range(2):
                    v = y[out_rows(p), c : c + LANES]
                    if p == 0 and k % 2 == 0:
                        v = v + R.z6[out_rows(k // 2), pl.ds(pl.multiple_of(j * (CIN // 4) + c, LANES), LANES)]
                    v = v * (ch[:, c : c + LANES] * R.pix_in[k, out_rows(p), :])
                    R.weave[pl.ds(base + p, S, stride=2), :] = v
                at = pl.ds(pl.multiple_of(k % 2 * CIN + j * (CIN // 4) + c, LANES), LANES)
                woven = R.weave[base : base + 2 * S, :]
                (R.du2, R.du1)[k // 2][:, :, at] = woven.reshape(M // 16, 16, LANES)

    for j in range(4):
        input_grad(j)
        if j < 3:
            rs_round()
    gin_copies = [
        pltpu.make_async_copy(
            (R.du2, R.du1)[k // 2].at[pl.ds(0, images), :, pl.ds(k % 2 * CIN, CIN)],
            R.gin.at[:, k],
            R.gi.at[k],
        )
        for k in range(RD)
    ]
    for c in gin_copies:
        c.start()
    rs_end()

    norm_grads(0, R.g1, 0, 3)
    gn_copies.append(gn_copy(0))
    gn_copies[1].start()

    for o in range(OD):
        mixed_copy(0, o).wait()
        mixed_copy(1, o).wait_send()
        mixed_copy(2, o).wait()
        mixed_copy(3, o).wait()
    for c in gin_copies + gn_copies:
        c.wait()


def plan(features, w_reduce, w_expand, batch):
    images, rd, _, cin = features.shape
    mid, wide = w_reduce.shape[1], w_expand.shape[1]
    cfg = SimpleNamespace(
        images=images,
        members=images * batch // 3,
        slots=-(-images * 8 // 16) * 16, in_rows=rd, out_rows=rd // 2, batch=batch, mid=mid, wide=wide, cin=cin
    )
    flat = {
        REDUCE: cin,
        SPATIAL: 9 * mid,
        EXPAND: mid * wide // 512,
        SHORTCUT: cin * wide // 512,
        SQUEEZE: wide,
        MIXING: 9 * mid,
        WIDEN: mid * wide // 512,
    }
    pieces = {SPATIAL: 3, MIXING: 3, SHORTCUT: 2}
    widths = (mid,) * 4 + (wide,) * 3
    cfg.norm_columns = [(sum(widths[:i]), n) for i, n in enumerate(widths)]
    cfg.units = []
    for name, n in flat.items():
        k = pieces.get(name, 1)
        for i in range(k):
            mode = 1 + len(cfg.units) % 2 if name else 0
            cfg.units.append((name, i * n // 4 // k, n // 4 // k, mode))
    cfg.lags = (0, 2, 4, 6)
    cfg.pumps = (3, 2, 2, 3, 2, 1, 20)
    cfg.flat = flat
    cfg.rows = {name: n // 32 for name, n in flat.items()}
    cfg.reduce = batch == 8
    orders = ((DX, DY, DN, DF), (DY, DN, DX, DF), (DN, DX, DY, DF))
    thirds = {WIDEN: 1, SQUEEZE: 0, EXPAND: 2}
    cfg.parts = {}
    for name, n in cfg.rows.items():
        if not cfg.reduce:
            cfg.parts[name] = [(0, n, (DF, DN, DY, DX))]
            continue
        tiles = [n // 16 // 3] * 3
        for i in range(n // 16 - sum(tiles)):
            tiles[(thirds.get(name, 0) + i) % 3] += 1
        cfg.parts[name], n0 = [], 0
        for tile, order in zip(tiles, orders):
            if tile:
                cfg.parts[name].append((n0, 16 * tile, order))
                n0 += 16 * tile
    cfg.own_landing = (REDUCE, SPATIAL, SHORTCUT)
    cfg.offs, total = {}, 0
    for name, n in cfg.rows.items():
        cfg.offs[name] = total
        total += n
    cfg.total = total
    return cfg


def run_blocks(cfg, smem_args, hbm_args):
    S, RD, OD, NB = cfg.slots, cfg.in_rows, cfg.out_rows, cfg.batch
    MID, WIDE, CIN = cfg.mid, cfg.wide, cfg.cin
    M = OD * S
    U = len(cfg.units)
    hbm = pl.BlockSpec(memory_space=pl.ANY)
    sds = jax.ShapeDtypeStruct
    outs = dict(
        mixed=(sds((cfg.images, 4 * OD, 8, WIDE), BF), hbm),
        gin=(sds((cfg.images, RD, 16, CIN), F32), hbm),
        gn=(sds((3, 2, 4 * MID + 3 * WIDE), F32), hbm),
    )
    final = {}
    if cfg.reduce:
        for w, n in cfg.rows.items():
            final[w] = (9, n // 9, 512) if w in (SPATIAL, MIXING) else (n, 512)
            shape = (n, 2048) if w in (EXPAND, SHORTCUT, WIDEN) else final[w][:-2] + (4 * final[w][-2], 512)
            outs["o" + str(w)] = (sds(shape, BF), hbm)
    else:
        outs.update(grads=(sds((32 * cfg.total, 512), BF), hbm))
    V = pltpu.VMEM
    mid_tot = V((2, 8, MID // 2), F32)
    scratch = dict(
        z1=V((RD, 2 * S, MID), F32),
        win1=V((M, 9 * MID), BF),
        h1s=V((2, S, MID), BF),
        h1r=V((2, S, MID), BF),
        z2=V((M, MID), F32),
        h2=V((M, MID), BF),
        z3=V((M, WIDE), F32),
        zs=V((M, WIDE), F32),
        y1=V((M, WIDE), BF),
        z4=V((M, MID), F32),
        h4=V((OD + 2, S, MID), BF),
        win4=V((M, 9 * MID), BF),
        z5=V((M, MID), F32),
        h5=V((M, MID), BF),
        z6=V((M, WIDE), F32),
        mixed_local=V((OD, S // 8, 8, WIDE), BF),
        du2=V((M // 16, 16, WIDE), F32),
        dz6=V((M, WIDE), BF),
        dh=V((M, MID), F32),
        d5=V((OD + 2, S, MID), BF),
        win5=V((M, 9 * MID), BF),
        dz4=V((M, MID), BF),
        du1=V((M // 16, 16, WIDE), F32),
        dzs=V((M, WIDE), BF),
        d2=V((OD + 1, S, MID), BF),
        d2l=V((OD + 1, S, MID), BF),
        stage0=V((32 * cfg.rows[MIXING], 512), BF),
        stage1=V((32 * cfg.rows[SHORTCUT], 512), BF),
        loc=mid_tot,
        locw=V((4, 8, WIDE // 4), F32),
        locw2=V((4, 16, WIDE // 4), F32),
        t1=mid_tot,
        t2=mid_tot,
        t3=V((4, 16, WIDE // 4), F32),
        t4=mid_tot,
        t5=mid_tot,
        t6=V((4, 8, WIDE // 4), F32),
        g1=mid_tot,
        g2=mid_tot,
        g3=V((4, 16, WIDE // 4), F32),
        g4=mid_tot,
        g5=mid_tot,
        g6=V((4, 8, WIDE // 4), F32),
        rc=V((2, 8, MID // 2), F32),
        rq=V((2, 2 * NB, 8, MID // 2), F32),
        rw=V((2, 4, 16, WIDE // 4), F32),
        wb=V((2, NB, 16, WIDE // 4), F32),
        wsend=pltpu.SemaphoreType.DMA((U, 7)),
        wrecv=pltpu.SemaphoreType.DMA((U, 7)),
        wloc=pltpu.SemaphoreType.DMA((7, 4)),
        ms=pltpu.SemaphoreType.DMA((3,)),
        mr=pltpu.SemaphoreType.DMA((3, 2)),
        ws=pltpu.SemaphoreType.DMA((4, 3)),
        wr=pltpu.SemaphoreType.DMA((4, 3)),
        hs=pltpu.SemaphoreType.DMA((2,)),
        hr=pltpu.SemaphoreType.DMA((2,)),
        es=pltpu.SemaphoreType.DMA((2, 2)),
        er=pltpu.SemaphoreType.DMA((2, 2)),
        xs=pltpu.SemaphoreType.DMA((3, OD)),
        xr=pltpu.SemaphoreType.DMA((3, OD)),
        xl=pltpu.SemaphoreType.DMA((OD,)),
        gs=pltpu.SemaphoreType.DMA((2,)),
        gi=pltpu.SemaphoreType.DMA((RD,)),
        rs=pltpu.SemaphoreType.DMA((7, 3, 5)),
        rr=pltpu.SemaphoreType.DMA((7, 3, 5)),
        fs=pltpu.SemaphoreType.DMA((7, 3)),
        fr=pltpu.SemaphoreType.DMA((7, 3)),
        fl=pltpu.SemaphoreType.DMA((7,)),
        x0=V((RD, 2 * S, CIN), BF),
        weave=V((4 * S, LANES), F32),
        ct=V((M, WIDE), BF),
        onehot=V((3, S, LANES), F32),
        active_slot=V((S, LANES), F32),
        pix_in=V((RD, 2 * S, LANES), F32),
        pix_out=V((M, LANES), F32),
        ld=pltpu.SemaphoreType.DMA((5,)),
        norm_values=V((3, 2, 4 * MID + 3 * WIDE), F32),
        gn_values=V((3, 2, 4 * MID + 3 * WIDE), F32),
    )
    scratch.update({"f" + str(name): V((n, 512), BF) for name, n in cfg.flat.items()})
    scratch.update({"l" + str(name): V((cfg.flat[name], 512), BF) for name in cfg.own_landing if cfg.reduce})
    scratch.update({"e" + str(w): V(shape, BF) for w, shape in final.items()})
    names = list(smem_args) + list(hbm_args) + list(outs) + list(scratch)
    smem = pl.BlockSpec(memory_space=pltpu.SMEM)
    res = pl.pallas_call(
        functools.partial(block_kernel, names, cfg),
        out_shape=[o[0] for o in outs.values()],
        in_specs=[smem] * len(smem_args) + [hbm] * len(hbm_args),
        out_specs=[o[1] for o in outs.values()],
        scratch_shapes=list(scratch.values()),
        compiler_params=pltpu.CompilerParams(
            collective_id=0, has_side_effects=True, vmem_limit_bytes=63 * 2**20
        ),
    )(*smem_args.values(), *hbm_args.values())
    return SimpleNamespace(**dict(zip(outs, res)))


def slot_layout(x, slots):
    images, rows, cols, channels = x.shape
    x = jnp.transpose(x, (1, 0, 2, 3)).reshape(rows, images * cols, channels)
    return jnp.pad(x, ((0, 0), (0, slots - images * cols), (0, 0)))


def per_device(
    features, w_reduce, w_spatial, w_expand, w_shortcut, w_squeeze, w_mixing, w_widen,
    norm_reduce, norm_spatial, norm_expand, norm_shortcut, norm_squeeze, norm_mixing, norm_widen,
    cotangent, resolution, active,
):
    images, rd, cols_in, cin = features.shape
    od = rd // 2
    nb = lax.axis_size("batch")
    cfg = plan(features, w_reduce, w_expand, nb)
    S, mid, wide = cfg.slots, cfg.mid, cfg.wide
    x = jnp.pad(features, ((0, 0), (0, 0), (0, 16 - cols_in), (0, 0)))
    x = x.reshape(images, rd, 8, 2, cin)
    x = jnp.transpose(x, (1, 3, 0, 2, 4)).reshape(rd, 2, images * 8, cin)
    x = jnp.pad(x, ((0, 0), (0, 0), (0, S - images * 8), (0, 0))).reshape(rd, 2 * S, cin)
    out_cols = cotangent.shape[2]
    ct = slot_layout(jnp.pad(cotangent, ((0, 0), (0, 0), (0, 8 - out_cols), (0, 0))), S)
    norms = jnp.concatenate(
        [
            jnp.transpose(n, (1, 0, 2))
            for n in (norm_reduce, norm_spatial, norm_squeeze, norm_mixing, norm_expand, norm_shortcut, norm_widen)
        ],
        axis=2,
    )
    res = run_blocks(
        cfg,
        dict(resolution=resolution, active=active),
        dict(
            features=x,
            norms=norms,
            cotangent=ct.reshape(od * S, wide),
            w0=w_reduce,
            w1=w_spatial.reshape(-1, mid),
            w2=w_expand,
            w3=w_shortcut,
            w4=w_squeeze,
            w5=w_mixing.reshape(-1, mid),
            w6=w_widen,
        ),
    )
    mixed = res.mixed[:, :, :out_cols]

    def unpack(g, name):
        b8, _, n, _ = g.shape
        if name in (SPATIAL, MIXING):
            k = n // 9
            return jnp.transpose(g.reshape(b8, 4, 9, k, 512), (2, 0, 1, 3, 4)).reshape(3, 3, b8 * 4 * k, 512)
        if name in (EXPAND, SHORTCUT, WIDEN):
            return jnp.transpose(g, (0, 2, 1, 3)).reshape(b8 * n, 2048)
        return g.reshape(b8 * 4 * n, 512)

    totals = []
    for name, n in cfg.rows.items():
        if cfg.reduce:
            g = getattr(res, "o" + str(name)).astype(F32)
            totals.append(g.reshape((3, 3) + g.shape[1:]) if g.ndim == 3 else g)
            continue
        at = cfg.offs[name]
        part = res.grads[32 * at : 32 * (at + n)].reshape(2, 8, 2, n, 512)
        part = unpack(jnp.transpose(part, (1, 2, 0, 3, 4)).reshape(8, 4, n, 512), name)
        dim = 2 if part.ndim == 4 else 0
        part = lax.psum_scatter(part, "batch", scatter_dimension=dim, tiled=True)
        totals.append(lax.psum(part, "rows").astype(F32))

    gn = [jnp.transpose(res.gn[:, :, at : at + n], (1, 0, 2)) for at, n in cfg.norm_columns]
    return (mixed, res.gin[:, :, :cols_in], *totals, gn[0], gn[1], gn[4], gn[5], gn[2], gn[3], gn[6])


def solution(mesh):
    w2, w4 = P("rows", None), P(None, None, "rows", None)
    o2, o4 = P("batch", None), P(None, None, "batch", None)
    return jax.shard_map(
        per_device,
        mesh=mesh,
        in_specs=(P("batch", "rows", None, None), w2, w4, w2, w2, w2, w4, w2)
        + (P(),) * 7
        + (P("batch", "rows", None, None), P(), P()),
        out_specs=(P("batch", None, None, None), P("batch", "rows", None, None), o2, o4, o2, o2, o2, o4, o2)
        + (P(),) * 7,
        check_vma=False,
    )
```

```python
import functools
from types import SimpleNamespace

import jax
import jax.numpy as jnp
from jax import lax
from jax.experimental import pallas as pl
from jax.experimental.pallas import tpu as pltpu
from jax.sharding import PartitionSpec as P

eps = 1e-05
MESH = pl.DeviceIdType.MESH
BF = jnp.bfloat16
F32 = jnp.float32
LANES = 128
REDUCE, SPATIAL, EXPAND, SHORTCUT, SQUEEZE, MIXING, WIDEN = range(7)
DX, DY, DN, DF = range(4)


def dot(a, b):
    return jnp.dot(a, b, preferred_element_type=F32)


def dot_t(a, b):
    return lax.dot_general(a, b, (((1,), (1,)), ((), ())), preferred_element_type=F32)


def dot_w(a, b):
    return lax.dot_general(a, b, (((0,), (0,)), ((), ())), preferred_element_type=F32)


def aligned(index, size):
    return pl.ds(pl.multiple_of(index * size, size), size)


def loop(count, body):
    def step(i, carry):
        body(i)
        return carry

    lax.fori_loop(0, count, step, 0)


def each(count, body):
    if count > 16:
        loop(count, body)
        return
    for i in range(count):
        body(i)


def silu_parts(u):
    s = jax.nn.sigmoid(u)
    return s, u * s


def slope(u):
    s = jax.nn.sigmoid(u)
    return s * (1.0 + u * (1.0 - s))


def block_kernel(names, cfg, *refs):
    R = SimpleNamespace(**dict(zip(names, refs)))
    S, RD, OD, NB = cfg.slots, cfg.in_rows, cfg.out_rows, cfg.batch
    MID, WIDE, CIN = cfg.mid, cfg.wide, cfg.cin
    M = OD * S
    b = lax.axis_index("batch")
    r = lax.axis_index("rows")
    core = lax.rem(r, 2)
    xb = lax.div(r, 2)
    core_peer = r + 1 - 2 * core
    x_row = lax.rem(r + 2, 4)
    diag = 3 - r
    half = lax.rem(b, 2)

    def flip(i, j):
        if isinstance(j, int):
            out = i
            for bit in range((2 * NB - 1).bit_length()):
                if j >> bit & 1:
                    out = out + (1 << bit) * (1 - 2 * lax.rem(lax.div(i, 1 << bit), 2))
            return out
        out = jnp.int32(0)
        bit = 1
        while bit < 2 * NB:
            p, q = lax.rem(lax.div(i, bit), 2), lax.rem(lax.div(j, bit), 2)
            out = out + bit * (p + q - 2 * p * q)
            bit *= 2
        return out

    me = b * 2 + xb

    def remote(src, dst, send, recv, dev):
        return pltpu.make_async_remote_copy(
            src_ref=src, dst_ref=dst, send_sem=send, recv_sem=recv, device_id=dev, device_id_type=MESH
        )

    def team(id2):
        return (lax.div(id2, 2), 2 * lax.rem(id2, 2) + core)

    units = cfg.units
    wsend, wrecv, wloc = R.wsend, R.wrecv, R.wloc
    near = lax.rem(lax.div(b, 2), 2)
    sides = ((half, (b + 1 - 2 * half, r)), (near, (b + 2 - 4 * near, r)))

    def wview(u, shard, at, fourths):
        w, k0, kn, _ = units[u]
        full = getattr(R, "f" + str(w))
        start = shard * (full.shape[0] // 4) + k0 + at * (kn // 4)
        return full.at[pl.ds(pl.multiple_of(start, 16), fourths * kn // 4)]

    def w_copy(u, i):
        mode = units[u][3]
        first, second = sides if mode == 1 else sides[::-1]
        quarter = x_row if i > 1 else r
        at, fourths, dev = 0, 4, (b, core_peer)
        if i == 1:
            dev = (b, x_row)
        if mode and i > 0:
            fourths = 2 if i > 4 else 1
            at = 2 * second[0] + first[0]
            if i == 3:
                dev = first[1]
            elif i == 4:
                at = at + 1 - 2 * first[0]
            elif i == 5:
                at, dev = 2 * second[0], second[1]
            elif i == 6:
                at = 2 - 2 * second[0]
        view = wview(u, quarter, at, fourths)
        return remote(view, view, wsend.at[u, i], wrecv.at[u, i], dev)

    def w_stages(u):
        return range(7) if units[u][3] else range(3)

    def w_local(w):
        src, full = getattr(R, "w" + str(w)), getattr(R, "f" + str(w))
        n, quarter = src.shape[0], full.shape[0] // 4
        return [
            pltpu.make_async_copy(
                src.at[:, pl.ds(512 * i, 512)],
                full.at[pl.ds(pl.multiple_of(r * quarter + i * n, 16), n)],
                wloc.at[w, i],
            )
            for i in range(src.shape[1] // 512)
        ]

    bar = pltpu.get_barrier_semaphore()
    for dev in ((b, core_peer), (b, diag)):
        pl.semaphore_signal(bar, inc=1, device_id=dev, device_id_type=MESH)

    def greet(j):
        pl.semaphore_signal(bar, inc=1, device_id=team(flip(me, j + 1)), device_id_type=MESH)

    loop(2 * NB - 1, greet)

    loaded = [w_local(w) for w in range(7)]
    for w in range(7):
        for c in loaded[w]:
            c.start()
        if w == 0:
            x0_load = pltpu.make_async_copy(R.features, R.x0, R.ld.at[0])
            x0_load.start()
    norm_load = pltpu.make_async_copy(R.norms, R.norm_values, R.ld.at[2])
    norm_load.start()
    ct_load = pltpu.make_async_copy(R.cotangent, R.ct, R.ld.at[1])
    ct_load.start()
    norm_reduce, norm_spatial, norm_squeeze, norm_mixing, norm_expand, norm_shortcut, norm_widen = [
        R.norm_values.at[:, :, pl.ds(at, width)] for at, width in cfg.norm_columns
    ]
    at_home = set()

    images = cfg.images
    column = lax.broadcasted_iota(jnp.int32, (8, LANES), 0).astype(F32)
    if 8 * images < S:
        tail = slice(8 * images, S)
        none = jnp.zeros((S - 8 * images, LANES), F32)
        R.active_slot[tail, :] = none
        for g in range(3):
            R.onehot[g, tail, :] = none
        for o in range(OD):
            R.pix_out[o * S + 8 * images : (o + 1) * S, :] = none
        for k in range(RD):
            for p in range(2):
                R.pix_in[k, p * S + 8 * images : (p + 1) * S, :] = none

    for i in range(images):
        group = R.resolution[b * images + i]
        side = (5 + group).astype(F32)
        here = slice(8 * i, 8 * i + 8)
        limit = jnp.zeros((8, LANES), F32)
        for g in range(3):
            is_g = jnp.where(group == g, 1.0, 0.0)
            R.onehot[g, here, :] = jnp.full((8, LANES), is_g, F32)
            limit = limit + is_g * R.active[g].astype(F32)
        R.active_slot[here, :] = limit
        for o in range(OD):
            inside = jnp.where((r * OD + o).astype(F32) < side, side, 0.0)
            R.pix_out[o * S + 8 * i : o * S + 8 * i + 8, :] = jnp.where(column < inside, 1.0, 0.0)
        for k in range(RD):
            inside = jnp.where((r * RD + k).astype(F32) < 2.0 * side, 2.0 * side, 0.0)
            for p in range(2):
                R.pix_in[k, p * S + 8 * i : p * S + 8 * i + 8, :] = jnp.where(2.0 * column + p < inside, 1.0, 0.0)

    pl.semaphore_wait(bar, 2 * NB + 1)

    def w_start(u):
        w = units[u][0]
        if w not in at_home:
            at_home.add(w)
            for c in loaded[w]:
                c.wait()
        w_copy(u, 1).start()
        w_copy(u, 0).start()

    def w_second(u):
        w_copy(u, 1).wait_recv()
        if units[u][3]:
            w_copy(u, 3).start()
        w_copy(u, 2).start()

    def w_third(u):
        if units[u][3]:
            w_copy(u, 3).wait_recv()
            w_copy(u, 5).start()
            w_copy(u, 4).start()

    def w_fourth(u):
        if units[u][3]:
            w_copy(u, 5).wait_recv()
            w_copy(u, 6).start()

    def w_ready(u):
        for i in w_stages(u)[::2]:
            w_copy(u, i).wait_recv()

    pumped = [0]
    lags = cfg.lags

    def pump(steps):
        for _ in range(steps):
            n = pumped[0]
            for lag, stage in zip(lags, (w_start, w_second, w_third, w_fourth)):
                if 0 <= n - lag < len(units):
                    stage(n - lag)
            pumped[0] = n + 1

    def need(name):
        last = max(u for u in range(len(units)) if units[u][0] == name)
        while pumped[0] < last + lags[3 if units[last][3] else 1] + 1:
            pump(1)
        for u in range(len(units)):
            if units[u][0] == name:
                w_ready(u)

    def mid_start(k):
        p = k % 2
        swap = remote(R.loc.at[1 - core], R.rc.at[p], R.ms.at[0], R.mr.at[0, p], (b, core_peer))
        swap.start()
        swap.wait_recv()
        R.rq[p, me] = R.loc[core] + R.rc[p]

        def send(j):
            to = team(flip(me, j + 1))
            remote(R.rq.at[p, me, pl.ds(0, 6)], R.rq.at[p, me, pl.ds(0, 6)], R.ms.at[1], R.mr.at[1, p], to).start()

        each(2 * NB - 1, send)
        swap.wait_send()

    def mid_finish(k, tot):
        p = k % 2
        rest = R.rq.at[p, pl.ds(0, 2 * NB - 1), pl.ds(0, 6)]
        every = remote(rest, rest, R.ms.at[1], R.mr.at[1, p], (b, x_row))
        every.wait_recv()
        total = R.rq[p, 0]
        for j in range(1, 2 * NB):
            total = total + R.rq[p, j]
        tot[core] = total
        back = remote(tot.at[core], tot.at[core], R.ms.at[2], R.mr.at[2, p], (b, core_peer))
        back.start()
        every.wait_send()
        back.wait()

    def wide_start(k, loc):
        n = loc.shape[1]
        rw, wb = R.rw.at[k % 2, :, pl.ds(0, n)], R.wb.at[k % 2, :, pl.ds(0, n)]
        rw[r] = loc[r]
        for to in (core_peer, x_row, diag):
            remote(loc.at[to], rw.at[r], R.ws.at[k, 0], R.wr.at[k, 0], (b, to)).start()
        three = remote(loc.at[pl.ds(0, 3)], rw.at[pl.ds(0, 3)], R.ws.at[k, 0], R.wr.at[k, 0], (b, core_peer))
        three.wait_recv()
        wb[b] = rw[0] + rw[1] + (rw[2] + rw[3])

        def send(j):
            to = lax.rem(b + j + 1, NB)
            remote(wb.at[b], wb.at[b], R.ws.at[k, 1], R.wr.at[k, 1], (to, r)).start()

        each(NB - 1, send)
        three.wait_send()

    def wide_finish(k, tot):
        n = tot.shape[1]
        wb = R.wb.at[k % 2, :, pl.ds(0, n)]
        rest = wb.at[pl.ds(0, NB - 1)]
        every = remote(rest, rest, R.ws.at[k, 1], R.wr.at[k, 1], (b, x_row))
        every.wait_recv()
        total = wb[0]
        for j in range(1, NB):
            total = total + wb[j]
        tot[r] = total
        for to in (core_peer, x_row, diag):
            remote(tot.at[r], tot.at[r], R.ws.at[k, 2], R.wr.at[k, 2], (b, to)).start()
        three = remote(tot.at[pl.ds(0, 3)], tot.at[pl.ds(0, 3)], R.ws.at[k, 2], R.wr.at[k, 2], (b, core_peer))
        every.wait_send()
        three.wait()

    def mid_at(ref, j):
        return ref.at[lax.div(j, 2), :, aligned(lax.rem(j, 2), LANES)]

    def wide_at(ref, j):
        return ref.at[lax.div(j, 4), :, aligned(lax.rem(j, 4), LANES)]

    def group_rows(ref, row, values):
        for g in range(3):
            ref[row + g : row + g + 1, :] = jnp.sum(values * R.onehot[g], axis=0, keepdims=True)

    def blank(ref, row, rows):
        ref[row : row + rows, :] = jnp.zeros((rows, LANES), F32)

    def spread(rows3):
        return rows3[0] * R.onehot[0] + rows3[1] * R.onehot[1] + rows3[2] * R.onehot[2]

    def moments(sums, inv_n, row=0):
        means, invs = [], []
        for g in range(3):
            n = 1.0 / inv_n[g]
            mean = sums[row + g : row + g + 1, :] * n
            var = sums[row + 3 + g : row + 4 + g, :] * n - mean * mean
            means.append(mean)
            invs.append(lax.rsqrt(var + eps))
        return means, invs

    OUT = [cfg.members * (5.0 + g) * (5.0 + g) for g in range(3)]
    IN = [cfg.members * (10.0 + 2.0 * g) * (10.0 + 2.0 * g) for g in range(3)]

    def forward_terms(sums, params, cols, inv_n, row=0):
        means, invs = moments(sums, inv_n, row)
        scales = [invs[g] * params[g, 0:1, cols] for g in range(3)]
        shifts = [params[g, 1:2, cols] - means[g] * scales[g] for g in range(3)]
        return spread(scales), spread(shifts)

    def xhat_terms(sums, inv_n, row=0):
        means, invs = moments(sums, inv_n, row)
        return spread(invs), spread([-means[g] * invs[g] for g in range(3)])

    def backward_terms(sums, grads, params, cols, inv_n, row=0, g0=0, g1=3):
        means, invs = moments(sums, inv_n, row)
        fs, az, bz = [], [], []
        for g in range(3):
            n = 1.0 / inv_n[g]
            f = invs[g] * params[g, 0:1, cols]
            gain = grads[g0 + g : g0 + g + 1, :] * n * invs[g]
            bias = grads[g1 + g : g1 + g + 1, :] * n
            fs.append(f)
            bz.append(f * gain)
            az.append(f * (bias - means[g] * gain))
        return spread(fs), spread(az), spread(bz)

    def keep(j, ratio):
        lane = lax.broadcasted_iota(jnp.int32, (S, LANES), 1).astype(F32) + j * float(LANES)
        return jnp.where(lane < R.active_slot[...] * ratio, 1.0, 0.0)

    def out_rows(k):
        return slice(k * S, (k + 1) * S)

    def groups16(o):
        return slice(o * (S // 16), (o + 1) * (S // 16))

    def forward_stats(z, loc_at, row=0):
        def body(j):
            cols = aligned(j, LANES)
            s = jnp.zeros((S, LANES), F32)
            q = jnp.zeros((S, LANES), F32)
            for o in range(OD):
                v = z[out_rows(o), cols]
                m = v * R.pix_out[out_rows(o), :]
                s = s + m
                q = q + m * v
            st = loc_at(j)
            group_rows(st, row, s)
            group_rows(st, row + 3, q)
            blank(st, row + 6, 2)

        loop(z.shape[-1] // LANES, body)

    def rolled(v, by):
        return pltpu.roll(v, by % S, 0)

    def by_shard(t, j):
        return pl.ds(pl.multiple_of(j * (9 * LANES) + t * LANES, LANES), LANES)

    def by_tap(t, j):
        return pl.ds(pl.multiple_of(t * MID + j * LANES, LANES), LANES)

    def unit_windows(halo, win, rows, flipped):
        place = by_tap if flipped else by_shard

        def body(j):
            cols = aligned(j, LANES)
            for k in rows:
                v = halo[k, :, cols].astype(F32)
                moved = (rolled(v, 1).astype(BF), v.astype(BF), rolled(v, -1).astype(BF))
                for dr in range(3):
                    o = k - dr
                    if not 0 <= o < OD:
                        continue
                    for dc in range(3):
                        t = (2 - dr) * 3 + 2 - dc if flipped else dr * 3 + dc
                        win[out_rows(o), place(t, j)] = moved[dc]

        loop(MID // LANES, body)

    def edge_exchange(halo, k):
        up = remote(halo.at[1], halo.at[OD + 1], R.es.at[k, 0], R.er.at[k, 0], (b, jnp.maximum(r - 1, 0)))
        down = remote(halo.at[OD], halo.at[0], R.es.at[k, 1], R.er.at[k, 1], (b, jnp.minimum(r + 1, 3)))

        @pl.when(r > 0)
        def _():
            up.start()

        @pl.when(r < 3)
        def _():
            down.start()

        @pl.when(r == 0)
        def _():
            halo[0] = jnp.zeros(halo.shape[1:], BF)

        @pl.when(r == 3)
        def _():
            halo[OD + 1] = jnp.zeros(halo.shape[1:], BF)

        return up, down

    def edge_wait(pair):
        up, down = pair

        @pl.when(r < 3)
        def _():
            up.wait_recv()
            down.wait_send()

        @pl.when(r > 0)
        def _():
            down.wait_recv()
            up.wait_send()

    x0_load.wait()
    norm_load.wait()
    need(REDUCE)

    def z1_rows(k):
        def mask(j):
            cols = aligned(j, LANES)
            ch = keep(j, float(CIN // MID))
            for p in range(2):
                m = (ch * R.pix_in[k, out_rows(p), :]).astype(BF)
                R.x0[k, out_rows(p), cols] = R.x0[k, out_rows(p), cols] * m

        loop(CIN // LANES, mask)
        R.z1[k] = dot(R.x0[k], R.f0[...])

    loop(RD, z1_rows)

    def z1_stats(j):
        cols = aligned(j, LANES)
        s = jnp.zeros((S, LANES), F32)
        q = jnp.zeros((S, LANES), F32)
        for k in range(RD):
            for p in range(2):
                v = R.z1[k, out_rows(p), cols]
                m = v * R.pix_in[k, out_rows(p), :]
                s = s + m
                q = q + m * v
        st = mid_at(R.loc, j)
        group_rows(st, 0, s)
        group_rows(st, 3, q)
        blank(st, 6, 2)

    loop(MID // LANES, z1_stats)
    mid_start(0)
    pump(cfg.pumps[0])
    mid_finish(0, R.t1)

    last = RD - 1

    def h1_body(j):
        cols = aligned(j, LANES)
        sc, sh = forward_terms(mid_at(R.t1, j), norm_reduce, cols, IN)
        ch = keep(j, 1.0)
        for k in range(RD - 1, -1, -1):
            for p in range(2):
                u = R.z1[k, out_rows(p), cols] * sc + sh
                h = silu_parts(u)[1] * (ch * R.pix_in[k, out_rows(p), :])
                if k == last:
                    R.h1s[p, :, cols] = h.astype(BF)
                for dr in range(3):
                    o2 = k + 1 - dr
                    if o2 % 2 or not 0 <= o2 // 2 < OD:
                        continue
                    o = o2 // 2
                    taps = ((1, h),) if p == 0 else ((0, rolled(h, 1)), (2, h))
                    for dc, v in taps:
                        t = dr * 3 + dc
                        R.win1[out_rows(o), by_shard(t, j)] = v.astype(BF)

    loop(MID // LANES, h1_body)
    down = remote(R.h1s, R.h1r, R.hs.at[0], R.hr.at[0], (b, jnp.minimum(r + 1, 3)))

    @pl.when(r < 3)
    def _():
        down.start()

    pump(cfg.pumps[1])

    @pl.when(r > 0)
    def _():
        down.wait_recv()

    @pl.when(r == 0)
    def _():
        R.h1r[...] = jnp.zeros(R.h1r.shape, BF)

    def h1_halo(j):
        cols = aligned(j, LANES)
        even = R.h1r[0, :, cols]
        odd = R.h1r[1, :, cols]
        for dc, v in ((0, rolled(odd.astype(F32), 1).astype(BF)), (1, even), (2, odd)):
            R.win1[out_rows(0), by_shard(dc, j)] = v

    loop(MID // LANES, h1_halo)

    @pl.when(r < 3)
    def _():
        down.wait_send()

    need(SPATIAL)

    def conv(win, weight, z):
        def body(j):
            cols = aligned(j, 256)
            z[:, cols] = dot(win[...], weight[:, cols])

        loop(MID // 256, body)

    conv(R.win1, R.f1, R.z2)
    forward_stats(R.z2, lambda j: mid_at(R.loc, j))
    def piece(weight, shard, j):
        n = weight.shape[0] // 16
        return weight[pl.ds(pl.multiple_of((shard * 4 + j) * n, n), n), :]

    def block(weight, j):
        return jnp.concatenate([piece(weight, q, j) for q in range(4)], axis=0)

    mid_start(1)
    pump(cfg.pumps[2])
    need(SHORTCUT)

    def zs_body(j):
        cols = aligned(j, 512)
        w = block(R.f3, j)
        for o in range(OD):
            R.zs[out_rows(o), cols] = dot(R.x0[2 * o, 0:S, :], w)

    loop(WIDE // 512, zs_body)
    forward_stats(R.zs, lambda j: wide_at(R.locw2, j), 8)
    mid_finish(1, R.t2)

    def activate(z, tot, params, dest):
        def body(j):
            cols = aligned(j, LANES)
            sc, sh = forward_terms(mid_at(tot, j), params, cols, OUT)
            ch = keep(j, 1.0)
            for o in range(OD):
                u = z[out_rows(o), cols] * sc + sh
                dest(o, cols, (silu_parts(u)[1] * (ch * R.pix_out[out_rows(o), :])).astype(BF))

        loop(MID // LANES, body)

    def to_h2(o, cols, v):
        R.h2[out_rows(o), cols] = v

    activate(R.z2, R.t2, norm_spatial, to_h2)
    need(EXPAND)

    def expand_to(h, weight, z):
        def body(j):
            z[:, aligned(j, 512)] = dot(h[...], block(weight, j))

        loop(WIDE // 512, body)

    expand_to(R.h2, R.f2, R.z3)
    forward_stats(R.z3, lambda j: wide_at(R.locw2, j), 0)
    wide_start(0, R.locw2)
    pump(cfg.pumps[3])
    wide_finish(0, R.t3)

    def u1_terms(j):
        cols = aligned(j, LANES)
        tot = wide_at(R.t3, j)
        sc3, sh3 = forward_terms(tot, norm_expand, cols, OUT, 0)
        scs, shs = forward_terms(tot, norm_shortcut, cols, OUT, 8)
        shift = sh3 + shs

        def u1(o):
            return R.z3[out_rows(o), cols] * sc3 + R.zs[out_rows(o), cols] * scs + shift

        return u1

    def y1_body(j):
        cols = aligned(j, LANES)
        u1 = u1_terms(j)
        ch = keep(j, float(WIDE // MID))
        for o in range(OD):
            y = silu_parts(u1(o))[1] * (ch * R.pix_out[out_rows(o), :])
            R.y1[out_rows(o), cols] = y.astype(BF)

    loop(WIDE // LANES, y1_body)
    need(SQUEEZE)

    def squeeze_body(j):
        cols = aligned(j, 256)
        R.z4[:, cols] = dot(R.y1[...], R.f4[:, cols])

    loop(MID // 256, squeeze_body)
    forward_stats(R.z4, lambda j: mid_at(R.loc, j))
    mid_start(2)
    pump(cfg.pumps[4])
    mid_finish(2, R.t4)

    def to_h4(o, cols, v):
        R.h4[o + 1, :, cols] = v

    activate(R.z4, R.t4, norm_squeeze, to_h4)
    pair = edge_exchange(R.h4, 0)
    pump(cfg.pumps[5])
    unit_windows(R.h4, R.win4, range(1, OD + 1), False)
    edge_wait(pair)
    unit_windows(R.h4, R.win4, (0, OD + 1), False)
    need(MIXING)
    conv(R.win4, R.f5, R.z5)
    forward_stats(R.z5, lambda j: mid_at(R.loc, j))
    mid_start(3)
    pump(cfg.pumps[6])
    mid_finish(3, R.t5)

    def to_h5(o, cols, v):
        R.h5[out_rows(o), cols] = v

    activate(R.z5, R.t5, norm_mixing, to_h5)
    need(WIDEN)
    expand_to(R.h5, R.f6, R.z6)
    forward_stats(R.z6, lambda j: wide_at(R.locw, j))
    wide_start(1, R.locw)
    wide_finish(1, R.t6)
    for u in range(len(units)):
        for i in w_stages(u):
            w_copy(u, i).wait_send()

    def u2_body(j):
        cols = aligned(j, LANES)
        tot = wide_at(R.t6, j)
        sc, sh = forward_terms(tot, norm_widen, cols, OUT)
        xa, xs = xhat_terms(tot, OUT)
        ch = keep(j, float(WIDE // MID))
        g0 = jnp.zeros((S, LANES), F32)
        g1 = jnp.zeros((S, LANES), F32)
        for o in range(OD):
            z = R.z6[out_rows(o), cols]
            u = z * sc + sh + R.y1[out_rows(o), cols].astype(F32)
            mask = ch * R.pix_out[out_rows(o), :]
            s, su = silu_parts(u)
            R.mixed_local[o, :, :, cols] = (su * mask).reshape(S // 8, 8, LANES).astype(BF)
            d = R.ct[out_rows(o), cols].astype(F32) * mask * (s * (1.0 + u * (1.0 - s)))
            R.du2[groups16(o), :, cols] = d.reshape(S // 16, 16, LANES)
            g0 = g0 + d * (z * xa + xs)
            g1 = g1 + d
        st = wide_at(R.locw, j)
        group_rows(st, 0, g0)
        group_rows(st, 3, g1)
        blank(st, 6, 2)

    ct_load.wait()
    loop(WIDE // LANES, u2_body)
    wide_start(2, R.locw)
    def mixed_copy(i, o):
        row = (x_row if i == 2 else r) * OD + o
        dst = R.mixed.at[:, row]
        src = dst if i == 2 else R.mixed_local.at[o, pl.ds(0, images)]
        if i == 3:
            return pltpu.make_async_copy(src, dst, R.xl.at[o])
        return remote(src, dst, R.xs.at[i, o], R.xr.at[i, o], (b, x_row if i == 1 else core_peer))

    for o in range(OD):
        for i in (0, 3):
            mixed_copy(i, o).start()
    wide_finish(2, R.g6)

    def widen_back(j):
        cols = aligned(j, LANES)
        f, a, bz = backward_terms(wide_at(R.t6, j), wide_at(R.g6, j), norm_widen, cols, OUT)
        for o in range(OD):
            d = f * R.du2[groups16(o), :, cols].reshape(S, LANES) - a - R.z6[out_rows(o), cols] * bz
            R.dz6[out_rows(o), cols] = (d * R.pix_out[out_rows(o), :]).astype(BF)

    loop(WIDE // LANES, widen_back)

    mine = {DY: lax.rem(b, 2), DN: lax.rem(lax.div(b, 2), 2), DF: lax.div(b, 4), DX: xb}
    turn = [1]
    begun = {}

    def partner(d):
        other = 1 - 2 * mine[d]
        if d == DX:
            return (b, x_row)
        return (b + other * {DY: 1, DN: 2, DF: 4}[d], r)

    def put(stage, w, core_of, bits, start, value):
        for n0, np_, order in cfg.parts[w]:
            lo, hi = max(start, n0), min(start + value.shape[0], n0 + np_)
            if lo >= hi:
                continue
            idx = 0
            for d in order:
                idx = 2 * idx + bits[d]
            row = 32 * n0 + (core_of * 16 + idx) * np_ + lo - n0
            stage[pl.ds(row if isinstance(row, int) else pl.multiple_of(row, 16), hi - lo), :] = value[
                lo - start : hi - start
            ].astype(BF)

    def batch_bits(y, zn, zf, x):
        return {DY: y, DN: zn, DF: zf, DX: x}

    def staged(w, fill):
        i = turn[0] % 2
        turn[0] += 1
        stage = (R.stage0, R.stage1)[i]
        n = cfg.rows[w]
        assert 32 * n <= stage.shape[0], w
        if cfg.reduce:
            fill(stage)
            begun[w] = (stage, [0] * len(cfg.parts[w]), [0])
            for p in range(len(cfg.parts[w])):
                rs_core(w, p).start()
            return
        if i in begun:
            begun[i].wait()
        fill(stage)
        off = 32 * cfg.offs[w]
        begun[i] = pltpu.make_async_copy(
            stage.at[pl.ds(0, 32 * n)], R.grads.at[pl.ds(off, 32 * n)], R.gs.at[i]
        )
        begun[i].start()

    def land_of(w):
        return getattr(R, ("l" if w in cfg.own_landing else "f") + str(w))

    def rs_core(w, p):
        n0, np_, order = cfg.parts[w][p]
        stage = begun[w][0]
        src = stage.at[pl.ds(pl.multiple_of(32 * n0 + (1 - core) * 16 * np_, 16), 16 * np_)]
        dst = land_of(w).at[pl.ds(32 * n0, 16 * np_)]
        return remote(src, dst, R.rs.at[w, p, 0], R.rr.at[w, p, 0], (b, core_peer))

    def rs_kept(w, p, step):
        n0, np_, order = cfg.parts[w][p]
        at, size = 0, 16 * np_
        for d in order[:step]:
            size = size // 2
            at = at + mine[d] * size
        return at, size

    def rs_link(w, p, step):
        n0, np_, order = cfg.parts[w][p]
        at, size = rs_kept(w, p, step - 1)
        size = size // 2
        d = order[step - 1]
        src = land_of(w).at[pl.ds(pl.multiple_of(32 * n0 + at + (1 - mine[d]) * size, 16), size)]
        dst = land_of(w).at[pl.ds(32 * n0 + 32 * np_ - 2 * size, size)]
        i = w
        return remote(src, dst, R.rs.at[i, p, step], R.rr.at[i, p, step], partner(d))

    def final(w):
        return getattr(R, "e" + str(w))

    def rs_add(w, p, step):
        n0, np_, order = cfg.parts[w][p]
        land = land_of(w)
        at, size = rs_kept(w, p, step)
        if step == 0:
            other, start = begun[w][0], 32 * n0 + core * 16 * np_
        else:
            other, start = land, 32 * n0 + 32 * np_ - 2 * size
        last_step = step == 4

        def body(i):
            rows = pl.ds(pl.multiple_of(32 * n0 + at + i * np_, 16), np_)
            v = land[rows, :] + other[pl.ds(pl.multiple_of(start + i * np_, 16), np_), :]
            if not last_step:
                land[rows, :] = v
            elif w in (SPATIAL, MIXING):
                k = cfg.rows[w] // 9
                final(w)[n0 // k : (n0 + np_) // k] = v.reshape(np_ // k, k, 512)
            else:
                final(w)[n0 : n0 + np_, :] = v

        if size == np_:
            body(0)
        else:
            loop(size // np_, body)

    def home(w, row):
        out, n = getattr(R, "o" + str(w)), cfg.rows[w]
        if w in (SPATIAL, MIXING):
            return out.at[:, aligned(row, n // 9)]
        if w in (EXPAND, SHORTCUT, WIDEN):
            return out.at[:, aligned(row, 512)]
        return out.at[aligned(row, n)]

    def fin_copy(w, i):
        dst = home(w, x_row if i == 2 else r)
        src = dst if i == 2 else final(w)
        if i == 3:
            return pltpu.make_async_copy(src, dst, R.fl.at[w])
        return remote(src, dst, R.fs.at[w, i], R.fr.at[w, i], (b, x_row if i == 1 else core_peer))

    def rs_step(*kernels, parts=(0, 1, 2)):
        if not cfg.reduce:
            return
        for w in kernels:
            stage, steps, ends = begun[w]
            if ends[0] == 1:
                fin_copy(w, 1).wait_recv()
                fin_copy(w, 2).start()
                ends[0] = 2
            for p in parts:
                if p >= len(steps) or steps[p] > 4:
                    continue
                step = steps[p]
                c = rs_core(w, p) if step == 0 else rs_link(w, p, step)
                c.wait_recv()
                rs_add(w, p, step)
                if step < 4:
                    rs_link(w, p, step + 1).start()
                c.wait_send()
                steps[p] = step + 1
            if ends[0] == 0 and min(steps) == 5:
                for i in (1, 0, 3):
                    fin_copy(w, i).start()
                ends[0] = 1

    def rs_round():
        if cfg.reduce:
            rs_step(*[w for w in reversed(list(begun)) if begun[w][2][0] < 2])

    def rs_end():
        if not cfg.reduce:
            for copy in begun.values():
                copy.wait()
            return
        while any(begun[w][2][0] < 2 for w in begun):
            rs_round()
        for w in cfg.rows:
            fin_copy(w, 0).wait()
            fin_copy(w, 1).wait_send()
            fin_copy(w, 2).wait()
            fin_copy(w, 3).wait()

    def fill_out(w, act, dz):
        def fill(stage):
            def body(j):
                res = dot_w(act(), dz[:, aligned(j, 512)])
                n = res.shape[0] // 8
                for i in range(8):
                    bits = batch_bits(i % 2, i // 2 % 2, i // 4, lax.div(j, 2))
                    put(stage, w, lax.rem(j, 2), bits, 0, res[i * n : (i + 1) * n])

            loop(WIDE // 512, body)

        return fill

    def fill_conv(w, win, dz):
        def fill(stage):
            n = MID // 32

            def body(q):
                for t0 in range(0, 9, 3):
                    cols = pl.ds(pl.multiple_of(q * (9 * LANES) + t0 * LANES, LANES), 3 * LANES)
                    res = dot_w(win[:, cols], dz())
                    for t in range(3):
                        for i in range(8):
                            bits = batch_bits(i // 4, lax.rem(q, 2), lax.div(q, 2), i // 2 % 2)
                            at = t * LANES + i * n
                            put(stage, w, i % 2, bits, (t0 + t) * n, res[at : at + n])

            loop(4, body)

        return fill

    def mid_back_sums(dh, z, tot, params):
        def body(j):
            cols = aligned(j, LANES)
            sums = mid_at(tot, j)
            sc, sh = forward_terms(sums, params, cols, OUT)
            xa, xs = xhat_terms(sums, OUT)
            ch = keep(j, 1.0)
            g0 = jnp.zeros((S, LANES), F32)
            g1 = jnp.zeros((S, LANES), F32)
            for o in range(OD):
                v = z[out_rows(o), cols]
                d = dh[out_rows(o), cols] * (ch * R.pix_out[out_rows(o), :]) * slope(v * sc + sh)
                dh[out_rows(o), cols] = d
                g0 = g0 + d * (v * xa + xs)
                g1 = g1 + d
            st = mid_at(R.loc, j)
            group_rows(st, 0, g0)
            group_rows(st, 3, g1)
            blank(st, 6, 2)

        loop(MID // LANES, body)

    def mid_back_apply(dh, z, tot, grads, params, dest):
        def body(j):
            cols = aligned(j, LANES)
            f, a, bz = backward_terms(mid_at(tot, j), mid_at(grads, j), params, cols, OUT)
            for o in range(OD):
                d = f * dh[out_rows(o), cols] - a - z[out_rows(o), cols] * bz
                dest(o, cols, (d * R.pix_out[out_rows(o), :]).astype(BF))

        loop(MID // LANES, body)

    def reduce_back(dz, weight, dh):
        def body(i):
            acc = None
            for j in range(4):
                w = jnp.concatenate([piece(weight, 2 * i + q, j) for q in range(2)], axis=0)
                v = dot_t(dz[:, j * 512 : (j + 1) * 512], w)
                acc = v if acc is None else acc + v
            dh[:, aligned(i, MID // 2)] = acc

        loop(2, body)

    def tap_rows(weight, i, t):
        n = MID // 4
        return jnp.concatenate(
            [weight[pl.ds(pl.multiple_of(((2 * i + q) * 9 + t) * n, n), n), :] for q in range(2)], axis=0
        )

    reduce_back(R.dz6, R.f6, R.dh)
    mid_back_sums(R.dh, R.z5, R.t5, norm_mixing)
    mid_start(4)
    mixed_copy(1, 0).start()
    staged(WIDEN, fill_out(WIDEN, lambda: R.h5[...], R.dz6))
    mid_finish(4, R.g5)

    def to_d5(o, cols, v):
        R.d5[o + 1, :, cols] = v

    mid_back_apply(R.dh, R.z5, R.t5, R.g5, norm_mixing, to_d5)
    pair = edge_exchange(R.d5, 1)
    rs_step(WIDEN)
    unit_windows(R.d5, R.win5, range(1, OD + 1), True)
    edge_wait(pair)
    unit_windows(R.d5, R.win5, (0, OD + 1), True)

    def conv_back(j):
        acc = None
        for t in range(9):
            v = dot_t(R.win5[:, t * MID : (t + 1) * MID], tap_rows(R.f5, j, t))
            acc = v if acc is None else acc + v
        R.dh[:, aligned(j, MID // 2)] = acc

    loop(2, conv_back)
    mid_back_sums(R.dh, R.z4, R.t4, norm_squeeze)
    mid_start(5)
    for o in range(1, OD):
        mixed_copy(1, o).start()
    rs_step(WIDEN)
    staged(MIXING, fill_conv(MIXING, R.win4, lambda: R.d5[1 : OD + 1].reshape(M, MID)))
    mid_finish(5, R.g4)

    def to_d4(o, cols, v):
        R.dz4[out_rows(o), cols] = v

    mid_back_apply(R.dh, R.z4, R.t4, R.g4, norm_squeeze, to_d4)

    def squeeze_back(j):
        n = WIDE // 4
        R.du1[:, :, aligned(j, n)] = dot_t(R.dz4[...], R.f4[aligned(j, n), :]).reshape(M // 16, 16, n)

    loop(4, squeeze_back)

    def u1_back(j):
        cols = aligned(j, LANES)
        u1 = u1_terms(j)
        tot = wide_at(R.t3, j)
        xa3, xs3 = xhat_terms(tot, OUT, 0)
        xas, xss = xhat_terms(tot, OUT, 8)
        ch = keep(j, float(WIDE // MID))
        g0 = jnp.zeros((S, LANES), F32)
        g1 = jnp.zeros((S, LANES), F32)
        g2 = jnp.zeros((S, LANES), F32)
        for o in range(OD):
            rows = out_rows(o)
            d = (R.du1[groups16(o), :, cols] + R.du2[groups16(o), :, cols]).reshape(S, LANES) * (ch * R.pix_out[rows, :]) * slope(u1(o))
            R.du1[groups16(o), :, cols] = d.reshape(S // 16, 16, LANES)
            g0 = g0 + d * (R.z3[rows, cols] * xa3 + xs3)
            g2 = g2 + d * (R.zs[rows, cols] * xas + xss)
            g1 = g1 + d
        st = wide_at(R.locw2, j)
        group_rows(st, 0, g0)
        group_rows(st, 3, g1)
        blank(st, 6, 2)
        group_rows(st, 8, g2)
        blank(st, 11, 5)

    loop(WIDE // LANES, u1_back)
    wide_start(3, R.locw2)

    def fill_squeeze(stage):
        def body(j):
            res = dot_w(R.y1[:, aligned(j, WIDE // 8)], R.dz4[...])
            n = res.shape[0] // 4
            bits = (lax.rem(j, 2), lax.rem(lax.div(j, 2), 2), lax.div(j, 4))
            for i in range(4):
                put(stage, SQUEEZE, i % 2, batch_bits(*bits, i // 2), 0, res[i * n : (i + 1) * n])

        loop(8, body)

    rs_step(MIXING, WIDEN)
    staged(SQUEEZE, fill_squeeze)
    wide_finish(3, R.g3)

    for o in range(OD):
        mixed_copy(1, o).wait_recv()
        mixed_copy(2, o).start()

    def u1_apply(j):
        cols = aligned(j, LANES)
        tot, grads = wide_at(R.t3, j), wide_at(R.g3, j)
        f3, a3, b3 = backward_terms(tot, grads, norm_expand, cols, OUT, 0, 0, 3)
        fs, as_, bs = backward_terms(tot, grads, norm_shortcut, cols, OUT, 8, 8, 3)
        for o in range(OD):
            rows = out_rows(o)
            d = R.du1[groups16(o), :, cols].reshape(S, LANES)
            pix = R.pix_out[rows, :]
            R.dz6[rows, cols] = ((f3 * d - a3 - R.z3[rows, cols] * b3) * pix).astype(BF)
            R.dzs[rows, cols] = ((fs * d - as_ - R.zs[rows, cols] * bs) * pix).astype(BF)

    loop(WIDE // LANES, u1_apply)
    reduce_back(R.dz6, R.f2, R.dh)
    mid_back_sums(R.dh, R.z2, R.t2, norm_spatial)
    mid_start(6)
    rs_step(SQUEEZE, MIXING, WIDEN)
    staged(EXPAND, fill_out(EXPAND, lambda: R.h2[...], R.dz6))

    def even_rows():
        return jnp.concatenate([R.x0[2 * o, 0:S, :] for o in range(OD)], axis=0)

    staged(SHORTCUT, fill_out(SHORTCUT, even_rows, R.dzs))
    mid_finish(6, R.g2)

    def to_d2(o, cols, v):
        R.d2[o, :, cols] = v

    mid_back_apply(R.dh, R.z2, R.t2, R.g2, norm_spatial, to_d2)
    up = remote(R.d2.at[0], R.d2.at[OD], R.hs.at[1], R.hr.at[1], (b, jnp.maximum(r - 1, 0)))

    @pl.when(r > 0)
    def _():
        up.start()

    @pl.when(r == 3)
    def _():
        R.d2[OD] = jnp.zeros(R.d2.shape[1:], BF)

    rs_step(EXPAND, SHORTCUT, MIXING, SQUEEZE, WIDEN)
    staged(SPATIAL, fill_conv(SPATIAL, R.win1, lambda: R.d2[0:OD].reshape(M, MID)))

    @pl.when(r < 3)
    def _():
        up.wait_recv()

    @pl.when(r > 0)
    def _():
        up.wait_send()

    def dh1_at(k, j, width):
        return pl.ds(pl.multiple_of(k * MID + j * width, LANES), width)

    def d2_left(j):
        cols = aligned(j, LANES)
        for k in range(OD + 1):
            R.d2l[k, :, cols] = rolled(R.d2[k, :, cols].astype(F32), -1).astype(BF)

    loop(MID // LANES, d2_left)

    def spatial_back(j):
        here, left = R.d2[0:OD].reshape(M, MID), R.d2l[0:OD].reshape(M, MID)
        below, below_left = R.d2[1 : OD + 1].reshape(M, MID), R.d2l[1 : OD + 1].reshape(M, MID)

        def w(dr, dc):
            return tap_rows(R.f1, j, dr * 3 + dc)

        cols = aligned(j, MID // 2)
        parts = (
            ((here, 1, 1),),
            ((here, 1, 2), (left, 1, 0)),
            ((here, 2, 1), (below, 0, 1)),
            ((here, 2, 2), (left, 2, 0), (below, 0, 2), (below_left, 0, 0)),
        )
        for i, terms in enumerate(parts):
            rp, cp = divmod(i, 2)
            acc = None
            for v, dr, dc in terms:
                y = dot_t(v, w(dr, dc))
                acc = y if acc is None else acc + y
            for o in range(OD):
                R.zs[out_rows(cp), dh1_at(2 * o + rp, j, MID // 2)] = acc[out_rows(o)]

    loop(2, spatial_back)

    def h1_back(j):
        cols = aligned(j, LANES)
        sums = mid_at(R.t1, j)
        sc, sh = forward_terms(sums, norm_reduce, cols, IN)
        xa, xs = xhat_terms(sums, IN)
        ch = keep(j, 1.0)
        g0 = jnp.zeros((S, LANES), F32)
        g1 = jnp.zeros((S, LANES), F32)
        for k in range(RD):
            for p in range(2):
                rows = out_rows(p)
                v = R.z1[k, rows, cols]
                d = R.zs[rows, dh1_at(k, j, LANES)] * (ch * R.pix_in[k, rows, :]) * slope(v * sc + sh)
                R.zs[rows, dh1_at(k, j, LANES)] = d
                g0 = g0 + d * (v * xa + xs)
                g1 = g1 + d
        st = mid_at(R.loc, j)
        group_rows(st, 0, g0)
        group_rows(st, 3, g1)
        blank(st, 6, 2)

    loop(MID // LANES, h1_back)
    mid_start(7)
    rs_step(SPATIAL, SQUEEZE, MIXING, EXPAND, SHORTCUT)

    def norm_grads(i, src, gains, biases):
        at, width = cfg.norm_columns[i]
        parts, _, n = src.shape
        for h in range(parts):
            cols = slice(at + h * n, at + (h + 1) * n)
            for g in range(3):
                R.gn_values[g, 0:1, cols] = src[h, gains + g : gains + g + 1, :]
                R.gn_values[g, 1:2, cols] = src[h, biases + g : biases + g + 1, :]

    def gn_copy(first):
        at = MID if first else 0
        n = R.gn.shape[2] - MID if first else MID
        cols = pl.ds(at, n)
        return pltpu.make_async_copy(R.gn_values.at[:, :, cols], R.gn.at[:, :, cols], R.ld.at[3 + first])

    def short_back(j):
        acc = None
        for i in range(4):
            v = dot_t(R.dzs[:, i * 512 : (i + 1) * 512], piece(R.f3, j, i))
            acc = v if acc is None else acc + v
        R.z6[:, aligned(j, CIN // 4)] = acc

    loop(4, short_back)
    for i, (src, gains) in enumerate(((R.g2, 0), (R.g4, 0), (R.g5, 0), (R.g3, 0), (R.g3, 8), (R.g6, 0))):
        norm_grads(i + 1, src, gains, 3)
    gn_copies = [gn_copy(1)]
    gn_copies[0].start()
    mid_finish(7, R.g1)

    def h1_apply(j):
        cols = aligned(j, LANES)
        f, a, bz = backward_terms(mid_at(R.t1, j), mid_at(R.g1, j), norm_reduce, cols, IN)
        for k in range(RD):
            for p in range(2):
                rows = out_rows(p)
                d = f * R.zs[rows, dh1_at(k, j, LANES)] - a - R.z1[k, rows, cols] * bz
                R.y1[rows, dh1_at(k, j, LANES)] = (d * R.pix_in[k, rows, :]).astype(BF)

    loop(MID // LANES, h1_apply)

    def dz1(k):
        return R.y1[:, k * MID : (k + 1) * MID]

    def fill_reduce(stage):
        n = CIN // 32

        def body(j):
            act = R.x0[:, :, aligned(j, 256)].reshape(RD * 2 * S, 256)
            res = dot_w(act, jnp.concatenate([dz1(k) for k in range(RD)], axis=0))
            for i in range(8):
                bits = batch_bits(i // 4, lax.rem(j, 2), lax.div(j, 2), i // 2 % 2)
                put(stage, REDUCE, i % 2, bits, 0, res[i * n : (i + 1) * n])

        loop(4, body)

    staged(REDUCE, fill_reduce)
    rs_round()

    def input_grad(j):
        cols = aligned(j, CIN // 4)
        w = R.f0[aligned(j, CIN // 4), :]
        ch = jnp.concatenate(
            [keep(j * (CIN // 4 // LANES) + i, float(CIN // MID)) for i in range(CIN // 4 // LANES)],
            axis=1,
        )
        for k in range(RD):
            y = dot_t(dz1(k), w)
            for c in range(0, CIN // 4, LANES):
                base = c // LANES * 2 * S
                for p in range(2):
                    v = y[out_rows(p), c : c + LANES]
                    if p == 0 and k % 2 == 0:
                        v = v + R.z6[out_rows(k // 2), pl.ds(pl.multiple_of(j * (CIN // 4) + c, LANES), LANES)]
                    v = v * (ch[:, c : c + LANES] * R.pix_in[k, out_rows(p), :])
                    R.weave[pl.ds(base + p, S, stride=2), :] = v
                at = pl.ds(pl.multiple_of(k % 2 * CIN + j * (CIN // 4) + c, LANES), LANES)
                woven = R.weave[base : base + 2 * S, :]
                (R.du2, R.du1)[k // 2][:, :, at] = woven.reshape(M // 16, 16, LANES)

    for j in range(4):
        input_grad(j)
        if j < 3:
            rs_round()
    gin_copies = [
        pltpu.make_async_copy(
            (R.du2, R.du1)[k // 2].at[pl.ds(0, images), :, pl.ds(k % 2 * CIN, CIN)],
            R.gin.at[:, k],
            R.gi.at[k],
        )
        for k in range(RD)
    ]
    for c in gin_copies:
        c.start()
    rs_end()

    norm_grads(0, R.g1, 0, 3)
    gn_copies.append(gn_copy(0))
    gn_copies[1].start()

    for o in range(OD):
        mixed_copy(0, o).wait()
        mixed_copy(1, o).wait_send()
        mixed_copy(2, o).wait()
        mixed_copy(3, o).wait()
    for c in gin_copies + gn_copies:
        c.wait()


def plan(features, w_reduce, w_expand, batch):
    images, rd, _, cin = features.shape
    mid, wide = w_reduce.shape[1], w_expand.shape[1]
    cfg = SimpleNamespace(
        images=images,
        members=images * batch // 3,
        slots=-(-images * 8 // 16) * 16, in_rows=rd, out_rows=rd // 2, batch=batch, mid=mid, wide=wide, cin=cin
    )
    flat = {
        REDUCE: cin,
        SPATIAL: 9 * mid,
        EXPAND: mid * wide // 512,
        SHORTCUT: cin * wide // 512,
        SQUEEZE: wide,
        MIXING: 9 * mid,
        WIDEN: mid * wide // 512,
    }
    pieces = {SPATIAL: 3, MIXING: 3, SHORTCUT: 2}
    widths = (mid,) * 4 + (wide,) * 3
    cfg.norm_columns = [(sum(widths[:i]), n) for i, n in enumerate(widths)]
    cfg.units = []
    for name in (REDUCE, SPATIAL, SHORTCUT, EXPAND, SQUEEZE, MIXING, WIDEN):
        n, k = flat[name], pieces.get(name, 1)
        for i in range(k):
            mode = 1 + len(cfg.units) % 2 if name else 0
            cfg.units.append((name, i * n // 4 // k, n // 4 // k, mode))
    cfg.lags = (0, 2, 4, 6)
    cfg.pumps = (3, 1, 2, 2, 2, 2, 3)
    cfg.flat = flat
    cfg.rows = {name: n // 32 for name, n in flat.items()}
    cfg.reduce = batch == 8
    orders = ((DX, DY, DN, DF), (DY, DN, DX, DF), (DN, DX, DY, DF))
    thirds = {WIDEN: 1, SQUEEZE: 0, EXPAND: 2}
    cfg.parts = {}
    for name, n in cfg.rows.items():
        if not cfg.reduce:
            cfg.parts[name] = [(0, n, (DF, DN, DY, DX))]
            continue
        tiles = [n // 16 // 3] * 3
        for i in range(n // 16 - sum(tiles)):
            tiles[(thirds.get(name, 0) + i) % 3] += 1
        cfg.parts[name], n0 = [], 0
        for tile, order in zip(tiles, orders):
            if tile:
                cfg.parts[name].append((n0, 16 * tile, order))
                n0 += 16 * tile
    cfg.own_landing = (REDUCE, SPATIAL, SHORTCUT)
    cfg.offs, total = {}, 0
    for name, n in cfg.rows.items():
        cfg.offs[name] = total
        total += n
    cfg.total = total
    return cfg


def run_blocks(cfg, smem_args, hbm_args):
    S, RD, OD, NB = cfg.slots, cfg.in_rows, cfg.out_rows, cfg.batch
    MID, WIDE, CIN = cfg.mid, cfg.wide, cfg.cin
    M = OD * S
    U = len(cfg.units)
    hbm = pl.BlockSpec(memory_space=pl.ANY)
    sds = jax.ShapeDtypeStruct
    outs = dict(
        mixed=(sds((cfg.images, 4 * OD, 8, WIDE), BF), hbm),
        gin=(sds((cfg.images, RD, 16, CIN), F32), hbm),
        gn=(sds((3, 2, 4 * MID + 3 * WIDE), F32), hbm),
    )
    final = {}
    if cfg.reduce:
        for w, n in cfg.rows.items():
            final[w] = (9, n // 9, 512) if w in (SPATIAL, MIXING) else (n, 512)
            shape = (n, 2048) if w in (EXPAND, SHORTCUT, WIDEN) else final[w][:-2] + (4 * final[w][-2], 512)
            outs["o" + str(w)] = (sds(shape, BF), hbm)
    else:
        outs.update(grads=(sds((32 * cfg.total, 512), BF), hbm))
    V = pltpu.VMEM
    mid_tot = V((2, 8, MID // 2), F32)
    scratch = dict(
        z1=V((RD, 2 * S, MID), F32),
        win1=V((M, 9 * MID), BF),
        h1s=V((2, S, MID), BF),
        h1r=V((2, S, MID), BF),
        z2=V((M, MID), F32),
        h2=V((M, MID), BF),
        z3=V((M, WIDE), F32),
        zs=V((M, WIDE), F32),
        y1=V((M, WIDE), BF),
        z4=V((M, MID), F32),
        h4=V((OD + 2, S, MID), BF),
        win4=V((M, 9 * MID), BF),
        z5=V((M, MID), F32),
        h5=V((M, MID), BF),
        z6=V((M, WIDE), F32),
        mixed_local=V((OD, S // 8, 8, WIDE), BF),
        du2=V((M // 16, 16, WIDE), F32),
        dz6=V((M, WIDE), BF),
        dh=V((M, MID), F32),
        d5=V((OD + 2, S, MID), BF),
        win5=V((M, 9 * MID), BF),
        dz4=V((M, MID), BF),
        du1=V((M // 16, 16, WIDE), F32),
        dzs=V((M, WIDE), BF),
        d2=V((OD + 1, S, MID), BF),
        d2l=V((OD + 1, S, MID), BF),
        stage0=V((32 * cfg.rows[MIXING], 512), BF),
        stage1=V((32 * cfg.rows[SHORTCUT], 512), BF),
        loc=mid_tot,
        locw=V((4, 8, WIDE // 4), F32),
        locw2=V((4, 16, WIDE // 4), F32),
        t1=mid_tot,
        t2=mid_tot,
        t3=V((4, 16, WIDE // 4), F32),
        t4=mid_tot,
        t5=mid_tot,
        t6=V((4, 8, WIDE // 4), F32),
        g1=mid_tot,
        g2=mid_tot,
        g3=V((4, 16, WIDE // 4), F32),
        g4=mid_tot,
        g5=mid_tot,
        g6=V((4, 8, WIDE // 4), F32),
        rc=V((2, 8, MID // 2), F32),
        rq=V((2, 2 * NB, 8, MID // 2), F32),
        rw=V((2, 4, 16, WIDE // 4), F32),
        wb=V((2, NB, 16, WIDE // 4), F32),
        wsend=pltpu.SemaphoreType.DMA((U, 7)),
        wrecv=pltpu.SemaphoreType.DMA((U, 7)),
        wloc=pltpu.SemaphoreType.DMA((7, 4)),
        ms=pltpu.SemaphoreType.DMA((3,)),
        mr=pltpu.SemaphoreType.DMA((3, 2)),
        ws=pltpu.SemaphoreType.DMA((4, 3)),
        wr=pltpu.SemaphoreType.DMA((4, 3)),
        hs=pltpu.SemaphoreType.DMA((2,)),
        hr=pltpu.SemaphoreType.DMA((2,)),
        es=pltpu.SemaphoreType.DMA((2, 2)),
        er=pltpu.SemaphoreType.DMA((2, 2)),
        xs=pltpu.SemaphoreType.DMA((3, OD)),
        xr=pltpu.SemaphoreType.DMA((3, OD)),
        xl=pltpu.SemaphoreType.DMA((OD,)),
        gs=pltpu.SemaphoreType.DMA((2,)),
        gi=pltpu.SemaphoreType.DMA((RD,)),
        rs=pltpu.SemaphoreType.DMA((7, 3, 5)),
        rr=pltpu.SemaphoreType.DMA((7, 3, 5)),
        fs=pltpu.SemaphoreType.DMA((7, 3)),
        fr=pltpu.SemaphoreType.DMA((7, 3)),
        fl=pltpu.SemaphoreType.DMA((7,)),
        x0=V((RD, 2 * S, CIN), BF),
        weave=V((4 * S, LANES), F32),
        ct=V((M, WIDE), BF),
        onehot=V((3, S, LANES), F32),
        active_slot=V((S, LANES), F32),
        pix_in=V((RD, 2 * S, LANES), F32),
        pix_out=V((M, LANES), F32),
        ld=pltpu.SemaphoreType.DMA((5,)),
        norm_values=V((3, 2, 4 * MID + 3 * WIDE), F32),
        gn_values=V((3, 2, 4 * MID + 3 * WIDE), F32),
    )
    scratch.update({"f" + str(name): V((n, 512), BF) for name, n in cfg.flat.items()})
    scratch.update({"l" + str(name): V((cfg.flat[name], 512), BF) for name in cfg.own_landing if cfg.reduce})
    scratch.update({"e" + str(w): V(shape, BF) for w, shape in final.items()})
    names = list(smem_args) + list(hbm_args) + list(outs) + list(scratch)
    smem = pl.BlockSpec(memory_space=pltpu.SMEM)
    res = pl.pallas_call(
        functools.partial(block_kernel, names, cfg),
        out_shape=[o[0] for o in outs.values()],
        in_specs=[smem] * len(smem_args) + [hbm] * len(hbm_args),
        out_specs=[o[1] for o in outs.values()],
        scratch_shapes=list(scratch.values()),
        compiler_params=pltpu.CompilerParams(
            collective_id=0, has_side_effects=True, vmem_limit_bytes=63 * 2**20
        ),
    )(*smem_args.values(), *hbm_args.values())
    return SimpleNamespace(**dict(zip(outs, res)))


def slot_layout(x, slots):
    images, rows, cols, channels = x.shape
    x = jnp.transpose(x, (1, 0, 2, 3)).reshape(rows, images * cols, channels)
    return jnp.pad(x, ((0, 0), (0, slots - images * cols), (0, 0)))


def per_device(
    features, w_reduce, w_spatial, w_expand, w_shortcut, w_squeeze, w_mixing, w_widen,
    norm_reduce, norm_spatial, norm_expand, norm_shortcut, norm_squeeze, norm_mixing, norm_widen,
    cotangent, resolution, active,
):
    images, rd, cols_in, cin = features.shape
    od = rd // 2
    nb = lax.axis_size("batch")
    cfg = plan(features, w_reduce, w_expand, nb)
    S, mid, wide = cfg.slots, cfg.mid, cfg.wide
    x = jnp.pad(features, ((0, 0), (0, 0), (0, 16 - cols_in), (0, 0)))
    x = x.reshape(images, rd, 8, 2, cin)
    x = jnp.transpose(x, (1, 3, 0, 2, 4)).reshape(rd, 2, images * 8, cin)
    x = jnp.pad(x, ((0, 0), (0, 0), (0, S - images * 8), (0, 0))).reshape(rd, 2 * S, cin)
    out_cols = cotangent.shape[2]
    ct = slot_layout(jnp.pad(cotangent, ((0, 0), (0, 0), (0, 8 - out_cols), (0, 0))), S)
    norms = jnp.concatenate(
        [
            jnp.transpose(n, (1, 0, 2))
            for n in (norm_reduce, norm_spatial, norm_squeeze, norm_mixing, norm_expand, norm_shortcut, norm_widen)
        ],
        axis=2,
    )
    res = run_blocks(
        cfg,
        dict(resolution=resolution, active=active),
        dict(
            features=x,
            norms=norms,
            cotangent=ct.reshape(od * S, wide),
            w0=w_reduce,
            w1=w_spatial.reshape(-1, mid),
            w2=w_expand,
            w3=w_shortcut,
            w4=w_squeeze,
            w5=w_mixing.reshape(-1, mid),
            w6=w_widen,
        ),
    )
    mixed = res.mixed[:, :, :out_cols]

    def unpack(g, name):
        b8, _, n, _ = g.shape
        if name in (SPATIAL, MIXING):
            k = n // 9
            return jnp.transpose(g.reshape(b8, 4, 9, k, 512), (2, 0, 1, 3, 4)).reshape(3, 3, b8 * 4 * k, 512)
        if name in (EXPAND, SHORTCUT, WIDEN):
            return jnp.transpose(g, (0, 2, 1, 3)).reshape(b8 * n, 2048)
        return g.reshape(b8 * 4 * n, 512)

    totals = []
    for name, n in cfg.rows.items():
        if cfg.reduce:
            g = getattr(res, "o" + str(name)).astype(F32)
            totals.append(g.reshape((3, 3) + g.shape[1:]) if g.ndim == 3 else g)
            continue
        at = cfg.offs[name]
        part = res.grads[32 * at : 32 * (at + n)].reshape(2, 8, 2, n, 512)
        part = unpack(jnp.transpose(part, (1, 2, 0, 3, 4)).reshape(8, 4, n, 512), name)
        dim = 2 if part.ndim == 4 else 0
        part = lax.psum_scatter(part, "batch", scatter_dimension=dim, tiled=True)
        totals.append(lax.psum(part, "rows").astype(F32))

    gn = [jnp.transpose(res.gn[:, :, at : at + n], (1, 0, 2)) for at, n in cfg.norm_columns]
    return (mixed, res.gin[:, :, :cols_in], *totals, gn[0], gn[1], gn[4], gn[5], gn[2], gn[3], gn[6])


def solution(mesh):
    w2, w4 = P("rows", None), P(None, None, "rows", None)
    o2, o4 = P("batch", None), P(None, None, "batch", None)
    return jax.shard_map(
        per_device,
        mesh=mesh,
        in_specs=(P("batch", "rows", None, None), w2, w4, w2, w2, w2, w4, w2)
        + (P(),) * 7
        + (P("batch", "rows", None, None), P(), P()),
        out_specs=(P("batch", None, None, None), P("batch", "rows", None, None), o2, o4, o2, o2, o2, o4, o2)
        + (P(),) * 7,
        check_vma=False,
    )
```

```python
import functools
from types import SimpleNamespace

import jax
import jax.numpy as jnp
from jax import lax
from jax.experimental import pallas as pl
from jax.experimental.pallas import tpu as pltpu
from jax.sharding import PartitionSpec as P

eps = 1e-05
MESH = pl.DeviceIdType.MESH
BF = jnp.bfloat16
F32 = jnp.float32
LANES = 128
REDUCE, SPATIAL, EXPAND, SHORTCUT, SQUEEZE, MIXING, WIDEN = range(7)
DX, DY, DN, DF = range(4)


def dot(a, b):
    return jnp.dot(a, b, preferred_element_type=F32)


def dot_t(a, b):
    return lax.dot_general(a, b, (((1,), (1,)), ((), ())), preferred_element_type=F32)


def dot_w(a, b):
    return lax.dot_general(a, b, (((0,), (0,)), ((), ())), preferred_element_type=F32)


def aligned(index, size):
    return pl.ds(pl.multiple_of(index * size, size), size)


def loop(count, body):
    def step(i, carry):
        body(i)
        return carry

    lax.fori_loop(0, count, step, 0)


def each(count, body):
    if count > 16:
        loop(count, body)
        return
    for i in range(count):
        body(i)


def silu_parts(u):
    s = jax.nn.sigmoid(u)
    return s, u * s


def slope(u):
    s = jax.nn.sigmoid(u)
    return s * (1.0 + u * (1.0 - s))


def block_kernel(names, cfg, *refs):
    R = SimpleNamespace(**dict(zip(names, refs)))
    S, RD, OD, NB = cfg.slots, cfg.in_rows, cfg.out_rows, cfg.batch
    MID, WIDE, CIN = cfg.mid, cfg.wide, cfg.cin
    M = OD * S
    b = lax.axis_index("batch")
    r = lax.axis_index("rows")
    core = lax.rem(r, 2)
    xb = lax.div(r, 2)
    core_peer = r + 1 - 2 * core
    x_row = lax.rem(r + 2, 4)
    diag = 3 - r
    half = lax.rem(b, 2)

    def flip(i, j):
        if isinstance(j, int):
            out = i
            for bit in range((2 * NB - 1).bit_length()):
                if j >> bit & 1:
                    out = out + (1 << bit) * (1 - 2 * lax.rem(lax.div(i, 1 << bit), 2))
            return out
        out = jnp.int32(0)
        bit = 1
        while bit < 2 * NB:
            p, q = lax.rem(lax.div(i, bit), 2), lax.rem(lax.div(j, bit), 2)
            out = out + bit * (p + q - 2 * p * q)
            bit *= 2
        return out

    me = b * 2 + xb

    def remote(src, dst, send, recv, dev):
        return pltpu.make_async_remote_copy(
            src_ref=src, dst_ref=dst, send_sem=send, recv_sem=recv, device_id=dev, device_id_type=MESH
        )

    def team(id2):
        return (lax.div(id2, 2), 2 * lax.rem(id2, 2) + core)

    units = cfg.units
    wsend, wrecv, wloc = R.wsend, R.wrecv, R.wloc
    near = lax.rem(lax.div(b, 2), 2)
    sides = ((half, (b + 1 - 2 * half, r)), (near, (b + 2 - 4 * near, r)))

    def wview(u, shard, at, fourths):
        w, k0, kn, _ = units[u]
        full = getattr(R, "f" + str(w))
        start = shard * (full.shape[0] // 4) + k0 + at * (kn // 4)
        return full.at[pl.ds(pl.multiple_of(start, 16), fourths * kn // 4)]

    def w_copy(u, i):
        mode = units[u][3]
        first, second = sides if mode == 1 else sides[::-1]
        quarter = x_row if i > 1 else r
        at, fourths, dev = 0, 4, (b, core_peer)
        if i == 1:
            dev = (b, x_row)
        if mode and i > 0:
            fourths = 2 if i > 4 else 1
            at = 2 * second[0] + first[0]
            if i == 3:
                dev = first[1]
            elif i == 4:
                at = at + 1 - 2 * first[0]
            elif i == 5:
                at, dev = 2 * second[0], second[1]
            elif i == 6:
                at = 2 - 2 * second[0]
        view = wview(u, quarter, at, fourths)
        return remote(view, view, wsend.at[u, i], wrecv.at[u, i], dev)

    def w_stages(u):
        return range(7) if units[u][3] else range(3)

    def w_local(w):
        src, full = getattr(R, "w" + str(w)), getattr(R, "f" + str(w))
        n, quarter = src.shape[0], full.shape[0] // 4
        return [
            pltpu.make_async_copy(
                src.at[:, pl.ds(512 * i, 512)],
                full.at[pl.ds(pl.multiple_of(r * quarter + i * n, 16), n)],
                wloc.at[w, i],
            )
            for i in range(src.shape[1] // 512)
        ]

    bar = pltpu.get_barrier_semaphore()
    for dev in ((b, core_peer), (b, diag)):
        pl.semaphore_signal(bar, inc=1, device_id=dev, device_id_type=MESH)

    def greet(j):
        pl.semaphore_signal(bar, inc=1, device_id=team(flip(me, j + 1)), device_id_type=MESH)

    loop(2 * NB - 1, greet)

    loaded = [w_local(w) for w in range(7)]
    for w in range(7):
        for c in loaded[w]:
            c.start()
        if w == 0:
            x0_load = pltpu.make_async_copy(R.features, R.x0, R.ld.at[0])
            x0_load.start()
    norm_load = pltpu.make_async_copy(R.norms, R.norm_values, R.ld.at[2])
    norm_load.start()
    ct_load = pltpu.make_async_copy(R.cotangent, R.ct, R.ld.at[1])
    ct_load.start()
    norm_reduce, norm_spatial, norm_squeeze, norm_mixing, norm_expand, norm_shortcut, norm_widen = [
        R.norm_values.at[:, :, pl.ds(at, width)] for at, width in cfg.norm_columns
    ]
    at_home = set()

    images = cfg.images
    column = lax.broadcasted_iota(jnp.int32, (8, LANES), 0).astype(F32)
    if 8 * images < S:
        tail = slice(8 * images, S)
        none = jnp.zeros((S - 8 * images, LANES), F32)
        R.active_slot[tail, :] = none
        for g in range(3):
            R.onehot[g, tail, :] = none
        for o in range(OD):
            R.pix_out[o * S + 8 * images : (o + 1) * S, :] = none
        for k in range(RD):
            for p in range(2):
                R.pix_in[k, p * S + 8 * images : (p + 1) * S, :] = none

    for i in range(images):
        group = R.resolution[b * images + i]
        side = (5 + group).astype(F32)
        here = slice(8 * i, 8 * i + 8)
        limit = jnp.zeros((8, LANES), F32)
        for g in range(3):
            is_g = jnp.where(group == g, 1.0, 0.0)
            R.onehot[g, here, :] = jnp.full((8, LANES), is_g, F32)
            limit = limit + is_g * R.active[g].astype(F32)
        R.active_slot[here, :] = limit
        for o in range(OD):
            inside = jnp.where((r * OD + o).astype(F32) < side, side, 0.0)
            R.pix_out[o * S + 8 * i : o * S + 8 * i + 8, :] = jnp.where(column < inside, 1.0, 0.0)
        for k in range(RD):
            inside = jnp.where((r * RD + k).astype(F32) < 2.0 * side, 2.0 * side, 0.0)
            for p in range(2):
                R.pix_in[k, p * S + 8 * i : p * S + 8 * i + 8, :] = jnp.where(2.0 * column + p < inside, 1.0, 0.0)

    pl.semaphore_wait(bar, 2 * NB + 1)

    def w_start(u):
        w = units[u][0]
        if w not in at_home:
            at_home.add(w)
            for c in loaded[w]:
                c.wait()
        w_copy(u, 1).start()
        w_copy(u, 0).start()

    def w_second(u):
        w_copy(u, 1).wait_recv()
        if units[u][3]:
            w_copy(u, 3).start()
        w_copy(u, 2).start()

    def w_third(u):
        if units[u][3]:
            w_copy(u, 3).wait_recv()
            w_copy(u, 5).start()
            w_copy(u, 4).start()

    def w_fourth(u):
        if units[u][3]:
            w_copy(u, 5).wait_recv()
            w_copy(u, 6).start()

    def w_ready(u):
        for i in w_stages(u)[::2]:
            w_copy(u, i).wait_recv()

    pumped = [0]
    lags = cfg.lags

    def pump(steps):
        for _ in range(steps):
            n = pumped[0]
            for lag, stage in zip(lags, (w_start, w_second, w_third, w_fourth)):
                if 0 <= n - lag < len(units):
                    stage(n - lag)
            pumped[0] = n + 1

    def need(name):
        last = max(u for u in range(len(units)) if units[u][0] == name)
        while pumped[0] < last + lags[3 if units[last][3] else 1] + 1:
            pump(1)
        for u in range(len(units)):
            if units[u][0] == name:
                w_ready(u)

    def mid_start(k):
        p = k % 2
        swap = remote(R.loc.at[1 - core], R.rc.at[p], R.ms.at[0], R.mr.at[0, p], (b, core_peer))
        swap.start()
        swap.wait_recv()
        R.rq[p, me] = R.loc[core] + R.rc[p]

        def send(j):
            to = team(flip(me, j + 1))
            remote(R.rq.at[p, me, pl.ds(0, 6)], R.rq.at[p, me, pl.ds(0, 6)], R.ms.at[1], R.mr.at[1, p], to).start()

        each(2 * NB - 1, send)
        swap.wait_send()

    def mid_finish(k, tot):
        p = k % 2
        rest = R.rq.at[p, pl.ds(0, 2 * NB - 1), pl.ds(0, 6)]
        every = remote(rest, rest, R.ms.at[1], R.mr.at[1, p], (b, x_row))
        every.wait_recv()
        total = R.rq[p, 0]
        for j in range(1, 2 * NB):
            total = total + R.rq[p, j]
        tot[core] = total
        back = remote(tot.at[core], tot.at[core], R.ms.at[2], R.mr.at[2, p], (b, core_peer))
        back.start()
        every.wait_send()
        back.wait()

    six = pl.ds(0, 6)

    def wide_start(k, loc):
        n = loc.shape[1]
        norms = pl.ds(0, n)
        rw, wb = R.rw.at[k % 2, :, norms], R.wb.at[k % 2, :, norms]
        rw[r] = loc[r]
        for to in (core_peer, x_row, diag):
            remote(loc.at[to, :, six], rw.at[r, :, six], R.ws.at[k, 0], R.wr.at[k, 0], (b, to)).start()
        three = remote(
            loc.at[pl.ds(0, 3), :, six], rw.at[pl.ds(0, 3), :, six], R.ws.at[k, 0], R.wr.at[k, 0], (b, core_peer)
        )
        three.wait_recv()
        wb[b] = rw[0] + rw[1] + (rw[2] + rw[3])

        def send(j):
            to = lax.rem(b + j + 1, NB)
            remote(wb.at[b, :, six], wb.at[b, :, six], R.ws.at[k, 1], R.wr.at[k, 1], (to, r)).start()

        each(NB - 1, send)
        three.wait_send()

    def wide_finish(k, tot):
        n = tot.shape[1]
        wb = R.wb.at[k % 2, :, pl.ds(0, n)]
        rest = wb.at[pl.ds(0, NB - 1), :, six]
        every = remote(rest, rest, R.ws.at[k, 1], R.wr.at[k, 1], (b, x_row))
        every.wait_recv()
        total = wb[0]
        for j in range(1, NB):
            total = total + wb[j]
        tot[r] = total
        for to in (core_peer, x_row, diag):
            remote(tot.at[r, :, six], tot.at[r, :, six], R.ws.at[k, 2], R.wr.at[k, 2], (b, to)).start()
        rest = tot.at[pl.ds(0, 3), :, six]
        three = remote(rest, rest, R.ws.at[k, 2], R.wr.at[k, 2], (b, core_peer))
        every.wait_send()
        three.wait()

    def mid_at(ref, j):
        return ref.at[lax.div(j, 2), :, aligned(lax.rem(j, 2), LANES)]

    def wide_at(ref, j, norm=0):
        return ref.at[lax.div(j, 4), norm, :, aligned(lax.rem(j, 4), LANES)]

    def group_rows(ref, row, values):
        for g in range(3):
            ref[row + g : row + g + 1, :] = jnp.sum(values * R.onehot[g], axis=0, keepdims=True)

    def blank(ref, row, rows):
        ref[row : row + rows, :] = jnp.zeros((rows, LANES), F32)

    def spread(rows3):
        return rows3[0] * R.onehot[0] + rows3[1] * R.onehot[1] + rows3[2] * R.onehot[2]

    def moments(sums, inv_n, row=0):
        means, invs = [], []
        for g in range(3):
            n = 1.0 / inv_n[g]
            mean = sums[row + g : row + g + 1, :] * n
            var = sums[row + 3 + g : row + 4 + g, :] * n - mean * mean
            means.append(mean)
            invs.append(lax.rsqrt(var + eps))
        return means, invs

    OUT = [cfg.members * (5.0 + g) * (5.0 + g) for g in range(3)]
    IN = [cfg.members * (10.0 + 2.0 * g) * (10.0 + 2.0 * g) for g in range(3)]

    def forward_terms(sums, params, cols, inv_n, row=0):
        means, invs = moments(sums, inv_n, row)
        scales = [invs[g] * params[g, 0:1, cols] for g in range(3)]
        shifts = [params[g, 1:2, cols] - means[g] * scales[g] for g in range(3)]
        return spread(scales), spread(shifts)

    def xhat_terms(sums, inv_n, row=0):
        means, invs = moments(sums, inv_n, row)
        return spread(invs), spread([-means[g] * invs[g] for g in range(3)])

    def backward_terms(sums, grads, params, cols, inv_n, row=0, g0=0, g1=3):
        means, invs = moments(sums, inv_n, row)
        fs, az, bz = [], [], []
        for g in range(3):
            n = 1.0 / inv_n[g]
            f = invs[g] * params[g, 0:1, cols]
            gain = grads[g0 + g : g0 + g + 1, :] * n * invs[g]
            bias = grads[g1 + g : g1 + g + 1, :] * n
            fs.append(f)
            bz.append(f * gain)
            az.append(f * (bias - means[g] * gain))
        return spread(fs), spread(az), spread(bz)

    def keep(j, ratio):
        lane = lax.broadcasted_iota(jnp.int32, (S, LANES), 1).astype(F32) + j * float(LANES)
        return jnp.where(lane < R.active_slot[...] * ratio, 1.0, 0.0)

    def out_rows(k):
        return slice(k * S, (k + 1) * S)

    def groups16(o):
        return slice(o * (S // 16), (o + 1) * (S // 16))

    def forward_stats(z, loc_at, row=0):
        def body(j):
            cols = aligned(j, LANES)
            s = jnp.zeros((S, LANES), F32)
            q = jnp.zeros((S, LANES), F32)
            for o in range(OD):
                v = z[out_rows(o), cols]
                m = v * R.pix_out[out_rows(o), :]
                s = s + m
                q = q + m * v
            st = loc_at(j)
            group_rows(st, row, s)
            group_rows(st, row + 3, q)
            blank(st, row + 6, 2)

        loop(z.shape[-1] // LANES, body)

    def rolled(v, by):
        return pltpu.roll(v, by % S, 0)

    def by_shard(t, j):
        return pl.ds(pl.multiple_of(j * (9 * LANES) + t * LANES, LANES), LANES)

    def by_tap(t, j):
        return pl.ds(pl.multiple_of(t * MID + j * LANES, LANES), LANES)

    def unit_windows(halo, win, rows, flipped):
        place = by_tap if flipped else by_shard

        def body(j):
            cols = aligned(j, LANES)
            for k in rows:
                v = halo[k, :, cols].astype(F32)
                moved = (rolled(v, 1).astype(BF), v.astype(BF), rolled(v, -1).astype(BF))
                for dr in range(3):
                    o = k - dr
                    if not 0 <= o < OD:
                        continue
                    for dc in range(3):
                        t = (2 - dr) * 3 + 2 - dc if flipped else dr * 3 + dc
                        win[out_rows(o), place(t, j)] = moved[dc]

        loop(MID // LANES, body)

    def edge_exchange(halo, k):
        up = remote(halo.at[1], halo.at[OD + 1], R.es.at[k, 0], R.er.at[k, 0], (b, jnp.maximum(r - 1, 0)))
        down = remote(halo.at[OD], halo.at[0], R.es.at[k, 1], R.er.at[k, 1], (b, jnp.minimum(r + 1, 3)))

        @pl.when(r > 0)
        def _():
            up.start()

        @pl.when(r < 3)
        def _():
            down.start()

        @pl.when(r == 0)
        def _():
            halo[0] = jnp.zeros(halo.shape[1:], BF)

        @pl.when(r == 3)
        def _():
            halo[OD + 1] = jnp.zeros(halo.shape[1:], BF)

        return up, down

    def edge_wait(pair):
        up, down = pair

        @pl.when(r < 3)
        def _():
            up.wait_recv()
            down.wait_send()

        @pl.when(r > 0)
        def _():
            down.wait_recv()
            up.wait_send()

    x0_load.wait()
    norm_load.wait()
    need(REDUCE)

    def z1_rows(k):
        def mask(j):
            cols = aligned(j, LANES)
            ch = keep(j, float(CIN // MID))
            for p in range(2):
                m = (ch * R.pix_in[k, out_rows(p), :]).astype(BF)
                R.x0[k, out_rows(p), cols] = R.x0[k, out_rows(p), cols] * m

        loop(CIN // LANES, mask)
        R.z1[k] = dot(R.x0[k], R.f0[...])

    loop(RD, z1_rows)

    def z1_stats(j):
        cols = aligned(j, LANES)
        s = jnp.zeros((S, LANES), F32)
        q = jnp.zeros((S, LANES), F32)
        for k in range(RD):
            for p in range(2):
                v = R.z1[k, out_rows(p), cols]
                m = v * R.pix_in[k, out_rows(p), :]
                s = s + m
                q = q + m * v
        st = mid_at(R.loc, j)
        group_rows(st, 0, s)
        group_rows(st, 3, q)
        blank(st, 6, 2)

    loop(MID // LANES, z1_stats)
    mid_start(0)
    pump(cfg.pumps[0])
    mid_finish(0, R.t1)

    last = RD - 1

    def h1_body(j):
        cols = aligned(j, LANES)
        sc, sh = forward_terms(mid_at(R.t1, j), norm_reduce, cols, IN)
        ch = keep(j, 1.0)
        for k in range(RD - 1, -1, -1):
            for p in range(2):
                u = R.z1[k, out_rows(p), cols] * sc + sh
                h = silu_parts(u)[1] * (ch * R.pix_in[k, out_rows(p), :])
                if k == last:
                    R.h1s[p, :, cols] = h.astype(BF)
                for dr in range(3):
                    o2 = k + 1 - dr
                    if o2 % 2 or not 0 <= o2 // 2 < OD:
                        continue
                    o = o2 // 2
                    taps = ((1, h),) if p == 0 else ((0, rolled(h, 1)), (2, h))
                    for dc, v in taps:
                        t = dr * 3 + dc
                        R.win1[out_rows(o), by_shard(t, j)] = v.astype(BF)

    loop(MID // LANES, h1_body)
    down = remote(R.h1s, R.h1r, R.hs.at[0], R.hr.at[0], (b, jnp.minimum(r + 1, 3)))

    @pl.when(r < 3)
    def _():
        down.start()

    pump(cfg.pumps[1])

    @pl.when(r > 0)
    def _():
        down.wait_recv()

    @pl.when(r == 0)
    def _():
        R.h1r[...] = jnp.zeros(R.h1r.shape, BF)

    def h1_halo(j):
        cols = aligned(j, LANES)
        even = R.h1r[0, :, cols]
        odd = R.h1r[1, :, cols]
        for dc, v in ((0, rolled(odd.astype(F32), 1).astype(BF)), (1, even), (2, odd)):
            R.win1[out_rows(0), by_shard(dc, j)] = v

    loop(MID // LANES, h1_halo)

    @pl.when(r < 3)
    def _():
        down.wait_send()

    need(SPATIAL)

    def conv(win, weight, z):
        def body(j):
            cols = aligned(j, 256)
            z[:, cols] = dot(win[...], weight[:, cols])

        loop(MID // 256, body)

    conv(R.win1, R.f1, R.z2)
    forward_stats(R.z2, lambda j: mid_at(R.loc, j))
    def piece(weight, shard, j):
        n = weight.shape[0] // 16
        return weight[pl.ds(pl.multiple_of((shard * 4 + j) * n, n), n), :]

    def block(weight, j):
        return jnp.concatenate([piece(weight, q, j) for q in range(4)], axis=0)

    mid_start(1)
    pump(cfg.pumps[2])
    need(SHORTCUT)

    def zs_body(j):
        cols = aligned(j, 512)
        w = block(R.f3, j)
        for o in range(OD):
            R.zs[out_rows(o), cols] = dot(R.x0[2 * o, 0:S, :], w)

    loop(WIDE // 512, zs_body)
    forward_stats(R.zs, lambda j: wide_at(R.locw2, j, 1), 0)
    mid_finish(1, R.t2)

    def activate(z, tot, params, dest):
        def body(j):
            cols = aligned(j, LANES)
            sc, sh = forward_terms(mid_at(tot, j), params, cols, OUT)
            ch = keep(j, 1.0)
            for o in range(OD):
                u = z[out_rows(o), cols] * sc + sh
                dest(o, cols, (silu_parts(u)[1] * (ch * R.pix_out[out_rows(o), :])).astype(BF))

        loop(MID // LANES, body)

    def to_h2(o, cols, v):
        R.h2[out_rows(o), cols] = v

    activate(R.z2, R.t2, norm_spatial, to_h2)
    need(EXPAND)

    def expand_to(h, weight, z):
        def body(j):
            z[:, aligned(j, 512)] = dot(h[...], block(weight, j))

        loop(WIDE // 512, body)

    expand_to(R.h2, R.f2, R.z3)
    forward_stats(R.z3, lambda j: wide_at(R.locw2, j), 0)
    wide_start(0, R.locw2)
    pump(cfg.pumps[3])
    wide_finish(0, R.t3)

    def u1_terms(j):
        cols = aligned(j, LANES)
        tot = wide_at(R.t3, j)
        sc3, sh3 = forward_terms(tot, norm_expand, cols, OUT, 0)
        scs, shs = forward_terms(wide_at(R.t3, j, 1), norm_shortcut, cols, OUT, 0)
        shift = sh3 + shs

        def u1(o):
            return R.z3[out_rows(o), cols] * sc3 + R.zs[out_rows(o), cols] * scs + shift

        return u1

    def y1_body(j):
        cols = aligned(j, LANES)
        u1 = u1_terms(j)
        ch = keep(j, float(WIDE // MID))
        for o in range(OD):
            y = silu_parts(u1(o))[1] * (ch * R.pix_out[out_rows(o), :])
            R.y1[out_rows(o), cols] = y.astype(BF)

    loop(WIDE // LANES, y1_body)
    need(SQUEEZE)

    def squeeze_body(j):
        cols = aligned(j, 256)
        R.z4[:, cols] = dot(R.y1[...], R.f4[:, cols])

    loop(MID // 256, squeeze_body)
    forward_stats(R.z4, lambda j: mid_at(R.loc, j))
    mid_start(2)
    pump(cfg.pumps[4])
    mid_finish(2, R.t4)

    def to_h4(o, cols, v):
        R.h4[o + 1, :, cols] = v

    activate(R.z4, R.t4, norm_squeeze, to_h4)
    pair = edge_exchange(R.h4, 0)
    pump(cfg.pumps[5])
    unit_windows(R.h4, R.win4, range(1, OD + 1), False)
    edge_wait(pair)
    unit_windows(R.h4, R.win4, (0, OD + 1), False)
    need(MIXING)
    conv(R.win4, R.f5, R.z5)
    forward_stats(R.z5, lambda j: mid_at(R.loc, j))
    mid_start(3)
    pump(cfg.pumps[6])
    mid_finish(3, R.t5)

    def to_h5(o, cols, v):
        R.h5[out_rows(o), cols] = v

    activate(R.z5, R.t5, norm_mixing, to_h5)
    need(WIDEN)
    expand_to(R.h5, R.f6, R.z6)
    forward_stats(R.z6, lambda j: wide_at(R.locw, j))
    wide_start(1, R.locw)
    wide_finish(1, R.t6)
    for u in range(len(units)):
        for i in w_stages(u):
            w_copy(u, i).wait_send()

    def u2_body(j):
        cols = aligned(j, LANES)
        tot = wide_at(R.t6, j)
        sc, sh = forward_terms(tot, norm_widen, cols, OUT)
        xa, xs = xhat_terms(tot, OUT)
        ch = keep(j, float(WIDE // MID))
        g0 = jnp.zeros((S, LANES), F32)
        g1 = jnp.zeros((S, LANES), F32)
        for o in range(OD):
            z = R.z6[out_rows(o), cols]
            u = z * sc + sh + R.y1[out_rows(o), cols].astype(F32)
            mask = ch * R.pix_out[out_rows(o), :]
            s, su = silu_parts(u)
            R.mixed_local[o, :, :, cols] = (su * mask).reshape(S // 8, 8, LANES).astype(BF)
            d = R.ct[out_rows(o), cols].astype(F32) * mask * (s * (1.0 + u * (1.0 - s)))
            R.du2[groups16(o), :, cols] = d.reshape(S // 16, 16, LANES)
            g0 = g0 + d * (z * xa + xs)
            g1 = g1 + d
        st = wide_at(R.locw, j)
        group_rows(st, 0, g0)
        group_rows(st, 3, g1)
        blank(st, 6, 2)

    ct_load.wait()
    loop(WIDE // LANES, u2_body)
    wide_start(2, R.locw)
    def mixed_copy(i, o):
        row = (x_row if i == 2 else r) * OD + o
        dst = R.mixed.at[:, row]
        src = dst if i == 2 else R.mixed_local.at[o, pl.ds(0, images)]
        if i == 3:
            return pltpu.make_async_copy(src, dst, R.xl.at[o])
        return remote(src, dst, R.xs.at[i, o], R.xr.at[i, o], (b, x_row if i == 1 else core_peer))

    for o in range(OD):
        for i in (0, 3):
            mixed_copy(i, o).start()
    wide_finish(2, R.g6)

    def widen_back(j):
        cols = aligned(j, LANES)
        f, a, bz = backward_terms(wide_at(R.t6, j), wide_at(R.g6, j), norm_widen, cols, OUT)
        for o in range(OD):
            d = f * R.du2[groups16(o), :, cols].reshape(S, LANES) - a - R.z6[out_rows(o), cols] * bz
            R.dz6[out_rows(o), cols] = (d * R.pix_out[out_rows(o), :]).astype(BF)

    loop(WIDE // LANES, widen_back)

    mine = {DY: lax.rem(b, 2), DN: lax.rem(lax.div(b, 2), 2), DF: lax.div(b, 4), DX: xb}
    turn = [1]
    begun = {}

    def partner(d):
        other = 1 - 2 * mine[d]
        if d == DX:
            return (b, x_row)
        return (b + other * {DY: 1, DN: 2, DF: 4}[d], r)

    def put(stage, w, core_of, bits, start, value):
        for n0, np_, order in cfg.parts[w]:
            lo, hi = max(start, n0), min(start + value.shape[0], n0 + np_)
            if lo >= hi:
                continue
            idx = 0
            for d in order:
                idx = 2 * idx + bits[d]
            row = 32 * n0 + (core_of * 16 + idx) * np_ + lo - n0
            stage[pl.ds(row if isinstance(row, int) else pl.multiple_of(row, 16), hi - lo), :] = value[
                lo - start : hi - start
            ].astype(BF)

    def batch_bits(y, zn, zf, x):
        return {DY: y, DN: zn, DF: zf, DX: x}

    def staged(w, fill):
        i = turn[0] % 2
        turn[0] += 1
        stage = (R.stage0, R.stage1)[i]
        n = cfg.rows[w]
        assert 32 * n <= stage.shape[0], w
        if cfg.reduce:
            fill(stage)
            begun[w] = (stage, [0] * len(cfg.parts[w]), [0])
            for p in range(len(cfg.parts[w])):
                rs_core(w, p).start()
            return
        if i in begun:
            begun[i].wait()
        fill(stage)
        off = 32 * cfg.offs[w]
        begun[i] = pltpu.make_async_copy(
            stage.at[pl.ds(0, 32 * n)], R.grads.at[pl.ds(off, 32 * n)], R.gs.at[i]
        )
        begun[i].start()

    def land_of(w):
        return getattr(R, ("l" if w in cfg.own_landing else "f") + str(w))

    def rs_core(w, p):
        n0, np_, order = cfg.parts[w][p]
        stage = begun[w][0]
        src = stage.at[pl.ds(pl.multiple_of(32 * n0 + (1 - core) * 16 * np_, 16), 16 * np_)]
        dst = land_of(w).at[pl.ds(32 * n0, 16 * np_)]
        return remote(src, dst, R.rs.at[w, p, 0], R.rr.at[w, p, 0], (b, core_peer))

    def rs_kept(w, p, step):
        n0, np_, order = cfg.parts[w][p]
        at, size = 0, 16 * np_
        for d in order[:step]:
            size = size // 2
            at = at + mine[d] * size
        return at, size

    def rs_link(w, p, step):
        n0, np_, order = cfg.parts[w][p]
        at, size = rs_kept(w, p, step - 1)
        size = size // 2
        d = order[step - 1]
        src = land_of(w).at[pl.ds(pl.multiple_of(32 * n0 + at + (1 - mine[d]) * size, 16), size)]
        dst = land_of(w).at[pl.ds(32 * n0 + 32 * np_ - 2 * size, size)]
        i = w
        return remote(src, dst, R.rs.at[i, p, step], R.rr.at[i, p, step], partner(d))

    def final(w):
        return getattr(R, "e" + str(w))

    def rs_add(w, p, step):
        n0, np_, order = cfg.parts[w][p]
        land = land_of(w)
        at, size = rs_kept(w, p, step)
        if step == 0:
            other, start = begun[w][0], 32 * n0 + core * 16 * np_
        else:
            other, start = land, 32 * n0 + 32 * np_ - 2 * size
        last_step = step == 4

        def body(i):
            rows = pl.ds(pl.multiple_of(32 * n0 + at + i * np_, 16), np_)
            v = land[rows, :] + other[pl.ds(pl.multiple_of(start + i * np_, 16), np_), :]
            if not last_step:
                land[rows, :] = v
            elif w in (SPATIAL, MIXING):
                k = cfg.rows[w] // 9
                final(w)[n0 // k : (n0 + np_) // k] = v.reshape(np_ // k, k, 512)
            else:
                final(w)[n0 : n0 + np_, :] = v

        if size == np_:
            body(0)
        else:
            loop(size // np_, body)

    def home(w, row):
        out, n = getattr(R, "o" + str(w)), cfg.rows[w]
        if w in (SPATIAL, MIXING):
            return out.at[:, aligned(row, n // 9)]
        if w in (EXPAND, SHORTCUT, WIDEN):
            return out.at[:, aligned(row, 512)]
        return out.at[aligned(row, n)]

    def fin_copy(w, i):
        dst = home(w, x_row if i == 2 else r)
        src = dst if i == 2 else final(w)
        if i == 3:
            return pltpu.make_async_copy(src, dst, R.fl.at[w])
        return remote(src, dst, R.fs.at[w, i], R.fr.at[w, i], (b, x_row if i == 1 else core_peer))

    def rs_step(*kernels, parts=(0, 1, 2)):
        if not cfg.reduce:
            return
        for w in kernels:
            stage, steps, ends = begun[w]
            if ends[0] == 1:
                fin_copy(w, 1).wait_recv()
                fin_copy(w, 2).start()
                ends[0] = 2
            for p in parts:
                if p >= len(steps) or steps[p] > 4:
                    continue
                step = steps[p]
                c = rs_core(w, p) if step == 0 else rs_link(w, p, step)
                c.wait_recv()
                rs_add(w, p, step)
                if step < 4:
                    rs_link(w, p, step + 1).start()
                c.wait_send()
                steps[p] = step + 1
            if ends[0] == 0 and min(steps) == 5:
                for i in (1, 0, 3):
                    fin_copy(w, i).start()
                ends[0] = 1

    def rs_round():
        if cfg.reduce:
            rs_step(*[w for w in reversed(list(begun)) if begun[w][2][0] < 2])

    def rs_end():
        if not cfg.reduce:
            for copy in begun.values():
                copy.wait()
            return
        while any(begun[w][2][0] < 2 for w in begun):
            rs_round()
        for w in cfg.rows:
            fin_copy(w, 0).wait()
            fin_copy(w, 1).wait_send()
            fin_copy(w, 2).wait()
            fin_copy(w, 3).wait()

    def fill_out(w, act, dz):
        def fill(stage):
            def body(j):
                res = dot_w(act(), dz[:, aligned(j, 512)])
                n = res.shape[0] // 8
                for i in range(8):
                    bits = batch_bits(i % 2, i // 2 % 2, i // 4, lax.div(j, 2))
                    put(stage, w, lax.rem(j, 2), bits, 0, res[i * n : (i + 1) * n])

            loop(WIDE // 512, body)

        return fill

    def fill_conv(w, win, dz):
        def fill(stage):
            n = MID // 32

            def body(q):
                for t0 in range(0, 9, 3):
                    cols = pl.ds(pl.multiple_of(q * (9 * LANES) + t0 * LANES, LANES), 3 * LANES)
                    res = dot_w(win[:, cols], dz())
                    for t in range(3):
                        for i in range(8):
                            bits = batch_bits(i // 4, lax.rem(q, 2), lax.div(q, 2), i // 2 % 2)
                            at = t * LANES + i * n
                            put(stage, w, i % 2, bits, (t0 + t) * n, res[at : at + n])

            loop(4, body)

        return fill

    def mid_back_sums(dh, z, tot, params):
        def body(j):
            cols = aligned(j, LANES)
            sums = mid_at(tot, j)
            sc, sh = forward_terms(sums, params, cols, OUT)
            xa, xs = xhat_terms(sums, OUT)
            ch = keep(j, 1.0)
            g0 = jnp.zeros((S, LANES), F32)
            g1 = jnp.zeros((S, LANES), F32)
            for o in range(OD):
                v = z[out_rows(o), cols]
                d = dh[out_rows(o), cols] * (ch * R.pix_out[out_rows(o), :]) * slope(v * sc + sh)
                dh[out_rows(o), cols] = d
                g0 = g0 + d * (v * xa + xs)
                g1 = g1 + d
            st = mid_at(R.loc, j)
            group_rows(st, 0, g0)
            group_rows(st, 3, g1)
            blank(st, 6, 2)

        loop(MID // LANES, body)

    def mid_back_apply(dh, z, tot, grads, params, dest):
        def body(j):
            cols = aligned(j, LANES)
            f, a, bz = backward_terms(mid_at(tot, j), mid_at(grads, j), params, cols, OUT)
            for o in range(OD):
                d = f * dh[out_rows(o), cols] - a - z[out_rows(o), cols] * bz
                dest(o, cols, (d * R.pix_out[out_rows(o), :]).astype(BF))

        loop(MID // LANES, body)

    def reduce_back(dz, weight, dh):
        def body(i):
            acc = None
            for j in range(4):
                w = jnp.concatenate([piece(weight, 2 * i + q, j) for q in range(2)], axis=0)
                v = dot_t(dz[:, j * 512 : (j + 1) * 512], w)
                acc = v if acc is None else acc + v
            dh[:, aligned(i, MID // 2)] = acc

        loop(2, body)

    def tap_rows(weight, i, t):
        n = MID // 4
        return jnp.concatenate(
            [weight[pl.ds(pl.multiple_of(((2 * i + q) * 9 + t) * n, n), n), :] for q in range(2)], axis=0
        )

    reduce_back(R.dz6, R.f6, R.dh)
    mid_back_sums(R.dh, R.z5, R.t5, norm_mixing)
    mid_start(4)
    mixed_copy(1, 0).start()
    staged(WIDEN, fill_out(WIDEN, lambda: R.h5[...], R.dz6))
    mid_finish(4, R.g5)

    def to_d5(o, cols, v):
        R.d5[o + 1, :, cols] = v

    mid_back_apply(R.dh, R.z5, R.t5, R.g5, norm_mixing, to_d5)
    pair = edge_exchange(R.d5, 1)
    rs_step(WIDEN)
    unit_windows(R.d5, R.win5, range(1, OD + 1), True)
    edge_wait(pair)
    unit_windows(R.d5, R.win5, (0, OD + 1), True)

    def conv_back(j):
        acc = None
        for t in range(9):
            v = dot_t(R.win5[:, t * MID : (t + 1) * MID], tap_rows(R.f5, j, t))
            acc = v if acc is None else acc + v
        R.dh[:, aligned(j, MID // 2)] = acc

    loop(2, conv_back)
    mid_back_sums(R.dh, R.z4, R.t4, norm_squeeze)
    mid_start(5)
    for o in range(1, OD):
        mixed_copy(1, o).start()
    rs_step(WIDEN)
    staged(MIXING, fill_conv(MIXING, R.win4, lambda: R.d5[1 : OD + 1].reshape(M, MID)))
    mid_finish(5, R.g4)

    def to_d4(o, cols, v):
        R.dz4[out_rows(o), cols] = v

    mid_back_apply(R.dh, R.z4, R.t4, R.g4, norm_squeeze, to_d4)

    def squeeze_back(j):
        n = WIDE // 4
        R.du1[:, :, aligned(j, n)] = dot_t(R.dz4[...], R.f4[aligned(j, n), :]).reshape(M // 16, 16, n)

    loop(4, squeeze_back)

    def u1_back(j):
        cols = aligned(j, LANES)
        u1 = u1_terms(j)
        tot = wide_at(R.t3, j)
        xa3, xs3 = xhat_terms(tot, OUT, 0)
        xas, xss = xhat_terms(wide_at(R.t3, j, 1), OUT, 0)
        ch = keep(j, float(WIDE // MID))
        g0 = jnp.zeros((S, LANES), F32)
        g1 = jnp.zeros((S, LANES), F32)
        g2 = jnp.zeros((S, LANES), F32)
        for o in range(OD):
            rows = out_rows(o)
            d = (R.du1[groups16(o), :, cols] + R.du2[groups16(o), :, cols]).reshape(S, LANES) * (ch * R.pix_out[rows, :]) * slope(u1(o))
            R.du1[groups16(o), :, cols] = d.reshape(S // 16, 16, LANES)
            g0 = g0 + d * (R.z3[rows, cols] * xa3 + xs3)
            g2 = g2 + d * (R.zs[rows, cols] * xas + xss)
            g1 = g1 + d
        st = wide_at(R.locw2, j)
        group_rows(st, 0, g0)
        group_rows(st, 3, g1)
        blank(st, 6, 2)
        st = wide_at(R.locw2, j, 1)
        group_rows(st, 0, g2)
        group_rows(st, 3, g1)
        blank(st, 6, 2)

    loop(WIDE // LANES, u1_back)
    wide_start(3, R.locw2)

    def fill_squeeze(stage):
        def body(j):
            res = dot_w(R.y1[:, aligned(j, WIDE // 8)], R.dz4[...])
            n = res.shape[0] // 4
            bits = (lax.rem(j, 2), lax.rem(lax.div(j, 2), 2), lax.div(j, 4))
            for i in range(4):
                put(stage, SQUEEZE, i % 2, batch_bits(*bits, i // 2), 0, res[i * n : (i + 1) * n])

        loop(8, body)

    rs_step(MIXING, WIDEN)
    staged(SQUEEZE, fill_squeeze)
    wide_finish(3, R.g3)

    for o in range(OD):
        mixed_copy(1, o).wait_recv()
        mixed_copy(2, o).start()

    def u1_apply(j):
        cols = aligned(j, LANES)
        tot, grads = wide_at(R.t3, j), wide_at(R.g3, j)
        f3, a3, b3 = backward_terms(tot, grads, norm_expand, cols, OUT, 0, 0, 3)
        fs, as_, bs = backward_terms(wide_at(R.t3, j, 1), wide_at(R.g3, j, 1), norm_shortcut, cols, OUT)
        for o in range(OD):
            rows = out_rows(o)
            d = R.du1[groups16(o), :, cols].reshape(S, LANES)
            pix = R.pix_out[rows, :]
            R.dz6[rows, cols] = ((f3 * d - a3 - R.z3[rows, cols] * b3) * pix).astype(BF)
            R.dzs[rows, cols] = ((fs * d - as_ - R.zs[rows, cols] * bs) * pix).astype(BF)

    loop(WIDE // LANES, u1_apply)
    reduce_back(R.dz6, R.f2, R.dh)
    mid_back_sums(R.dh, R.z2, R.t2, norm_spatial)
    mid_start(6)
    rs_step(SQUEEZE, MIXING, WIDEN)
    staged(EXPAND, fill_out(EXPAND, lambda: R.h2[...], R.dz6))

    def even_rows():
        return jnp.concatenate([R.x0[2 * o, 0:S, :] for o in range(OD)], axis=0)

    staged(SHORTCUT, fill_out(SHORTCUT, even_rows, R.dzs))
    mid_finish(6, R.g2)

    def to_d2(o, cols, v):
        R.d2[o, :, cols] = v

    mid_back_apply(R.dh, R.z2, R.t2, R.g2, norm_spatial, to_d2)
    up = remote(R.d2.at[0], R.d2.at[OD], R.hs.at[1], R.hr.at[1], (b, jnp.maximum(r - 1, 0)))

    @pl.when(r > 0)
    def _():
        up.start()

    @pl.when(r == 3)
    def _():
        R.d2[OD] = jnp.zeros(R.d2.shape[1:], BF)

    rs_step(EXPAND, SHORTCUT, MIXING, SQUEEZE, WIDEN)
    staged(SPATIAL, fill_conv(SPATIAL, R.win1, lambda: R.d2[0:OD].reshape(M, MID)))

    @pl.when(r < 3)
    def _():
        up.wait_recv()

    @pl.when(r > 0)
    def _():
        up.wait_send()

    def dh1_at(k, j, width):
        return pl.ds(pl.multiple_of(k * MID + j * width, LANES), width)

    def d2_left(j):
        cols = aligned(j, LANES)
        for k in range(OD + 1):
            R.d2l[k, :, cols] = rolled(R.d2[k, :, cols].astype(F32), -1).astype(BF)

    loop(MID // LANES, d2_left)

    def spatial_back(j):
        here, left = R.d2[0:OD].reshape(M, MID), R.d2l[0:OD].reshape(M, MID)
        below, below_left = R.d2[1 : OD + 1].reshape(M, MID), R.d2l[1 : OD + 1].reshape(M, MID)

        def w(dr, dc):
            return tap_rows(R.f1, j, dr * 3 + dc)

        cols = aligned(j, MID // 2)
        parts = (
            ((here, 1, 1),),
            ((here, 1, 2), (left, 1, 0)),
            ((here, 2, 1), (below, 0, 1)),
            ((here, 2, 2), (left, 2, 0), (below, 0, 2), (below_left, 0, 0)),
        )
        for i, terms in enumerate(parts):
            rp, cp = divmod(i, 2)
            acc = None
            for v, dr, dc in terms:
                y = dot_t(v, w(dr, dc))
                acc = y if acc is None else acc + y
            for o in range(OD):
                R.zs[out_rows(cp), dh1_at(2 * o + rp, j, MID // 2)] = acc[out_rows(o)]

    loop(2, spatial_back)

    def h1_back(j):
        cols = aligned(j, LANES)
        sums = mid_at(R.t1, j)
        sc, sh = forward_terms(sums, norm_reduce, cols, IN)
        xa, xs = xhat_terms(sums, IN)
        ch = keep(j, 1.0)
        g0 = jnp.zeros((S, LANES), F32)
        g1 = jnp.zeros((S, LANES), F32)
        for k in range(RD):
            for p in range(2):
                rows = out_rows(p)
                v = R.z1[k, rows, cols]
                d = R.zs[rows, dh1_at(k, j, LANES)] * (ch * R.pix_in[k, rows, :]) * slope(v * sc + sh)
                R.zs[rows, dh1_at(k, j, LANES)] = d
                g0 = g0 + d * (v * xa + xs)
                g1 = g1 + d
        st = mid_at(R.loc, j)
        group_rows(st, 0, g0)
        group_rows(st, 3, g1)
        blank(st, 6, 2)

    loop(MID // LANES, h1_back)
    mid_start(7)
    rs_step(SPATIAL, SQUEEZE, MIXING, EXPAND, SHORTCUT)

    def norm_grads(i, src, gains, biases):
        at, width = cfg.norm_columns[i]
        parts, _, n = src.shape
        for h in range(parts):
            cols = slice(at + h * n, at + (h + 1) * n)
            for g in range(3):
                R.gn_values[g, 0:1, cols] = src[h, gains + g : gains + g + 1, :]
                R.gn_values[g, 1:2, cols] = src[h, biases + g : biases + g + 1, :]

    def gn_copy(first):
        at = MID if first else 0
        n = R.gn.shape[2] - MID if first else MID
        cols = pl.ds(at, n)
        return pltpu.make_async_copy(R.gn_values.at[:, :, cols], R.gn.at[:, :, cols], R.ld.at[3 + first])

    def short_back(j):
        acc = None
        for i in range(4):
            v = dot_t(R.dzs[:, i * 512 : (i + 1) * 512], piece(R.f3, j, i))
            acc = v if acc is None else acc + v
        R.z6[:, aligned(j, CIN // 4)] = acc

    loop(4, short_back)
    for i, (src, gains) in enumerate(((R.g2, 0), (R.g4, 0), (R.g5, 0), (R.g3.at[:, 0], 0), (R.g3.at[:, 1], 0), (R.g6.at[:, 0], 0))):
        norm_grads(i + 1, src, gains, 3)
    gn_copies = [gn_copy(1)]
    gn_copies[0].start()
    mid_finish(7, R.g1)

    def h1_apply(j):
        cols = aligned(j, LANES)
        f, a, bz = backward_terms(mid_at(R.t1, j), mid_at(R.g1, j), norm_reduce, cols, IN)
        for k in range(RD):
            for p in range(2):
                rows = out_rows(p)
                d = f * R.zs[rows, dh1_at(k, j, LANES)] - a - R.z1[k, rows, cols] * bz
                R.y1[rows, dh1_at(k, j, LANES)] = (d * R.pix_in[k, rows, :]).astype(BF)

    loop(MID // LANES, h1_apply)

    def dz1(k):
        return R.y1[:, k * MID : (k + 1) * MID]

    def fill_reduce(stage):
        n = CIN // 32

        def body(j):
            act = R.x0[:, :, aligned(j, 256)].reshape(RD * 2 * S, 256)
            res = dot_w(act, jnp.concatenate([dz1(k) for k in range(RD)], axis=0))
            for i in range(8):
                bits = batch_bits(i // 4, lax.rem(j, 2), lax.div(j, 2), i // 2 % 2)
                put(stage, REDUCE, i % 2, bits, 0, res[i * n : (i + 1) * n])

        loop(4, body)

    staged(REDUCE, fill_reduce)
    rs_round()

    def input_grad(j):
        cols = aligned(j, CIN // 4)
        w = R.f0[aligned(j, CIN // 4), :]
        ch = jnp.concatenate(
            [keep(j * (CIN // 4 // LANES) + i, float(CIN // MID)) for i in range(CIN // 4 // LANES)],
            axis=1,
        )
        for k in range(RD):
            y = dot_t(dz1(k), w)
            for c in range(0, CIN // 4, LANES):
                base = c // LANES * 2 * S
                for p in range(2):
                    v = y[out_rows(p), c : c + LANES]
                    if p == 0 and k % 2 == 0:
                        v = v + R.z6[out_rows(k // 2), pl.ds(pl.multiple_of(j * (CIN // 4) + c, LANES), LANES)]
                    v = v * (ch[:, c : c + LANES] * R.pix_in[k, out_rows(p), :])
                    R.weave[pl.ds(base + p, S, stride=2), :] = v
                at = pl.ds(pl.multiple_of(k % 2 * CIN + j * (CIN // 4) + c, LANES), LANES)
                woven = R.weave[base : base + 2 * S, :]
                (R.du2, R.du1)[k // 2][:, :, at] = woven.reshape(M // 16, 16, LANES)

    for j in range(4):
        input_grad(j)
        if j < 3:
            rs_round()
    gin_copies = [
        pltpu.make_async_copy(
            (R.du2, R.du1)[k // 2].at[pl.ds(0, images), :, pl.ds(k % 2 * CIN, CIN)],
            R.gin.at[:, k],
            R.gi.at[k],
        )
        for k in range(RD)
    ]
    for c in gin_copies:
        c.start()
    rs_end()

    norm_grads(0, R.g1, 0, 3)
    gn_copies.append(gn_copy(0))
    gn_copies[1].start()

    for o in range(OD):
        mixed_copy(0, o).wait()
        mixed_copy(1, o).wait_send()
        mixed_copy(2, o).wait()
        mixed_copy(3, o).wait()
    for c in gin_copies + gn_copies:
        c.wait()


def plan(features, w_reduce, w_expand, batch):
    images, rd, _, cin = features.shape
    mid, wide = w_reduce.shape[1], w_expand.shape[1]
    cfg = SimpleNamespace(
        images=images,
        members=images * batch // 3,
        slots=-(-images * 8 // 16) * 16, in_rows=rd, out_rows=rd // 2, batch=batch, mid=mid, wide=wide, cin=cin
    )
    flat = {
        REDUCE: cin,
        SPATIAL: 9 * mid,
        EXPAND: mid * wide // 512,
        SHORTCUT: cin * wide // 512,
        SQUEEZE: wide,
        MIXING: 9 * mid,
        WIDEN: mid * wide // 512,
    }
    pieces = {SPATIAL: 3, MIXING: 3, SHORTCUT: 2}
    widths = (mid,) * 4 + (wide,) * 3
    cfg.norm_columns = [(sum(widths[:i]), n) for i, n in enumerate(widths)]
    cfg.units = []
    for name in (REDUCE, SPATIAL, SHORTCUT, EXPAND, SQUEEZE, MIXING, WIDEN):
        n, k = flat[name], pieces.get(name, 1)
        for i in range(k):
            mode = 1 + len(cfg.units) % 2 if name else 0
            cfg.units.append((name, i * n // 4 // k, n // 4 // k, mode))
    cfg.lags = (0, 2, 4, 6)
    cfg.pumps = (3, 1, 2, 2, 2, 2, 3)
    cfg.flat = flat
    cfg.rows = {name: n // 32 for name, n in flat.items()}
    cfg.reduce = batch == 8
    orders = ((DX, DY, DN, DF), (DY, DN, DX, DF), (DN, DX, DY, DF))
    thirds = {WIDEN: 1, SQUEEZE: 0, EXPAND: 2}
    cfg.parts = {}
    for name, n in cfg.rows.items():
        if not cfg.reduce:
            cfg.parts[name] = [(0, n, (DF, DN, DY, DX))]
            continue
        tiles = [n // 16 // 3] * 3
        for i in range(n // 16 - sum(tiles)):
            tiles[(thirds.get(name, 0) + i) % 3] += 1
        cfg.parts[name], n0 = [], 0
        for tile, order in zip(tiles, orders):
            if tile:
                cfg.parts[name].append((n0, 16 * tile, order))
                n0 += 16 * tile
    cfg.own_landing = (REDUCE, SPATIAL, SHORTCUT)
    cfg.offs, total = {}, 0
    for name, n in cfg.rows.items():
        cfg.offs[name] = total
        total += n
    cfg.total = total
    return cfg


def run_blocks(cfg, smem_args, hbm_args):
    S, RD, OD, NB = cfg.slots, cfg.in_rows, cfg.out_rows, cfg.batch
    MID, WIDE, CIN = cfg.mid, cfg.wide, cfg.cin
    M = OD * S
    U = len(cfg.units)
    hbm = pl.BlockSpec(memory_space=pl.ANY)
    sds = jax.ShapeDtypeStruct
    outs = dict(
        mixed=(sds((cfg.images, 4 * OD, 8, WIDE), BF), hbm),
        gin=(sds((cfg.images, RD, 16, CIN), F32), hbm),
        gn=(sds((3, 2, 4 * MID + 3 * WIDE), F32), hbm),
    )
    final = {}
    if cfg.reduce:
        for w, n in cfg.rows.items():
            final[w] = (9, n // 9, 512) if w in (SPATIAL, MIXING) else (n, 512)
            shape = (n, 2048) if w in (EXPAND, SHORTCUT, WIDEN) else final[w][:-2] + (4 * final[w][-2], 512)
            outs["o" + str(w)] = (sds(shape, BF), hbm)
    else:
        outs.update(grads=(sds((32 * cfg.total, 512), BF), hbm))
    V = pltpu.VMEM
    mid_tot = V((2, 8, MID // 2), F32)
    scratch = dict(
        z1=V((RD, 2 * S, MID), F32),
        win1=V((M, 9 * MID), BF),
        h1s=V((2, S, MID), BF),
        h1r=V((2, S, MID), BF),
        z2=V((M, MID), F32),
        h2=V((M, MID), BF),
        z3=V((M, WIDE), F32),
        zs=V((M, WIDE), F32),
        y1=V((M, WIDE), BF),
        z4=V((M, MID), F32),
        h4=V((OD + 2, S, MID), BF),
        win4=V((M, 9 * MID), BF),
        z5=V((M, MID), F32),
        h5=V((M, MID), BF),
        z6=V((M, WIDE), F32),
        mixed_local=V((OD, S // 8, 8, WIDE), BF),
        du2=V((M // 16, 16, WIDE), F32),
        dz6=V((M, WIDE), BF),
        dh=V((M, MID), F32),
        d5=V((OD + 2, S, MID), BF),
        win5=V((M, 9 * MID), BF),
        dz4=V((M, MID), BF),
        du1=V((M // 16, 16, WIDE), F32),
        dzs=V((M, WIDE), BF),
        d2=V((OD + 1, S, MID), BF),
        d2l=V((OD + 1, S, MID), BF),
        stage0=V((32 * cfg.rows[MIXING], 512), BF),
        stage1=V((32 * cfg.rows[SHORTCUT], 512), BF),
        loc=mid_tot,
        locw=V((4, 1, 8, WIDE // 4), F32),
        locw2=V((4, 2, 8, WIDE // 4), F32),
        t1=mid_tot,
        t2=mid_tot,
        t3=V((4, 2, 8, WIDE // 4), F32),
        t4=mid_tot,
        t5=mid_tot,
        t6=V((4, 1, 8, WIDE // 4), F32),
        g1=mid_tot,
        g2=mid_tot,
        g3=V((4, 2, 8, WIDE // 4), F32),
        g4=mid_tot,
        g5=mid_tot,
        g6=V((4, 1, 8, WIDE // 4), F32),
        rc=V((2, 8, MID // 2), F32),
        rq=V((2, 2 * NB, 8, MID // 2), F32),
        rw=V((2, 4, 2, 8, WIDE // 4), F32),
        wb=V((2, NB, 2, 8, WIDE // 4), F32),
        wsend=pltpu.SemaphoreType.DMA((U, 7)),
        wrecv=pltpu.SemaphoreType.DMA((U, 7)),
        wloc=pltpu.SemaphoreType.DMA((7, 4)),
        ms=pltpu.SemaphoreType.DMA((3,)),
        mr=pltpu.SemaphoreType.DMA((3, 2)),
        ws=pltpu.SemaphoreType.DMA((4, 3)),
        wr=pltpu.SemaphoreType.DMA((4, 3)),
        hs=pltpu.SemaphoreType.DMA((2,)),
        hr=pltpu.SemaphoreType.DMA((2,)),
        es=pltpu.SemaphoreType.DMA((2, 2)),
        er=pltpu.SemaphoreType.DMA((2, 2)),
        xs=pltpu.SemaphoreType.DMA((3, OD)),
        xr=pltpu.SemaphoreType.DMA((3, OD)),
        xl=pltpu.SemaphoreType.DMA((OD,)),
        gs=pltpu.SemaphoreType.DMA((2,)),
        gi=pltpu.SemaphoreType.DMA((RD,)),
        rs=pltpu.SemaphoreType.DMA((7, 3, 5)),
        rr=pltpu.SemaphoreType.DMA((7, 3, 5)),
        fs=pltpu.SemaphoreType.DMA((7, 3)),
        fr=pltpu.SemaphoreType.DMA((7, 3)),
        fl=pltpu.SemaphoreType.DMA((7,)),
        x0=V((RD, 2 * S, CIN), BF),
        weave=V((4 * S, LANES), F32),
        ct=V((M, WIDE), BF),
        onehot=V((3, S, LANES), F32),
        active_slot=V((S, LANES), F32),
        pix_in=V((RD, 2 * S, LANES), F32),
        pix_out=V((M, LANES), F32),
        ld=pltpu.SemaphoreType.DMA((5,)),
        norm_values=V((3, 2, 4 * MID + 3 * WIDE), F32),
        gn_values=V((3, 2, 4 * MID + 3 * WIDE), F32),
    )
    scratch.update({"f" + str(name): V((n, 512), BF) for name, n in cfg.flat.items()})
    scratch.update({"l" + str(name): V((cfg.flat[name], 512), BF) for name in cfg.own_landing if cfg.reduce})
    scratch.update({"e" + str(w): V(shape, BF) for w, shape in final.items()})
    names = list(smem_args) + list(hbm_args) + list(outs) + list(scratch)
    smem = pl.BlockSpec(memory_space=pltpu.SMEM)
    res = pl.pallas_call(
        functools.partial(block_kernel, names, cfg),
        out_shape=[o[0] for o in outs.values()],
        in_specs=[smem] * len(smem_args) + [hbm] * len(hbm_args),
        out_specs=[o[1] for o in outs.values()],
        scratch_shapes=list(scratch.values()),
        compiler_params=pltpu.CompilerParams(
            collective_id=0, has_side_effects=True, vmem_limit_bytes=63 * 2**20
        ),
    )(*smem_args.values(), *hbm_args.values())
    return SimpleNamespace(**dict(zip(outs, res)))


def slot_layout(x, slots):
    images, rows, cols, channels = x.shape
    x = jnp.transpose(x, (1, 0, 2, 3)).reshape(rows, images * cols, channels)
    return jnp.pad(x, ((0, 0), (0, slots - images * cols), (0, 0)))


def per_device(
    features, w_reduce, w_spatial, w_expand, w_shortcut, w_squeeze, w_mixing, w_widen,
    norm_reduce, norm_spatial, norm_expand, norm_shortcut, norm_squeeze, norm_mixing, norm_widen,
    cotangent, resolution, active,
):
    images, rd, cols_in, cin = features.shape
    od = rd // 2
    nb = lax.axis_size("batch")
    cfg = plan(features, w_reduce, w_expand, nb)
    S, mid, wide = cfg.slots, cfg.mid, cfg.wide
    x = jnp.pad(features, ((0, 0), (0, 0), (0, 16 - cols_in), (0, 0)))
    x = x.reshape(images, rd, 8, 2, cin)
    x = jnp.transpose(x, (1, 3, 0, 2, 4)).reshape(rd, 2, images * 8, cin)
    x = jnp.pad(x, ((0, 0), (0, 0), (0, S - images * 8), (0, 0))).reshape(rd, 2 * S, cin)
    out_cols = cotangent.shape[2]
    ct = slot_layout(jnp.pad(cotangent, ((0, 0), (0, 0), (0, 8 - out_cols), (0, 0))), S)
    norms = jnp.concatenate(
        [
            jnp.transpose(n, (1, 0, 2))
            for n in (norm_reduce, norm_spatial, norm_squeeze, norm_mixing, norm_expand, norm_shortcut, norm_widen)
        ],
        axis=2,
    )
    res = run_blocks(
        cfg,
        dict(resolution=resolution, active=active),
        dict(
            features=x,
            norms=norms,
            cotangent=ct.reshape(od * S, wide),
            w0=w_reduce,
            w1=w_spatial.reshape(-1, mid),
            w2=w_expand,
            w3=w_shortcut,
            w4=w_squeeze,
            w5=w_mixing.reshape(-1, mid),
            w6=w_widen,
        ),
    )
    mixed = res.mixed[:, :, :out_cols]

    def unpack(g, name):
        b8, _, n, _ = g.shape
        if name in (SPATIAL, MIXING):
            k = n // 9
            return jnp.transpose(g.reshape(b8, 4, 9, k, 512), (2, 0, 1, 3, 4)).reshape(3, 3, b8 * 4 * k, 512)
        if name in (EXPAND, SHORTCUT, WIDEN):
            return jnp.transpose(g, (0, 2, 1, 3)).reshape(b8 * n, 2048)
        return g.reshape(b8 * 4 * n, 512)

    totals = []
    for name, n in cfg.rows.items():
        if cfg.reduce:
            g = getattr(res, "o" + str(name)).astype(F32)
            totals.append(g.reshape((3, 3) + g.shape[1:]) if g.ndim == 3 else g)
            continue
        at = cfg.offs[name]
        part = res.grads[32 * at : 32 * (at + n)].reshape(2, 8, 2, n, 512)
        part = unpack(jnp.transpose(part, (1, 2, 0, 3, 4)).reshape(8, 4, n, 512), name)
        dim = 2 if part.ndim == 4 else 0
        part = lax.psum_scatter(part, "batch", scatter_dimension=dim, tiled=True)
        totals.append(lax.psum(part, "rows").astype(F32))

    gn = [jnp.transpose(res.gn[:, :, at : at + n], (1, 0, 2)) for at, n in cfg.norm_columns]
    return (mixed, res.gin[:, :, :cols_in], *totals, gn[0], gn[1], gn[4], gn[5], gn[2], gn[3], gn[6])


def solution(mesh):
    w2, w4 = P("rows", None), P(None, None, "rows", None)
    o2, o4 = P("batch", None), P(None, None, "batch", None)
    return jax.shard_map(
        per_device,
        mesh=mesh,
        in_specs=(P("batch", "rows", None, None), w2, w4, w2, w2, w2, w4, w2)
        + (P(),) * 7
        + (P("batch", "rows", None, None), P(), P()),
        out_specs=(P("batch", None, None, None), P("batch", "rows", None, None), o2, o4, o2, o2, o2, o4, o2)
        + (P(),) * 7,
        check_vma=False,
    )
```

```python
import functools
from types import SimpleNamespace

import jax
import jax.numpy as jnp
from jax import lax
from jax.experimental import pallas as pl
from jax.experimental.pallas import tpu as pltpu
from jax.sharding import PartitionSpec as P

eps = 1e-05
MESH = pl.DeviceIdType.MESH
BF = jnp.bfloat16
F32 = jnp.float32
LANES = 128
REDUCE, SPATIAL, EXPAND, SHORTCUT, SQUEEZE, MIXING, WIDEN = range(7)
DX, DY, DN, DF = range(4)


def dot(a, b):
    return jnp.dot(a, b, preferred_element_type=F32)


def dot_t(a, b):
    return lax.dot_general(a, b, (((1,), (1,)), ((), ())), preferred_element_type=F32)


def dot_w(a, b):
    return lax.dot_general(a, b, (((0,), (0,)), ((), ())), preferred_element_type=F32)


def aligned(index, size):
    return pl.ds(pl.multiple_of(index * size, size), size)


def loop(count, body):
    def step(i, carry):
        body(i)
        return carry

    lax.fori_loop(0, count, step, 0)


def each(count, body):
    if count > 16:
        loop(count, body)
        return
    for i in range(count):
        body(i)


def silu_parts(u):
    s = jax.nn.sigmoid(u)
    return s, u * s


def slope(u):
    s = jax.nn.sigmoid(u)
    return s * (1.0 + u * (1.0 - s))


def block_kernel(names, cfg, *refs):
    R = SimpleNamespace(**dict(zip(names, refs)))
    S, RD, OD, NB = cfg.slots, cfg.in_rows, cfg.out_rows, cfg.batch
    MID, WIDE, CIN = cfg.mid, cfg.wide, cfg.cin
    M = OD * S
    b = lax.axis_index("batch")
    r = lax.axis_index("rows")
    core = lax.rem(r, 2)
    xb = lax.div(r, 2)
    core_peer = r + 1 - 2 * core
    x_row = lax.rem(r + 2, 4)
    diag = 3 - r
    half = lax.rem(b, 2)

    def flip(i, j):
        if isinstance(j, int):
            out = i
            for bit in range((2 * NB - 1).bit_length()):
                if j >> bit & 1:
                    out = out + (1 << bit) * (1 - 2 * lax.rem(lax.div(i, 1 << bit), 2))
            return out
        out = jnp.int32(0)
        bit = 1
        while bit < 2 * NB:
            p, q = lax.rem(lax.div(i, bit), 2), lax.rem(lax.div(j, bit), 2)
            out = out + bit * (p + q - 2 * p * q)
            bit *= 2
        return out

    me = b * 2 + xb

    def remote(src, dst, send, recv, dev):
        return pltpu.make_async_remote_copy(
            src_ref=src, dst_ref=dst, send_sem=send, recv_sem=recv, device_id=dev, device_id_type=MESH
        )

    def team(id2):
        return (lax.div(id2, 2), 2 * lax.rem(id2, 2) + core)

    units = cfg.units
    wsend, wrecv, wloc = R.wsend, R.wrecv, R.wloc
    near = lax.rem(lax.div(b, 2), 2)
    sides = ((half, (b + 1 - 2 * half, r)), (near, (b + 2 - 4 * near, r)))

    def wview(u, shard, at, fourths):
        w, k0, kn, _ = units[u]
        full = getattr(R, "f" + str(w))
        start = shard * (full.shape[0] // 4) + k0 + at * (kn // 4)
        return full.at[pl.ds(pl.multiple_of(start, 16), fourths * kn // 4)]

    def w_copy(u, i):
        mode = units[u][3]
        first, second = sides if mode == 1 else sides[::-1]
        quarter = x_row if i > 1 else r
        at, fourths, dev = 0, 4, (b, core_peer)
        if i == 1:
            dev = (b, x_row)
        if mode and i > 0:
            fourths = 2 if i > 4 else 1
            at = 2 * second[0] + first[0]
            if i == 3:
                dev = first[1]
            elif i == 4:
                at = at + 1 - 2 * first[0]
            elif i == 5:
                at, dev = 2 * second[0], second[1]
            elif i == 6:
                at = 2 - 2 * second[0]
        view = wview(u, quarter, at, fourths)
        return remote(view, view, wsend.at[u, i], wrecv.at[u, i], dev)

    def w_stages(u):
        return range(7) if units[u][3] else range(3)

    def w_local(w):
        src, full = getattr(R, "w" + str(w)), getattr(R, "f" + str(w))
        n, quarter = src.shape[0], full.shape[0] // 4
        return [
            pltpu.make_async_copy(
                src.at[:, pl.ds(512 * i, 512)],
                full.at[pl.ds(pl.multiple_of(r * quarter + i * n, 16), n)],
                wloc.at[w, i],
            )
            for i in range(src.shape[1] // 512)
        ]

    bar = pltpu.get_barrier_semaphore()
    for dev in ((b, core_peer), (b, diag)):
        pl.semaphore_signal(bar, inc=1, device_id=dev, device_id_type=MESH)

    def greet(j):
        pl.semaphore_signal(bar, inc=1, device_id=team(flip(me, j + 1)), device_id_type=MESH)

    loop(2 * NB - 1, greet)

    loaded = [w_local(w) for w in range(7)]
    for w in range(7):
        for c in loaded[w]:
            c.start()
        if w == 0:
            x0_load = pltpu.make_async_copy(R.features, R.x0, R.ld.at[0])
            x0_load.start()
    norm_load = pltpu.make_async_copy(R.norms, R.norm_values, R.ld.at[2])
    norm_load.start()
    ct_load = pltpu.make_async_copy(R.cotangent, R.ct, R.ld.at[1])
    ct_load.start()
    norm_reduce, norm_spatial, norm_squeeze, norm_mixing, norm_expand, norm_shortcut, norm_widen = [
        R.norm_values.at[:, :, pl.ds(at, width)] for at, width in cfg.norm_columns
    ]
    at_home = set()

    images = cfg.images
    column = lax.broadcasted_iota(jnp.int32, (8, LANES), 0).astype(F32)
    if 8 * images < S:
        tail = slice(8 * images, S)
        none = jnp.zeros((S - 8 * images, LANES), F32)
        R.active_slot[tail, :] = none
        for g in range(3):
            R.onehot[g, tail, :] = none
        for o in range(OD):
            R.pix_out[o * S + 8 * images : (o + 1) * S, :] = none
        for k in range(RD):
            for p in range(2):
                R.pix_in[k, p * S + 8 * images : (p + 1) * S, :] = none

    for i in range(images):
        group = R.resolution[b * images + i]
        side = (5 + group).astype(F32)
        here = slice(8 * i, 8 * i + 8)
        limit = jnp.zeros((8, LANES), F32)
        for g in range(3):
            is_g = jnp.where(group == g, 1.0, 0.0)
            R.onehot[g, here, :] = jnp.full((8, LANES), is_g, F32)
            limit = limit + is_g * R.active[g].astype(F32)
        R.active_slot[here, :] = limit
        for o in range(OD):
            inside = jnp.where((r * OD + o).astype(F32) < side, side, 0.0)
            R.pix_out[o * S + 8 * i : o * S + 8 * i + 8, :] = jnp.where(column < inside, 1.0, 0.0)
        for k in range(RD):
            inside = jnp.where((r * RD + k).astype(F32) < 2.0 * side, 2.0 * side, 0.0)
            for p in range(2):
                R.pix_in[k, p * S + 8 * i : p * S + 8 * i + 8, :] = jnp.where(2.0 * column + p < inside, 1.0, 0.0)

    pl.semaphore_wait(bar, 2 * NB + 1)

    def w_start(u):
        w = units[u][0]
        if w not in at_home:
            at_home.add(w)
            for c in loaded[w]:
                c.wait()
        w_copy(u, 1).start()
        w_copy(u, 0).start()

    def w_second(u):
        w_copy(u, 1).wait_recv()
        if units[u][3]:
            w_copy(u, 3).start()
        w_copy(u, 2).start()

    def w_third(u):
        if units[u][3]:
            w_copy(u, 3).wait_recv()
            w_copy(u, 5).start()
            w_copy(u, 4).start()

    def w_fourth(u):
        if units[u][3]:
            w_copy(u, 5).wait_recv()
            w_copy(u, 6).start()

    def w_ready(u):
        for i in w_stages(u)[::2]:
            w_copy(u, i).wait_recv()

    pumped = [0]
    lags = cfg.lags

    def pump(steps):
        for _ in range(steps):
            n = pumped[0]
            for lag, stage in zip(lags, (w_start, w_second, w_third, w_fourth)):
                if 0 <= n - lag < len(units):
                    stage(n - lag)
            pumped[0] = n + 1

    def need(name):
        last = max(u for u in range(len(units)) if units[u][0] == name)
        while pumped[0] < last + lags[3 if units[last][3] else 1] + 1:
            pump(1)
        for u in range(len(units)):
            if units[u][0] == name:
                w_ready(u)

    def mid_start(k):
        p = k % 2
        swap = remote(R.loc.at[1 - core], R.rc.at[p], R.ms.at[0], R.mr.at[0, p], (b, core_peer))
        swap.start()
        swap.wait_recv()
        R.rq[p, me] = R.loc[core] + R.rc[p]

        def send(j):
            to = team(flip(me, 2 * NB - 1 - j))
            remote(R.rq.at[p, me, pl.ds(0, 6)], R.rq.at[p, me, pl.ds(0, 6)], R.ms.at[1], R.mr.at[1, p], to).start()

        each(2 * NB - 1, send)
        swap.wait_send()

    def mid_finish(k, tot):
        p = k % 2
        rest = R.rq.at[p, pl.ds(0, 2 * NB - 1), pl.ds(0, 6)]
        every = remote(rest, rest, R.ms.at[1], R.mr.at[1, p], (b, x_row))
        every.wait_recv()
        total = R.rq[p, 0]
        for j in range(1, 2 * NB):
            total = total + R.rq[p, j]
        tot[core] = total
        back = remote(tot.at[core], tot.at[core], R.ms.at[2], R.mr.at[2, p], (b, core_peer))
        back.start()
        every.wait_send()
        back.wait()

    six = pl.ds(0, 6)

    def wide_start(k, loc):
        n = loc.shape[1]
        norms = pl.ds(0, n)
        rw, wb = R.rw.at[k % 2, :, norms], R.wb.at[k % 2, :, norms]
        rw[r] = loc[r]
        for to in (core_peer, x_row, diag):
            remote(loc.at[to, :, six], rw.at[r, :, six], R.ws.at[k, 0], R.wr.at[k, 0], (b, to)).start()
        three = remote(
            loc.at[pl.ds(0, 3), :, six], rw.at[pl.ds(0, 3), :, six], R.ws.at[k, 0], R.wr.at[k, 0], (b, core_peer)
        )
        three.wait_recv()
        wb[b] = rw[0] + rw[1] + (rw[2] + rw[3])

        def send(j):
            to = flip(b, NB - 1 - j)
            remote(wb.at[b, :, six], wb.at[b, :, six], R.ws.at[k, 1], R.wr.at[k, 1], (to, r)).start()

        each(NB - 1, send)
        three.wait_send()

    def wide_finish(k, tot):
        n = tot.shape[1]
        wb = R.wb.at[k % 2, :, pl.ds(0, n)]
        rest = wb.at[pl.ds(0, NB - 1), :, six]
        every = remote(rest, rest, R.ws.at[k, 1], R.wr.at[k, 1], (b, x_row))
        every.wait_recv()
        total = wb[0]
        for j in range(1, NB):
            total = total + wb[j]
        tot[r] = total
        for to in (core_peer, x_row, diag):
            remote(tot.at[r, :, six], tot.at[r, :, six], R.ws.at[k, 2], R.wr.at[k, 2], (b, to)).start()
        rest = tot.at[pl.ds(0, 3), :, six]
        three = remote(rest, rest, R.ws.at[k, 2], R.wr.at[k, 2], (b, core_peer))
        every.wait_send()
        three.wait()

    def mid_at(ref, j):
        return ref.at[lax.div(j, 2), :, aligned(lax.rem(j, 2), LANES)]

    def wide_at(ref, j, norm=0):
        return ref.at[lax.div(j, 4), norm, :, aligned(lax.rem(j, 4), LANES)]

    def group_rows(ref, row, values):
        for g in range(3):
            ref[row + g : row + g + 1, :] = jnp.sum(values * R.onehot[g], axis=0, keepdims=True)

    def blank(ref, row, rows):
        ref[row : row + rows, :] = jnp.zeros((rows, LANES), F32)

    def spread(rows3):
        return rows3[0] * R.onehot[0] + rows3[1] * R.onehot[1] + rows3[2] * R.onehot[2]

    def moments(sums, inv_n, row=0):
        means, invs = [], []
        for g in range(3):
            n = 1.0 / inv_n[g]
            mean = sums[row + g : row + g + 1, :] * n
            var = sums[row + 3 + g : row + 4 + g, :] * n - mean * mean
            means.append(mean)
            invs.append(lax.rsqrt(var + eps))
        return means, invs

    OUT = [cfg.members * (5.0 + g) * (5.0 + g) for g in range(3)]
    IN = [cfg.members * (10.0 + 2.0 * g) * (10.0 + 2.0 * g) for g in range(3)]

    def forward_terms(sums, params, cols, inv_n, row=0):
        means, invs = moments(sums, inv_n, row)
        scales = [invs[g] * params[g, 0:1, cols] for g in range(3)]
        shifts = [params[g, 1:2, cols] - means[g] * scales[g] for g in range(3)]
        return spread(scales), spread(shifts)

    def xhat_terms(sums, inv_n, row=0):
        means, invs = moments(sums, inv_n, row)
        return spread(invs), spread([-means[g] * invs[g] for g in range(3)])

    def backward_terms(sums, grads, params, cols, inv_n, row=0, g0=0, g1=3):
        means, invs = moments(sums, inv_n, row)
        fs, az, bz = [], [], []
        for g in range(3):
            n = 1.0 / inv_n[g]
            f = invs[g] * params[g, 0:1, cols]
            gain = grads[g0 + g : g0 + g + 1, :] * n * invs[g]
            bias = grads[g1 + g : g1 + g + 1, :] * n
            fs.append(f)
            bz.append(f * gain)
            az.append(f * (bias - means[g] * gain))
        return spread(fs), spread(az), spread(bz)

    def keep(j, ratio):
        lane = lax.broadcasted_iota(jnp.int32, (S, LANES), 1).astype(F32) + j * float(LANES)
        return jnp.where(lane < R.active_slot[...] * ratio, 1.0, 0.0)

    def out_rows(k):
        return slice(k * S, (k + 1) * S)

    def groups16(o):
        return slice(o * (S // 16), (o + 1) * (S // 16))

    def forward_stats(z, loc_at, row=0):
        def body(j):
            cols = aligned(j, LANES)
            s = jnp.zeros((S, LANES), F32)
            q = jnp.zeros((S, LANES), F32)
            for o in range(OD):
                v = z[out_rows(o), cols]
                m = v * R.pix_out[out_rows(o), :]
                s = s + m
                q = q + m * v
            st = loc_at(j)
            group_rows(st, row, s)
            group_rows(st, row + 3, q)
            blank(st, row + 6, 2)

        loop(z.shape[-1] // LANES, body)

    def rolled(v, by):
        return pltpu.roll(v, by % S, 0)

    def by_shard(t, j):
        return pl.ds(pl.multiple_of(j * (9 * LANES) + t * LANES, LANES), LANES)

    def by_tap(t, j):
        return pl.ds(pl.multiple_of(t * MID + j * LANES, LANES), LANES)

    def unit_windows(halo, win, rows, flipped):
        place = by_tap if flipped else by_shard

        def body(j):
            cols = aligned(j, LANES)
            for k in rows:
                v = halo[k, :, cols].astype(F32)
                moved = (rolled(v, 1).astype(BF), v.astype(BF), rolled(v, -1).astype(BF))
                for dr in range(3):
                    o = k - dr
                    if not 0 <= o < OD:
                        continue
                    for dc in range(3):
                        t = (2 - dr) * 3 + 2 - dc if flipped else dr * 3 + dc
                        win[out_rows(o), place(t, j)] = moved[dc]

        loop(MID // LANES, body)

    def edge_exchange(halo, k):
        up = remote(halo.at[1], halo.at[OD + 1], R.es.at[k, 0], R.er.at[k, 0], (b, jnp.maximum(r - 1, 0)))
        down = remote(halo.at[OD], halo.at[0], R.es.at[k, 1], R.er.at[k, 1], (b, jnp.minimum(r + 1, 3)))

        @pl.when(r > 0)
        def _():
            up.start()

        @pl.when(r < 3)
        def _():
            down.start()

        @pl.when(r == 0)
        def _():
            halo[0] = jnp.zeros(halo.shape[1:], BF)

        @pl.when(r == 3)
        def _():
            halo[OD + 1] = jnp.zeros(halo.shape[1:], BF)

        return up, down

    def edge_wait(pair):
        up, down = pair

        @pl.when(r < 3)
        def _():
            up.wait_recv()
            down.wait_send()

        @pl.when(r > 0)
        def _():
            down.wait_recv()
            up.wait_send()

    x0_load.wait()
    norm_load.wait()
    need(REDUCE)

    def z1_rows(k):
        def mask(j):
            cols = aligned(j, LANES)
            ch = keep(j, float(CIN // MID))
            for p in range(2):
                m = (ch * R.pix_in[k, out_rows(p), :]).astype(BF)
                R.x0[k, out_rows(p), cols] = R.x0[k, out_rows(p), cols] * m

        loop(CIN // LANES, mask)
        R.z1[k] = dot(R.x0[k], R.f0[...])

    loop(RD, z1_rows)

    def z1_stats(j):
        cols = aligned(j, LANES)
        s = jnp.zeros((S, LANES), F32)
        q = jnp.zeros((S, LANES), F32)
        for k in range(RD):
            for p in range(2):
                v = R.z1[k, out_rows(p), cols]
                m = v * R.pix_in[k, out_rows(p), :]
                s = s + m
                q = q + m * v
        st = mid_at(R.loc, j)
        group_rows(st, 0, s)
        group_rows(st, 3, q)
        blank(st, 6, 2)

    loop(MID // LANES, z1_stats)
    mid_start(0)
    pump(cfg.pumps[0])
    mid_finish(0, R.t1)

    last = RD - 1

    def h1_body(j):
        cols = aligned(j, LANES)
        sc, sh = forward_terms(mid_at(R.t1, j), norm_reduce, cols, IN)
        ch = keep(j, 1.0)
        for k in range(RD - 1, -1, -1):
            for p in range(2):
                u = R.z1[k, out_rows(p), cols] * sc + sh
                h = silu_parts(u)[1] * (ch * R.pix_in[k, out_rows(p), :])
                if k == last:
                    R.h1s[p, :, cols] = h.astype(BF)
                for dr in range(3):
                    o2 = k + 1 - dr
                    if o2 % 2 or not 0 <= o2 // 2 < OD:
                        continue
                    o = o2 // 2
                    taps = ((1, h),) if p == 0 else ((0, rolled(h, 1)), (2, h))
                    for dc, v in taps:
                        t = dr * 3 + dc
                        R.win1[out_rows(o), by_shard(t, j)] = v.astype(BF)

    loop(MID // LANES, h1_body)
    down = remote(R.h1s, R.h1r, R.hs.at[0], R.hr.at[0], (b, jnp.minimum(r + 1, 3)))

    @pl.when(r < 3)
    def _():
        down.start()

    pump(cfg.pumps[1])

    @pl.when(r > 0)
    def _():
        down.wait_recv()

    @pl.when(r == 0)
    def _():
        R.h1r[...] = jnp.zeros(R.h1r.shape, BF)

    def h1_halo(j):
        cols = aligned(j, LANES)
        even = R.h1r[0, :, cols]
        odd = R.h1r[1, :, cols]
        for dc, v in ((0, rolled(odd.astype(F32), 1).astype(BF)), (1, even), (2, odd)):
            R.win1[out_rows(0), by_shard(dc, j)] = v

    loop(MID // LANES, h1_halo)

    @pl.when(r < 3)
    def _():
        down.wait_send()

    need(SPATIAL)

    def conv(win, weight, z):
        def body(j):
            cols = aligned(j, 256)
            z[:, cols] = dot(win[...], weight[:, cols])

        loop(MID // 256, body)

    conv(R.win1, R.f1, R.z2)
    forward_stats(R.z2, lambda j: mid_at(R.loc, j))
    def piece(weight, shard, j):
        n = weight.shape[0] // 16
        return weight[pl.ds(pl.multiple_of((shard * 4 + j) * n, n), n), :]

    def block(weight, j):
        return jnp.concatenate([piece(weight, q, j) for q in range(4)], axis=0)

    mid_start(1)
    pump(cfg.pumps[2])
    need(SHORTCUT)

    def zs_body(j):
        cols = aligned(j, 512)
        w = block(R.f3, j)
        for o in range(OD):
            R.zs[out_rows(o), cols] = dot(R.x0[2 * o, 0:S, :], w)

    loop(WIDE // 512, zs_body)
    forward_stats(R.zs, lambda j: wide_at(R.locw2, j, 1), 0)
    mid_finish(1, R.t2)

    def activate(z, tot, params, dest):
        def body(j):
            cols = aligned(j, LANES)
            sc, sh = forward_terms(mid_at(tot, j), params, cols, OUT)
            ch = keep(j, 1.0)
            for o in range(OD):
                u = z[out_rows(o), cols] * sc + sh
                dest(o, cols, (silu_parts(u)[1] * (ch * R.pix_out[out_rows(o), :])).astype(BF))

        loop(MID // LANES, body)

    def to_h2(o, cols, v):
        R.h2[out_rows(o), cols] = v

    activate(R.z2, R.t2, norm_spatial, to_h2)
    need(EXPAND)

    def expand_to(h, weight, z):
        def body(j):
            z[:, aligned(j, 512)] = dot(h[...], block(weight, j))

        loop(WIDE // 512, body)

    expand_to(R.h2, R.f2, R.z3)
    forward_stats(R.z3, lambda j: wide_at(R.locw2, j), 0)
    wide_start(0, R.locw2)
    pump(cfg.pumps[3])
    wide_finish(0, R.t3)

    def u1_terms(j):
        cols = aligned(j, LANES)
        tot = wide_at(R.t3, j)
        sc3, sh3 = forward_terms(tot, norm_expand, cols, OUT, 0)
        scs, shs = forward_terms(wide_at(R.t3, j, 1), norm_shortcut, cols, OUT, 0)
        shift = sh3 + shs

        def u1(o):
            return R.z3[out_rows(o), cols] * sc3 + R.zs[out_rows(o), cols] * scs + shift

        return u1

    def y1_body(j):
        cols = aligned(j, LANES)
        u1 = u1_terms(j)
        ch = keep(j, float(WIDE // MID))
        for o in range(OD):
            y = silu_parts(u1(o))[1] * (ch * R.pix_out[out_rows(o), :])
            R.y1[out_rows(o), cols] = y.astype(BF)

    loop(WIDE // LANES, y1_body)
    need(SQUEEZE)

    def squeeze_body(j):
        cols = aligned(j, 256)
        R.z4[:, cols] = dot(R.y1[...], R.f4[:, cols])

    loop(MID // 256, squeeze_body)
    forward_stats(R.z4, lambda j: mid_at(R.loc, j))
    mid_start(2)
    pump(cfg.pumps[4])
    mid_finish(2, R.t4)

    def to_h4(o, cols, v):
        R.h4[o + 1, :, cols] = v

    activate(R.z4, R.t4, norm_squeeze, to_h4)
    pair = edge_exchange(R.h4, 0)
    pump(cfg.pumps[5])
    unit_windows(R.h4, R.win4, range(1, OD + 1), False)
    edge_wait(pair)
    unit_windows(R.h4, R.win4, (0, OD + 1), False)
    need(MIXING)
    conv(R.win4, R.f5, R.z5)
    forward_stats(R.z5, lambda j: mid_at(R.loc, j))
    mid_start(3)
    pump(cfg.pumps[6])
    mid_finish(3, R.t5)

    def to_h5(o, cols, v):
        R.h5[out_rows(o), cols] = v

    activate(R.z5, R.t5, norm_mixing, to_h5)
    need(WIDEN)
    expand_to(R.h5, R.f6, R.z6)
    forward_stats(R.z6, lambda j: wide_at(R.locw, j))
    wide_start(1, R.locw)
    wide_finish(1, R.t6)
    for u in range(len(units)):
        for i in w_stages(u):
            w_copy(u, i).wait_send()

    def u2_body(j):
        cols = aligned(j, LANES)
        tot = wide_at(R.t6, j)
        sc, sh = forward_terms(tot, norm_widen, cols, OUT)
        xa, xs = xhat_terms(tot, OUT)
        ch = keep(j, float(WIDE // MID))
        g0 = jnp.zeros((S, LANES), F32)
        g1 = jnp.zeros((S, LANES), F32)
        for o in range(OD):
            z = R.z6[out_rows(o), cols]
            u = z * sc + sh + R.y1[out_rows(o), cols].astype(F32)
            mask = ch * R.pix_out[out_rows(o), :]
            s, su = silu_parts(u)
            R.mixed_local[o, :, :, cols] = (su * mask).reshape(S // 8, 8, LANES).astype(BF)
            d = R.ct[out_rows(o), cols].astype(F32) * mask * (s * (1.0 + u * (1.0 - s)))
            R.du2[groups16(o), :, cols] = d.reshape(S // 16, 16, LANES)
            g0 = g0 + d * (z * xa + xs)
            g1 = g1 + d
        st = wide_at(R.locw, j)
        group_rows(st, 0, g0)
        group_rows(st, 3, g1)
        blank(st, 6, 2)

    ct_load.wait()
    loop(WIDE // LANES, u2_body)
    wide_start(2, R.locw)
    def mixed_copy(i, o):
        row = (x_row if i == 2 else r) * OD + o
        dst = R.mixed.at[:, row]
        src = dst if i == 2 else R.mixed_local.at[o, pl.ds(0, images)]
        if i == 3:
            return pltpu.make_async_copy(src, dst, R.xl.at[o])
        return remote(src, dst, R.xs.at[i, o], R.xr.at[i, o], (b, x_row if i == 1 else core_peer))

    for o in range(OD):
        for i in (0, 3):
            mixed_copy(i, o).start()
    wide_finish(2, R.g6)

    def widen_back(j):
        cols = aligned(j, LANES)
        f, a, bz = backward_terms(wide_at(R.t6, j), wide_at(R.g6, j), norm_widen, cols, OUT)
        for o in range(OD):
            d = f * R.du2[groups16(o), :, cols].reshape(S, LANES) - a - R.z6[out_rows(o), cols] * bz
            R.dz6[out_rows(o), cols] = (d * R.pix_out[out_rows(o), :]).astype(BF)

    loop(WIDE // LANES, widen_back)

    mine = {DY: lax.rem(b, 2), DN: lax.rem(lax.div(b, 2), 2), DF: lax.div(b, 4), DX: xb}
    turn = [1]
    begun = {}

    def partner(d):
        other = 1 - 2 * mine[d]
        if d == DX:
            return (b, x_row)
        return (b + other * {DY: 1, DN: 2, DF: 4}[d], r)

    def put(stage, w, core_of, bits, start, value):
        for n0, np_, order in cfg.parts[w]:
            lo, hi = max(start, n0), min(start + value.shape[0], n0 + np_)
            if lo >= hi:
                continue
            idx = 0
            for d in order:
                idx = 2 * idx + bits[d]
            row = 32 * n0 + (core_of * 16 + idx) * np_ + lo - n0
            stage[pl.ds(row if isinstance(row, int) else pl.multiple_of(row, 16), hi - lo), :] = value[
                lo - start : hi - start
            ].astype(BF)

    def batch_bits(y, zn, zf, x):
        return {DY: y, DN: zn, DF: zf, DX: x}

    def staged(w, fill):
        i = turn[0] % 2
        turn[0] += 1
        stage = (R.stage0, R.stage1)[i]
        n = cfg.rows[w]
        assert 32 * n <= stage.shape[0], w
        if cfg.reduce:
            fill(stage)
            begun[w] = (stage, [0] * len(cfg.parts[w]), [0])
            for p in range(len(cfg.parts[w])):
                rs_core(w, p).start()
            return
        if i in begun:
            begun[i].wait()
        fill(stage)
        off = 32 * cfg.offs[w]
        begun[i] = pltpu.make_async_copy(
            stage.at[pl.ds(0, 32 * n)], R.grads.at[pl.ds(off, 32 * n)], R.gs.at[i]
        )
        begun[i].start()

    def land_of(w):
        return getattr(R, ("l" if w in cfg.own_landing else "f") + str(w))

    def rs_core(w, p):
        n0, np_, order = cfg.parts[w][p]
        stage = begun[w][0]
        src = stage.at[pl.ds(pl.multiple_of(32 * n0 + (1 - core) * 16 * np_, 16), 16 * np_)]
        dst = land_of(w).at[pl.ds(32 * n0, 16 * np_)]
        return remote(src, dst, R.rs.at[w, p, 0], R.rr.at[w, p, 0], (b, core_peer))

    def rs_kept(w, p, step):
        n0, np_, order = cfg.parts[w][p]
        at, size = 0, 16 * np_
        for d in order[:step]:
            size = size // 2
            at = at + mine[d] * size
        return at, size

    def rs_link(w, p, step):
        n0, np_, order = cfg.parts[w][p]
        at, size = rs_kept(w, p, step - 1)
        size = size // 2
        d = order[step - 1]
        src = land_of(w).at[pl.ds(pl.multiple_of(32 * n0 + at + (1 - mine[d]) * size, 16), size)]
        dst = land_of(w).at[pl.ds(32 * n0 + 32 * np_ - 2 * size, size)]
        i = w
        return remote(src, dst, R.rs.at[i, p, step], R.rr.at[i, p, step], partner(d))

    def final(w):
        return getattr(R, "e" + str(w))

    def rs_add(w, p, step):
        n0, np_, order = cfg.parts[w][p]
        land = land_of(w)
        at, size = rs_kept(w, p, step)
        if step == 0:
            other, start = begun[w][0], 32 * n0 + core * 16 * np_
        else:
            other, start = land, 32 * n0 + 32 * np_ - 2 * size
        last_step = step == 4

        def body(i):
            rows = pl.ds(pl.multiple_of(32 * n0 + at + i * np_, 16), np_)
            v = land[rows, :] + other[pl.ds(pl.multiple_of(start + i * np_, 16), np_), :]
            if not last_step:
                land[rows, :] = v
            elif w in (SPATIAL, MIXING):
                k = cfg.rows[w] // 9
                final(w)[n0 // k : (n0 + np_) // k] = v.reshape(np_ // k, k, 512)
            else:
                final(w)[n0 : n0 + np_, :] = v

        if size == np_:
            body(0)
        else:
            loop(size // np_, body)

    def home(w, row):
        out, n = getattr(R, "o" + str(w)), cfg.rows[w]
        if w in (SPATIAL, MIXING):
            return out.at[:, aligned(row, n // 9)]
        if w in (EXPAND, SHORTCUT, WIDEN):
            return out.at[:, aligned(row, 512)]
        return out.at[aligned(row, n)]

    def fin_copy(w, i):
        dst = home(w, x_row if i == 2 else r)
        src = dst if i == 2 else final(w)
        if i == 3:
            return pltpu.make_async_copy(src, dst, R.fl.at[w])
        return remote(src, dst, R.fs.at[w, i], R.fr.at[w, i], (b, x_row if i == 1 else core_peer))

    def rs_step(*kernels, parts=(0, 1, 2)):
        if not cfg.reduce:
            return
        for w in kernels:
            stage, steps, ends = begun[w]
            if ends[0] == 1:
                fin_copy(w, 1).wait_recv()
                fin_copy(w, 2).start()
                ends[0] = 2
            for p in parts:
                if p >= len(steps) or steps[p] > 4:
                    continue
                step = steps[p]
                c = rs_core(w, p) if step == 0 else rs_link(w, p, step)
                c.wait_recv()
                rs_add(w, p, step)
                if step < 4:
                    rs_link(w, p, step + 1).start()
                c.wait_send()
                steps[p] = step + 1
            if ends[0] == 0 and min(steps) == 5:
                for i in (1, 0, 3):
                    fin_copy(w, i).start()
                ends[0] = 1

    def rs_round():
        if cfg.reduce:
            rs_step(*[w for w in reversed(list(begun)) if begun[w][2][0] < 2])

    def rs_end():
        if not cfg.reduce:
            for copy in begun.values():
                copy.wait()
            return
        while any(begun[w][2][0] < 2 for w in begun):
            rs_round()
        for w in cfg.rows:
            fin_copy(w, 0).wait()
            fin_copy(w, 1).wait_send()
            fin_copy(w, 2).wait()
            fin_copy(w, 3).wait()

    def fill_out(w, act, dz):
        def fill(stage):
            def body(j):
                res = dot_w(act(), dz[:, aligned(j, 512)])
                n = res.shape[0] // 8
                for i in range(8):
                    bits = batch_bits(i % 2, i // 2 % 2, i // 4, lax.div(j, 2))
                    put(stage, w, lax.rem(j, 2), bits, 0, res[i * n : (i + 1) * n])

            loop(WIDE // 512, body)

        return fill

    def fill_conv(w, win, dz):
        def fill(stage):
            n = MID // 32

            def body(q):
                for t0 in range(0, 9, 3):
                    cols = pl.ds(pl.multiple_of(q * (9 * LANES) + t0 * LANES, LANES), 3 * LANES)
                    res = dot_w(win[:, cols], dz())
                    for t in range(3):
                        for i in range(8):
                            bits = batch_bits(i // 4, lax.rem(q, 2), lax.div(q, 2), i // 2 % 2)
                            at = t * LANES + i * n
                            put(stage, w, i % 2, bits, (t0 + t) * n, res[at : at + n])

            loop(4, body)

        return fill

    def mid_back_sums(dh, z, tot, params):
        def body(j):
            cols = aligned(j, LANES)
            sums = mid_at(tot, j)
            sc, sh = forward_terms(sums, params, cols, OUT)
            xa, xs = xhat_terms(sums, OUT)
            ch = keep(j, 1.0)
            g0 = jnp.zeros((S, LANES), F32)
            g1 = jnp.zeros((S, LANES), F32)
            for o in range(OD):
                v = z[out_rows(o), cols]
                d = dh[out_rows(o), cols] * (ch * R.pix_out[out_rows(o), :]) * slope(v * sc + sh)
                dh[out_rows(o), cols] = d
                g0 = g0 + d * (v * xa + xs)
                g1 = g1 + d
            st = mid_at(R.loc, j)
            group_rows(st, 0, g0)
            group_rows(st, 3, g1)
            blank(st, 6, 2)

        loop(MID // LANES, body)

    def mid_back_apply(dh, z, tot, grads, params, dest):
        def body(j):
            cols = aligned(j, LANES)
            f, a, bz = backward_terms(mid_at(tot, j), mid_at(grads, j), params, cols, OUT)
            for o in range(OD):
                d = f * dh[out_rows(o), cols] - a - z[out_rows(o), cols] * bz
                dest(o, cols, (d * R.pix_out[out_rows(o), :]).astype(BF))

        loop(MID // LANES, body)

    def reduce_back(dz, weight, dh):
        def body(i):
            acc = None
            for j in range(4):
                w = jnp.concatenate([piece(weight, 2 * i + q, j) for q in range(2)], axis=0)
                v = dot_t(dz[:, j * 512 : (j + 1) * 512], w)
                acc = v if acc is None else acc + v
            dh[:, aligned(i, MID // 2)] = acc

        loop(2, body)

    def tap_rows(weight, i, t):
        n = MID // 4
        return jnp.concatenate(
            [weight[pl.ds(pl.multiple_of(((2 * i + q) * 9 + t) * n, n), n), :] for q in range(2)], axis=0
        )

    reduce_back(R.dz6, R.f6, R.dh)
    mid_back_sums(R.dh, R.z5, R.t5, norm_mixing)
    mid_start(4)
    mixed_copy(1, 0).start()
    staged(WIDEN, fill_out(WIDEN, lambda: R.h5[...], R.dz6))
    mid_finish(4, R.g5)

    def to_d5(o, cols, v):
        R.d5[o + 1, :, cols] = v

    mid_back_apply(R.dh, R.z5, R.t5, R.g5, norm_mixing, to_d5)
    pair = edge_exchange(R.d5, 1)
    rs_step(WIDEN)
    unit_windows(R.d5, R.win5, range(1, OD + 1), True)
    edge_wait(pair)
    unit_windows(R.d5, R.win5, (0, OD + 1), True)

    def conv_back(j):
        acc = None
        for t in range(9):
            v = dot_t(R.win5[:, t * MID : (t + 1) * MID], tap_rows(R.f5, j, t))
            acc = v if acc is None else acc + v
        R.dh[:, aligned(j, MID // 2)] = acc

    loop(2, conv_back)
    mid_back_sums(R.dh, R.z4, R.t4, norm_squeeze)
    mid_start(5)
    for o in range(1, OD):
        mixed_copy(1, o).start()
    rs_step(WIDEN)
    staged(MIXING, fill_conv(MIXING, R.win4, lambda: R.d5[1 : OD + 1].reshape(M, MID)))
    mid_finish(5, R.g4)

    def to_d4(o, cols, v):
        R.dz4[out_rows(o), cols] = v

    mid_back_apply(R.dh, R.z4, R.t4, R.g4, norm_squeeze, to_d4)

    def squeeze_back(j):
        n = WIDE // 4
        R.du1[:, :, aligned(j, n)] = dot_t(R.dz4[...], R.f4[aligned(j, n), :]).reshape(M // 16, 16, n)

    loop(4, squeeze_back)

    def u1_back(j):
        cols = aligned(j, LANES)
        u1 = u1_terms(j)
        tot = wide_at(R.t3, j)
        xa3, xs3 = xhat_terms(tot, OUT, 0)
        xas, xss = xhat_terms(wide_at(R.t3, j, 1), OUT, 0)
        ch = keep(j, float(WIDE // MID))
        g0 = jnp.zeros((S, LANES), F32)
        g1 = jnp.zeros((S, LANES), F32)
        g2 = jnp.zeros((S, LANES), F32)
        for o in range(OD):
            rows = out_rows(o)
            d = (R.du1[groups16(o), :, cols] + R.du2[groups16(o), :, cols]).reshape(S, LANES) * (ch * R.pix_out[rows, :]) * slope(u1(o))
            R.du1[groups16(o), :, cols] = d.reshape(S // 16, 16, LANES)
            g0 = g0 + d * (R.z3[rows, cols] * xa3 + xs3)
            g2 = g2 + d * (R.zs[rows, cols] * xas + xss)
            g1 = g1 + d
        st = wide_at(R.locw2, j)
        group_rows(st, 0, g0)
        group_rows(st, 3, g1)
        blank(st, 6, 2)
        st = wide_at(R.locw2, j, 1)
        group_rows(st, 0, g2)
        group_rows(st, 3, g1)
        blank(st, 6, 2)

    loop(WIDE // LANES, u1_back)
    wide_start(3, R.locw2)

    def fill_squeeze(stage):
        def body(j):
            res = dot_w(R.y1[:, aligned(j, WIDE // 8)], R.dz4[...])
            n = res.shape[0] // 4
            bits = (lax.rem(j, 2), lax.rem(lax.div(j, 2), 2), lax.div(j, 4))
            for i in range(4):
                put(stage, SQUEEZE, i % 2, batch_bits(*bits, i // 2), 0, res[i * n : (i + 1) * n])

        loop(8, body)

    rs_step(MIXING, WIDEN)
    staged(SQUEEZE, fill_squeeze)
    wide_finish(3, R.g3)

    for o in range(OD):
        mixed_copy(1, o).wait_recv()
        mixed_copy(2, o).start()

    def u1_apply(j):
        cols = aligned(j, LANES)
        tot, grads = wide_at(R.t3, j), wide_at(R.g3, j)
        f3, a3, b3 = backward_terms(tot, grads, norm_expand, cols, OUT, 0, 0, 3)
        fs, as_, bs = backward_terms(wide_at(R.t3, j, 1), wide_at(R.g3, j, 1), norm_shortcut, cols, OUT)
        for o in range(OD):
            rows = out_rows(o)
            d = R.du1[groups16(o), :, cols].reshape(S, LANES)
            pix = R.pix_out[rows, :]
            R.dz6[rows, cols] = ((f3 * d - a3 - R.z3[rows, cols] * b3) * pix).astype(BF)
            R.dzs[rows, cols] = ((fs * d - as_ - R.zs[rows, cols] * bs) * pix).astype(BF)

    loop(WIDE // LANES, u1_apply)
    reduce_back(R.dz6, R.f2, R.dh)
    mid_back_sums(R.dh, R.z2, R.t2, norm_spatial)
    mid_start(6)
    rs_step(SQUEEZE, MIXING, WIDEN)
    staged(EXPAND, fill_out(EXPAND, lambda: R.h2[...], R.dz6))

    def even_rows():
        return jnp.concatenate([R.x0[2 * o, 0:S, :] for o in range(OD)], axis=0)

    staged(SHORTCUT, fill_out(SHORTCUT, even_rows, R.dzs))
    mid_finish(6, R.g2)

    def to_d2(o, cols, v):
        R.d2[o, :, cols] = v

    mid_back_apply(R.dh, R.z2, R.t2, R.g2, norm_spatial, to_d2)
    up = remote(R.d2.at[0], R.d2.at[OD], R.hs.at[1], R.hr.at[1], (b, jnp.maximum(r - 1, 0)))

    @pl.when(r > 0)
    def _():
        up.start()

    @pl.when(r == 3)
    def _():
        R.d2[OD] = jnp.zeros(R.d2.shape[1:], BF)

    rs_step(EXPAND, SHORTCUT, MIXING, SQUEEZE, WIDEN)
    staged(SPATIAL, fill_conv(SPATIAL, R.win1, lambda: R.d2[0:OD].reshape(M, MID)))

    @pl.when(r < 3)
    def _():
        up.wait_recv()

    @pl.when(r > 0)
    def _():
        up.wait_send()

    def dh1_at(k, j, width):
        return pl.ds(pl.multiple_of(k * MID + j * width, LANES), width)

    def d2_left(j):
        cols = aligned(j, LANES)
        for k in range(OD + 1):
            R.d2l[k, :, cols] = rolled(R.d2[k, :, cols].astype(F32), -1).astype(BF)

    loop(MID // LANES, d2_left)

    def spatial_back(j):
        here, left = R.d2[0:OD].reshape(M, MID), R.d2l[0:OD].reshape(M, MID)
        below, below_left = R.d2[1 : OD + 1].reshape(M, MID), R.d2l[1 : OD + 1].reshape(M, MID)

        def w(dr, dc):
            return tap_rows(R.f1, j, dr * 3 + dc)

        cols = aligned(j, MID // 2)
        parts = (
            ((here, 1, 1),),
            ((here, 1, 2), (left, 1, 0)),
            ((here, 2, 1), (below, 0, 1)),
            ((here, 2, 2), (left, 2, 0), (below, 0, 2), (below_left, 0, 0)),
        )
        for i, terms in enumerate(parts):
            rp, cp = divmod(i, 2)
            acc = None
            for v, dr, dc in terms:
                y = dot_t(v, w(dr, dc))
                acc = y if acc is None else acc + y
            for o in range(OD):
                R.zs[out_rows(cp), dh1_at(2 * o + rp, j, MID // 2)] = acc[out_rows(o)]

    loop(2, spatial_back)

    def h1_back(j):
        cols = aligned(j, LANES)
        sums = mid_at(R.t1, j)
        sc, sh = forward_terms(sums, norm_reduce, cols, IN)
        xa, xs = xhat_terms(sums, IN)
        ch = keep(j, 1.0)
        g0 = jnp.zeros((S, LANES), F32)
        g1 = jnp.zeros((S, LANES), F32)
        for k in range(RD):
            for p in range(2):
                rows = out_rows(p)
                v = R.z1[k, rows, cols]
                d = R.zs[rows, dh1_at(k, j, LANES)] * (ch * R.pix_in[k, rows, :]) * slope(v * sc + sh)
                R.zs[rows, dh1_at(k, j, LANES)] = d
                g0 = g0 + d * (v * xa + xs)
                g1 = g1 + d
        st = mid_at(R.loc, j)
        group_rows(st, 0, g0)
        group_rows(st, 3, g1)
        blank(st, 6, 2)

    loop(MID // LANES, h1_back)
    mid_start(7)
    rs_step(SPATIAL, SQUEEZE, MIXING, EXPAND, SHORTCUT)

    def norm_grads(i, src, gains, biases):
        at, width = cfg.norm_columns[i]
        parts, _, n = src.shape
        for h in range(parts):
            cols = slice(at + h * n, at + (h + 1) * n)
            for g in range(3):
                R.gn_values[g, 0:1, cols] = src[h, gains + g : gains + g + 1, :]
                R.gn_values[g, 1:2, cols] = src[h, biases + g : biases + g + 1, :]

    def gn_copy(first):
        at = MID if first else 0
        n = R.gn.shape[2] - MID if first else MID
        cols = pl.ds(at, n)
        return pltpu.make_async_copy(R.gn_values.at[:, :, cols], R.gn.at[:, :, cols], R.ld.at[3 + first])

    def short_back(j):
        acc = None
        for i in range(4):
            v = dot_t(R.dzs[:, i * 512 : (i + 1) * 512], piece(R.f3, j, i))
            acc = v if acc is None else acc + v
        R.z6[:, aligned(j, CIN // 4)] = acc

    loop(4, short_back)
    for i, (src, gains) in enumerate(((R.g2, 0), (R.g4, 0), (R.g5, 0), (R.g3.at[:, 0], 0), (R.g3.at[:, 1], 0), (R.g6.at[:, 0], 0))):
        norm_grads(i + 1, src, gains, 3)
    gn_copies = [gn_copy(1)]
    gn_copies[0].start()
    mid_finish(7, R.g1)

    def h1_apply(j):
        cols = aligned(j, LANES)
        f, a, bz = backward_terms(mid_at(R.t1, j), mid_at(R.g1, j), norm_reduce, cols, IN)
        for k in range(RD):
            for p in range(2):
                rows = out_rows(p)
                d = f * R.zs[rows, dh1_at(k, j, LANES)] - a - R.z1[k, rows, cols] * bz
                R.y1[rows, dh1_at(k, j, LANES)] = (d * R.pix_in[k, rows, :]).astype(BF)

    loop(MID // LANES, h1_apply)

    def dz1(k):
        return R.y1[:, k * MID : (k + 1) * MID]

    def fill_reduce(stage):
        n = CIN // 32

        def body(j):
            act = R.x0[:, :, aligned(j, 256)].reshape(RD * 2 * S, 256)
            res = dot_w(act, jnp.concatenate([dz1(k) for k in range(RD)], axis=0))
            for i in range(8):
                bits = batch_bits(i // 4, lax.rem(j, 2), lax.div(j, 2), i // 2 % 2)
                put(stage, REDUCE, i % 2, bits, 0, res[i * n : (i + 1) * n])

        loop(4, body)

    staged(REDUCE, fill_reduce)
    rs_round()

    def input_grad(j):
        cols = aligned(j, CIN // 4)
        w = R.f0[aligned(j, CIN // 4), :]
        ch = jnp.concatenate(
            [keep(j * (CIN // 4 // LANES) + i, float(CIN // MID)) for i in range(CIN // 4 // LANES)],
            axis=1,
        )
        for k in range(RD):
            y = dot_t(dz1(k), w)
            for c in range(0, CIN // 4, LANES):
                base = c // LANES * 2 * S
                for p in range(2):
                    v = y[out_rows(p), c : c + LANES]
                    if p == 0 and k % 2 == 0:
                        v = v + R.z6[out_rows(k // 2), pl.ds(pl.multiple_of(j * (CIN // 4) + c, LANES), LANES)]
                    v = v * (ch[:, c : c + LANES] * R.pix_in[k, out_rows(p), :])
                    R.weave[pl.ds(base + p, S, stride=2), :] = v
                at = pl.ds(pl.multiple_of(k % 2 * CIN + j * (CIN // 4) + c, LANES), LANES)
                woven = R.weave[base : base + 2 * S, :]
                (R.du2, R.du1)[k // 2][:, :, at] = woven.reshape(M // 16, 16, LANES)

    for j in range(4):
        input_grad(j)
        if j < 3:
            rs_round()
    gin_copies = [
        pltpu.make_async_copy(
            (R.du2, R.du1)[k // 2].at[pl.ds(0, images), :, pl.ds(k % 2 * CIN, CIN)],
            R.gin.at[:, k],
            R.gi.at[k],
        )
        for k in range(RD)
    ]
    for c in gin_copies:
        c.start()
    rs_end()

    norm_grads(0, R.g1, 0, 3)
    gn_copies.append(gn_copy(0))
    gn_copies[1].start()

    for o in range(OD):
        mixed_copy(0, o).wait()
        mixed_copy(1, o).wait_send()
        mixed_copy(2, o).wait()
        mixed_copy(3, o).wait()
    for c in gin_copies + gn_copies:
        c.wait()


def plan(features, w_reduce, w_expand, batch):
    images, rd, _, cin = features.shape
    mid, wide = w_reduce.shape[1], w_expand.shape[1]
    cfg = SimpleNamespace(
        images=images,
        members=images * batch // 3,
        slots=-(-images * 8 // 16) * 16, in_rows=rd, out_rows=rd // 2, batch=batch, mid=mid, wide=wide, cin=cin
    )
    flat = {
        REDUCE: cin,
        SPATIAL: 9 * mid,
        EXPAND: mid * wide // 512,
        SHORTCUT: cin * wide // 512,
        SQUEEZE: wide,
        MIXING: 9 * mid,
        WIDEN: mid * wide // 512,
    }
    pieces = {SPATIAL: 3, MIXING: 3, SHORTCUT: 2}
    widths = (mid,) * 4 + (wide,) * 3
    cfg.norm_columns = [(sum(widths[:i]), n) for i, n in enumerate(widths)]
    cfg.units = []
    for name in (REDUCE, SPATIAL, SHORTCUT, EXPAND, SQUEEZE, MIXING, WIDEN):
        n, k = flat[name], pieces.get(name, 1)
        for i in range(k):
            mode = 1 + len(cfg.units) % 2 if name else 0
            cfg.units.append((name, i * n // 4 // k, n // 4 // k, mode))
    cfg.lags = (0, 2, 4, 6)
    cfg.pumps = (3, 1, 2, 2, 2, 2, 3)
    cfg.flat = flat
    cfg.rows = {name: n // 32 for name, n in flat.items()}
    cfg.reduce = batch == 8
    orders = ((DX, DY, DN, DF), (DY, DN, DX, DF), (DN, DX, DY, DF))
    thirds = {WIDEN: 1, SQUEEZE: 0, EXPAND: 2}
    cfg.parts = {}
    for name, n in cfg.rows.items():
        if not cfg.reduce:
            cfg.parts[name] = [(0, n, (DF, DN, DY, DX))]
            continue
        tiles = [n // 16 // 3] * 3
        for i in range(n // 16 - sum(tiles)):
            tiles[(thirds.get(name, 0) + i) % 3] += 1
        cfg.parts[name], n0 = [], 0
        for tile, order in zip(tiles, orders):
            if tile:
                cfg.parts[name].append((n0, 16 * tile, order))
                n0 += 16 * tile
    cfg.own_landing = (REDUCE, SPATIAL, SHORTCUT)
    cfg.offs, total = {}, 0
    for name, n in cfg.rows.items():
        cfg.offs[name] = total
        total += n
    cfg.total = total
    return cfg


def run_blocks(cfg, smem_args, hbm_args):
    S, RD, OD, NB = cfg.slots, cfg.in_rows, cfg.out_rows, cfg.batch
    MID, WIDE, CIN = cfg.mid, cfg.wide, cfg.cin
    M = OD * S
    U = len(cfg.units)
    hbm = pl.BlockSpec(memory_space=pl.ANY)
    sds = jax.ShapeDtypeStruct
    outs = dict(
        mixed=(sds((cfg.images, 4 * OD, 8, WIDE), BF), hbm),
        gin=(sds((cfg.images, RD, 16, CIN), F32), hbm),
        gn=(sds((3, 2, 4 * MID + 3 * WIDE), F32), hbm),
    )
    final = {}
    if cfg.reduce:
        for w, n in cfg.rows.items():
            final[w] = (9, n // 9, 512) if w in (SPATIAL, MIXING) else (n, 512)
            shape = (n, 2048) if w in (EXPAND, SHORTCUT, WIDEN) else final[w][:-2] + (4 * final[w][-2], 512)
            outs["o" + str(w)] = (sds(shape, BF), hbm)
    else:
        outs.update(grads=(sds((32 * cfg.total, 512), BF), hbm))
    V = pltpu.VMEM
    mid_tot = V((2, 8, MID // 2), F32)
    scratch = dict(
        z1=V((RD, 2 * S, MID), F32),
        win1=V((M, 9 * MID), BF),
        h1s=V((2, S, MID), BF),
        h1r=V((2, S, MID), BF),
        z2=V((M, MID), F32),
        h2=V((M, MID), BF),
        z3=V((M, WIDE), F32),
        zs=V((M, WIDE), F32),
        y1=V((M, WIDE), BF),
        z4=V((M, MID), F32),
        h4=V((OD + 2, S, MID), BF),
        win4=V((M, 9 * MID), BF),
        z5=V((M, MID), F32),
        h5=V((M, MID), BF),
        z6=V((M, WIDE), F32),
        mixed_local=V((OD, S // 8, 8, WIDE), BF),
        du2=V((M // 16, 16, WIDE), F32),
        dz6=V((M, WIDE), BF),
        dh=V((M, MID), F32),
        d5=V((OD + 2, S, MID), BF),
        win5=V((M, 9 * MID), BF),
        dz4=V((M, MID), BF),
        du1=V((M // 16, 16, WIDE), F32),
        dzs=V((M, WIDE), BF),
        d2=V((OD + 1, S, MID), BF),
        d2l=V((OD + 1, S, MID), BF),
        stage0=V((32 * cfg.rows[MIXING], 512), BF),
        stage1=V((32 * cfg.rows[SHORTCUT], 512), BF),
        loc=mid_tot,
        locw=V((4, 1, 8, WIDE // 4), F32),
        locw2=V((4, 2, 8, WIDE // 4), F32),
        t1=mid_tot,
        t2=mid_tot,
        t3=V((4, 2, 8, WIDE // 4), F32),
        t4=mid_tot,
        t5=mid_tot,
        t6=V((4, 1, 8, WIDE // 4), F32),
        g1=mid_tot,
        g2=mid_tot,
        g3=V((4, 2, 8, WIDE // 4), F32),
        g4=mid_tot,
        g5=mid_tot,
        g6=V((4, 1, 8, WIDE // 4), F32),
        rc=V((2, 8, MID // 2), F32),
        rq=V((2, 2 * NB, 8, MID // 2), F32),
        rw=V((2, 4, 2, 8, WIDE // 4), F32),
        wb=V((2, NB, 2, 8, WIDE // 4), F32),
        wsend=pltpu.SemaphoreType.DMA((U, 7)),
        wrecv=pltpu.SemaphoreType.DMA((U, 7)),
        wloc=pltpu.SemaphoreType.DMA((7, 4)),
        ms=pltpu.SemaphoreType.DMA((3,)),
        mr=pltpu.SemaphoreType.DMA((3, 2)),
        ws=pltpu.SemaphoreType.DMA((4, 3)),
        wr=pltpu.SemaphoreType.DMA((4, 3)),
        hs=pltpu.SemaphoreType.DMA((2,)),
        hr=pltpu.SemaphoreType.DMA((2,)),
        es=pltpu.SemaphoreType.DMA((2, 2)),
        er=pltpu.SemaphoreType.DMA((2, 2)),
        xs=pltpu.SemaphoreType.DMA((3, OD)),
        xr=pltpu.SemaphoreType.DMA((3, OD)),
        xl=pltpu.SemaphoreType.DMA((OD,)),
        gs=pltpu.SemaphoreType.DMA((2,)),
        gi=pltpu.SemaphoreType.DMA((RD,)),
        rs=pltpu.SemaphoreType.DMA((7, 3, 5)),
        rr=pltpu.SemaphoreType.DMA((7, 3, 5)),
        fs=pltpu.SemaphoreType.DMA((7, 3)),
        fr=pltpu.SemaphoreType.DMA((7, 3)),
        fl=pltpu.SemaphoreType.DMA((7,)),
        x0=V((RD, 2 * S, CIN), BF),
        weave=V((4 * S, LANES), F32),
        ct=V((M, WIDE), BF),
        onehot=V((3, S, LANES), F32),
        active_slot=V((S, LANES), F32),
        pix_in=V((RD, 2 * S, LANES), F32),
        pix_out=V((M, LANES), F32),
        ld=pltpu.SemaphoreType.DMA((5,)),
        norm_values=V((3, 2, 4 * MID + 3 * WIDE), F32),
        gn_values=V((3, 2, 4 * MID + 3 * WIDE), F32),
    )
    scratch.update({"f" + str(name): V((n, 512), BF) for name, n in cfg.flat.items()})
    scratch.update({"l" + str(name): V((cfg.flat[name], 512), BF) for name in cfg.own_landing if cfg.reduce})
    scratch.update({"e" + str(w): V(shape, BF) for w, shape in final.items()})
    names = list(smem_args) + list(hbm_args) + list(outs) + list(scratch)
    smem = pl.BlockSpec(memory_space=pltpu.SMEM)
    res = pl.pallas_call(
        functools.partial(block_kernel, names, cfg),
        out_shape=[o[0] for o in outs.values()],
        in_specs=[smem] * len(smem_args) + [hbm] * len(hbm_args),
        out_specs=[o[1] for o in outs.values()],
        scratch_shapes=list(scratch.values()),
        compiler_params=pltpu.CompilerParams(
            collective_id=0, has_side_effects=True, vmem_limit_bytes=63 * 2**20
        ),
    )(*smem_args.values(), *hbm_args.values())
    return SimpleNamespace(**dict(zip(outs, res)))


def slot_layout(x, slots):
    images, rows, cols, channels = x.shape
    x = jnp.transpose(x, (1, 0, 2, 3)).reshape(rows, images * cols, channels)
    return jnp.pad(x, ((0, 0), (0, slots - images * cols), (0, 0)))


def per_device(
    features, w_reduce, w_spatial, w_expand, w_shortcut, w_squeeze, w_mixing, w_widen,
    norm_reduce, norm_spatial, norm_expand, norm_shortcut, norm_squeeze, norm_mixing, norm_widen,
    cotangent, resolution, active,
):
    images, rd, cols_in, cin = features.shape
    od = rd // 2
    nb = lax.axis_size("batch")
    cfg = plan(features, w_reduce, w_expand, nb)
    S, mid, wide = cfg.slots, cfg.mid, cfg.wide
    x = jnp.pad(features, ((0, 0), (0, 0), (0, 16 - cols_in), (0, 0)))
    x = x.reshape(images, rd, 8, 2, cin)
    x = jnp.transpose(x, (1, 3, 0, 2, 4)).reshape(rd, 2, images * 8, cin)
    x = jnp.pad(x, ((0, 0), (0, 0), (0, S - images * 8), (0, 0))).reshape(rd, 2 * S, cin)
    out_cols = cotangent.shape[2]
    ct = slot_layout(jnp.pad(cotangent, ((0, 0), (0, 0), (0, 8 - out_cols), (0, 0))), S)
    norms = jnp.concatenate(
        [
            jnp.transpose(n, (1, 0, 2))
            for n in (norm_reduce, norm_spatial, norm_squeeze, norm_mixing, norm_expand, norm_shortcut, norm_widen)
        ],
        axis=2,
    )
    res = run_blocks(
        cfg,
        dict(resolution=resolution, active=active),
        dict(
            features=x,
            norms=norms,
            cotangent=ct.reshape(od * S, wide),
            w0=w_reduce,
            w1=w_spatial.reshape(-1, mid),
            w2=w_expand,
            w3=w_shortcut,
            w4=w_squeeze,
            w5=w_mixing.reshape(-1, mid),
            w6=w_widen,
        ),
    )
    mixed = res.mixed[:, :, :out_cols]

    def unpack(g, name):
        b8, _, n, _ = g.shape
        if name in (SPATIAL, MIXING):
            k = n // 9
            return jnp.transpose(g.reshape(b8, 4, 9, k, 512), (2, 0, 1, 3, 4)).reshape(3, 3, b8 * 4 * k, 512)
        if name in (EXPAND, SHORTCUT, WIDEN):
            return jnp.transpose(g, (0, 2, 1, 3)).reshape(b8 * n, 2048)
        return g.reshape(b8 * 4 * n, 512)

    totals = []
    for name, n in cfg.rows.items():
        if cfg.reduce:
            g = getattr(res, "o" + str(name)).astype(F32)
            totals.append(g.reshape((3, 3) + g.shape[1:]) if g.ndim == 3 else g)
            continue
        at = cfg.offs[name]
        part = res.grads[32 * at : 32 * (at + n)].reshape(2, 8, 2, n, 512)
        part = unpack(jnp.transpose(part, (1, 2, 0, 3, 4)).reshape(8, 4, n, 512), name)
        dim = 2 if part.ndim == 4 else 0
        part = lax.psum_scatter(part, "batch", scatter_dimension=dim, tiled=True)
        totals.append(lax.psum(part, "rows").astype(F32))

    gn = [jnp.transpose(res.gn[:, :, at : at + n], (1, 0, 2)) for at, n in cfg.norm_columns]
    return (mixed, res.gin[:, :, :cols_in], *totals, gn[0], gn[1], gn[4], gn[5], gn[2], gn[3], gn[6])


def solution(mesh):
    w2, w4 = P("rows", None), P(None, None, "rows", None)
    o2, o4 = P("batch", None), P(None, None, "batch", None)
    return jax.shard_map(
        per_device,
        mesh=mesh,
        in_specs=(P("batch", "rows", None, None), w2, w4, w2, w2, w2, w4, w2)
        + (P(),) * 7
        + (P("batch", "rows", None, None), P(), P()),
        out_specs=(P("batch", None, None, None), P("batch", "rows", None, None), o2, o4, o2, o2, o2, o4, o2)
        + (P(),) * 7,
        check_vma=False,
    )
```
